32 devices in a mesh: grp: 2 (over y), seq: 4 (over z), fsdp: 2 (over x), chan: 2 (over core).
Axes of the slice: x: 2, y: 2, z: 4, core: 2. Of those that a mesh axis runs over, the one named last changes fastest.
Arguments:
- tokens: bfloat16 [2048, 4096], P(('grp', 'seq', 'fsdp'), 'chan'), parts along dimension 0, may hold values from -6 to 6
- proj_weight: bfloat16 [4096, 3, 512], P('fsdp', None, 'chan'), may hold values from -0.09375 to 0.09375
- short_weight: float32 [3, 3, 512], P(None, None, 'chan'), may hold values from -3 to 3
- skip_gain: float32 [512], P('chan'), may hold values from -4 to 4
- filter_taps: bfloat16 [1024, 512], P(('seq', 'fsdp'), 'chan'), may hold values from -0.1875 to 0.1875
Outputs:
- mixed_out: bfloat16 [2048, 512], P(('grp', 'seq', 'fsdp'), 'chan'), parts along dimension 0
The draws below stay inside these ranges and needn't reach their ends.
There are 2 independent parts, one for each index of `grp`. The reference program is written for one: setup_inputs(seed, part) draws one part's arguments, and reference() takes and returns one part's arrays. A program takes and returns all parts, laid end to end along the dimension named above; an argument that names none is the same for every part. Nothing has to cross between parts.
All inputs are finite; a program needn't handle non-finite values.
Results may differ from the reference program's by a relative error of at most 0.009.
Values may be sent and summed in bfloat16 or wider, within the bound.
No kernel may reach another device: no remote copies, remote signals or barrier semaphores. Data moves between devices by JAX's collectives and lax.ppermute only.
A program may use at most 64 MiB of HBM per device.

```python
import math
import jax
import jax.numpy as jnp
from jax import lax

D = 4096
C = 512
TOK_DEV = 128
L = 1024


def block_scale(rng, dims, split, low, top_value):
    factor_of = 1.0
    for dim, parts in split:
        steps = jax.random.uniform(jax.random.fold_in(jax.random.fold_in(rng, 6), dim), (parts,), jnp.float32, low / len(split), top_value / len(split))
        factor_of = factor_of * jnp.repeat(jnp.exp(steps), dims[dim] // parts).reshape((-1,) + (1,) * (len(dims) - 1 - dim))
    return factor_of


def normal_values(own_key, dims, deviation, bound, shards=(), kind=jnp.bfloat16):
    drawn = deviation * jax.random.normal(own_key, dims, jnp.float32)
    if shards:
        drawn = drawn * block_scale(own_key, dims, shards, -0.22, 0.18)
    return jnp.clip(drawn, -bound, bound).astype(kind)


def setup_inputs(seed: int = 0, part: int = 0) -> dict:
    splits = jax.random.split(jax.random.key(seed), 6)
    own_keys = jax.random.split(jax.random.fold_in(splits[5], part), 6)
    return {
        "tokens": normal_values(own_keys[0], (L, D), 1.0, 6.0, ((0, 8), (1, 2))),
        "proj_weight": normal_values(splits[1], (D, 3, C), D ** -0.5, 0.09375, ((0, 2), (2, 2))),
        "short_weight": normal_values(splits[2], (3, 3, C), 0.6, 3.0, ((2, 2),), jnp.float32),
        "skip_gain": normal_values(splits[3], (C,), 1.0, 4.0, ((0, 2),), jnp.float32),
        "filter_taps": normal_values(splits[4], (L, C), L ** -0.5, 0.1875, ((0, 8), (1, 2))),
    }


highest = lax.Precision.HIGHEST


def rounded(value):
    return lax.optimization_barrier(value.astype(jnp.bfloat16))


def index_grid(row_count, col_count):
    return (lax.broadcasted_iota(jnp.int32, (row_count, col_count), 0),
            lax.broadcasted_iota(jnp.int32, (row_count, col_count), 1))


def phase_pair(row_ids, col_ids, period):
    wrapped = (row_ids * col_ids) % period
    phase = wrapped.astype(jnp.float32) * (2.0 * math.pi / period)
    return jnp.cos(phase), jnp.sin(phase)


def spectrum(signal, first_cos, first_sin, twist_cos, twist_sin, last_cos, last_sin):
    values = signal.astype(jnp.float32)
    real_a = jnp.einsum("qp,bpm->bqm", first_cos, values, precision=highest)
    imag_a = -jnp.einsum("qp,bpm->bqm", first_sin, values, precision=highest)
    real_b = rounded(real_a * twist_cos + imag_a * twist_sin).astype(jnp.float32)
    imag_b = rounded(imag_a * twist_cos - real_a * twist_sin).astype(jnp.float32)
    real_x = jnp.einsum("bqm,mr->bqr", real_b, last_cos, precision=highest) + jnp.einsum("bqm,mr->bqr", imag_b, last_sin, precision=highest)
    imag_x = jnp.einsum("bqm,mr->bqr", imag_b, last_cos, precision=highest) - jnp.einsum("bqm,mr->bqr", real_b, last_sin, precision=highest)
    return rounded(real_x).astype(jnp.float32), rounded(imag_x).astype(jnp.float32)


def invert(real_z, imag_z, first_cos, first_sin, twist_cos, twist_sin, last_cos, last_sin, length):
    real_v = jnp.einsum("bqr,mr->bqm", real_z, last_cos, precision=highest) - jnp.einsum("bqr,mr->bqm", imag_z, last_sin, precision=highest)
    imag_v = jnp.einsum("bqr,mr->bqm", imag_z, last_cos, precision=highest) + jnp.einsum("bqr,mr->bqm", real_z, last_sin, precision=highest)
    real_w = rounded(real_v * twist_cos - imag_v * twist_sin).astype(jnp.float32)
    imag_w = rounded(imag_v * twist_cos + real_v * twist_sin).astype(jnp.float32)
    summed = jnp.einsum("qp,bqm->bpm", first_cos, real_w, precision=highest) - jnp.einsum("qp,bqm->bpm", first_sin, imag_w, precision=highest)
    return (summed * (1.0 / length)).astype(jnp.bfloat16)


def reference(tokens, proj_weight, short_weight, skip_gain, filter_taps):
    total_rows, model_width = tokens.shape
    width = proj_weight.shape[2]
    block_rows = TOK_DEV
    weight_flat = proj_weight.reshape(model_width, 3 * width).astype(jnp.float32)

    def project(block):
        return jnp.dot(block.astype(jnp.float32), weight_flat, precision=highest).astype(jnp.bfloat16)

    projected = lax.map(project, tokens.reshape(total_rows // block_rows, block_rows, model_width))
    projected = lax.optimization_barrier(projected)
    projected = projected.reshape(total_rows, 3, width).astype(jnp.float32)
    padded = jnp.pad(projected, ((2, 0), (0, 0), (0, 0)))
    mixed = short_weight[0] * padded[2:] + short_weight[1] * padded[1:-1] + short_weight[2] * padded[:-2]
    query = mixed[:, 0]
    product = rounded(mixed[:, 1] * mixed[:, 2])

    half_rows = total_rows // block_rows
    period_rows = 2 * half_rows
    length = period_rows * block_rows
    bin_ids, tap_ids = index_grid(period_rows, half_rows)
    first_cos, first_sin = phase_pair(bin_ids, tap_ids, period_rows)
    first_cos = rounded(first_cos).astype(jnp.float32)
    first_sin = rounded(first_sin).astype(jnp.float32)
    col_ids, freq_ids = index_grid(block_rows, block_rows)
    last_cos, last_sin = phase_pair(col_ids, freq_ids, block_rows)
    last_cos = rounded(last_cos).astype(jnp.float32)
    last_sin = rounded(last_sin).astype(jnp.float32)
    row_ids, mid_ids = index_grid(period_rows, block_rows)
    twist_cos, twist_sin = phase_pair(row_ids, mid_ids, length)

    group_size = 8
    signal_blocks = jnp.transpose(product).reshape(width // group_size, group_size, half_rows, block_rows)
    filter_blocks = jnp.transpose(filter_taps).reshape(width // group_size, group_size, half_rows, block_rows)

    def convolve(pair):
        signal, taps = pair
        sig_real, sig_imag = spectrum(signal, first_cos, first_sin, twist_cos, twist_sin, last_cos, last_sin)
        tap_real, tap_imag = spectrum(taps, first_cos, first_sin, twist_cos, twist_sin, last_cos, last_sin)
        real_z = rounded(sig_real * tap_real - sig_imag * tap_imag).astype(jnp.float32)
        imag_z = rounded(sig_real * tap_imag + sig_imag * tap_real).astype(jnp.float32)
        return invert(real_z, imag_z, first_cos, first_sin, twist_cos, twist_sin, last_cos, last_sin, length)

    convolved = lax.map(convolve, (signal_blocks, filter_blocks))
    conv = jnp.transpose(convolved.reshape(width, total_rows))
    result = query * (conv.astype(jnp.float32) + skip_gain * product.astype(jnp.float32))
    return result.astype(jnp.bfloat16)
```

```python
import functools
import math

import jax
import jax.numpy as jnp
import numpy as np
from jax import lax
from jax.experimental import pallas as pl
from jax.experimental.pallas import tpu as pltpu
from jax.sharding import PartitionSpec as P

HALO = 16
F32 = jnp.float32
BF16 = jnp.bfloat16


def shifted(value, axis, steps):
    count = lax.axis_size(axis)
    initial, last = (max(0, -steps), min(count, count - steps))
    return lax.ppermute(value, axis, [(source, source + steps) for source in range(initial, last)])


def index_grid(row_count, col_count):
    return (
        lax.broadcasted_iota(jnp.int32, (row_count, col_count), 0),
        lax.broadcasted_iota(jnp.int32, (row_count, col_count), 1),
    )


def phase_pair(row_ids, col_ids, period):
    wrapped = row_ids * col_ids % period
    phase = wrapped.astype(jnp.float32) * (2.0 * math.pi / period)
    return (jnp.cos(phase), jnp.sin(phase))


def multiply(real_x, imag_x):
    sig_real = real_x[0].astype(jnp.float32)
    sig_imag = imag_x[0].astype(jnp.float32)
    tap_real = real_x[1].astype(jnp.float32)
    tap_imag = imag_x[1].astype(jnp.float32)
    real_z = (sig_real * tap_real - sig_imag * tap_imag).astype(jnp.bfloat16)
    imag_z = (sig_real * tap_imag + sig_imag * tap_real).astype(jnp.bfloat16)
    return (real_z, imag_z)


def spread(stacked, groups, inner_shape):
    shaped = stacked.reshape((2, groups, 1) + inner_shape)
    moved = lax.all_to_all(shaped, ("seq", "fsdp"), split_axis=1, concat_axis=2, tiled=True)
    return moved.reshape((2, groups) + inner_shape)


def any_mesh(tokens, proj_weight, short_weight, skip_gain, filter_taps):
    whole = lax.all_gather(tokens, "chan", axis=1, tiled=True)
    row_count = whole.shape[0]
    width = proj_weight.shape[2]
    flat_width = 3 * width
    piece = lax.all_gather(proj_weight, "fsdp", axis=0, tiled=True)
    summed = jnp.dot(
        whole, piece.reshape(piece.shape[0], flat_width), preferred_element_type=jnp.float32
    )
    projected = summed.astype(jnp.bfloat16).reshape(row_count, 3, width)
    earlier = shifted(projected[row_count - 2 :], ("seq", "fsdp"), 1)
    extended = jnp.concatenate([earlier, projected], axis=0).astype(jnp.float32)
    mixed = (
        short_weight[0] * extended[2:]
        + short_weight[1] * extended[1:-1]
        + short_weight[2] * extended[:-2]
    )
    query = mixed[:, 0]
    product = (mixed[:, 1] * mixed[:, 2]).astype(jnp.bfloat16)
    groups = lax.axis_size(("seq", "fsdp"))
    position = lax.axis_index(("seq", "fsdp"))
    period_rows = 2 * groups
    length = period_rows * row_count
    scale = 1.0 / length
    bin_ids, tap_ids = index_grid(period_rows, groups)
    first_cos, first_sin = phase_pair(bin_ids, tap_ids, period_rows)
    first_cos = first_cos.astype(jnp.bfloat16)
    first_sin = first_sin.astype(jnp.bfloat16)
    col_ids, freq_ids = index_grid(row_count, row_count)
    last_cos, last_sin = phase_pair(col_ids, freq_ids, row_count)
    last_cos = last_cos.astype(jnp.bfloat16)
    last_sin = last_sin.astype(jnp.bfloat16)
    stacked = jnp.stack([product, filter_taps])
    f32 = jnp.float32
    per_dev = row_count // groups
    per_bins = period_rows // groups
    arrived = spread(stacked.reshape(2, groups, per_dev, width), groups, (per_dev, width))
    real_a = jnp.einsum("qp,kpmc->kqmc", first_cos, arrived, preferred_element_type=f32)
    imag_a = -jnp.einsum("qp,kpmc->kqmc", first_sin, arrived, preferred_element_type=f32)
    row_ids, mid_ids = index_grid(period_rows, per_dev)
    twist_cos, twist_sin = phase_pair(row_ids, mid_ids + position * per_dev, length)
    twist_cos = twist_cos[:, :, None]
    twist_sin = twist_sin[:, :, None]
    real_b = (real_a * twist_cos + imag_a * twist_sin).astype(jnp.bfloat16)
    imag_b = (imag_a * twist_cos - real_a * twist_sin).astype(jnp.bfloat16)
    outgoing = jnp.stack([real_b, imag_b]).reshape(2, 2, groups, per_bins, 1, per_dev, width)
    turned = lax.all_to_all(outgoing, ("seq", "fsdp"), split_axis=2, concat_axis=4, tiled=True)
    turned = turned.reshape(2, 2, per_bins, row_count, width)
    real_b = turned[0]
    imag_b = turned[1]
    real_x = (
        jnp.einsum("kqmc,mr->kqrc", real_b, last_cos, preferred_element_type=f32)
        + jnp.einsum("kqmc,mr->kqrc", imag_b, last_sin, preferred_element_type=f32)
    ).astype(jnp.bfloat16)
    imag_x = (
        jnp.einsum("kqmc,mr->kqrc", imag_b, last_cos, preferred_element_type=f32)
        - jnp.einsum("kqmc,mr->kqrc", real_b, last_sin, preferred_element_type=f32)
    ).astype(jnp.bfloat16)
    real_z, imag_z = multiply(real_x, imag_x)
    real_v = jnp.einsum("qrc,mr->qmc", real_z, last_cos, preferred_element_type=f32) - jnp.einsum(
        "qrc,mr->qmc", imag_z, last_sin, preferred_element_type=f32
    )
    imag_v = jnp.einsum("qrc,mr->qmc", imag_z, last_cos, preferred_element_type=f32) + jnp.einsum(
        "qrc,mr->qmc", real_z, last_sin, preferred_element_type=f32
    )
    row_ids, mid_ids = index_grid(per_bins, row_count)
    twist_cos, twist_sin = phase_pair(row_ids + position * per_bins, mid_ids, length)
    twist_cos = twist_cos[:, :, None]
    twist_sin = twist_sin[:, :, None]
    real_w = (real_v * twist_cos - imag_v * twist_sin).astype(jnp.bfloat16)
    imag_w = (imag_v * twist_cos + real_v * twist_sin).astype(jnp.bfloat16)
    backward = jnp.stack([real_w, imag_w]).reshape(2, 1, per_bins, groups, per_dev, width)
    returned = lax.all_to_all(backward, ("seq", "fsdp"), split_axis=3, concat_axis=1, tiled=True)
    returned = returned.reshape(2, period_rows, per_dev, width)
    conv_rows = jnp.einsum(
        "qp,qmc->pmc", first_cos, returned[0], preferred_element_type=f32
    ) - jnp.einsum("qp,qmc->pmc", first_sin, returned[1], preferred_element_type=f32)
    conv_rows = (conv_rows * scale).astype(jnp.bfloat16)
    homed = lax.all_to_all(
        conv_rows.reshape(groups, 1, per_dev, width),
        ("seq", "fsdp"),
        split_axis=0,
        concat_axis=1,
        tiled=True,
    )
    conv = homed.reshape(row_count, width)
    result = query * (conv.astype(jnp.float32) + skip_gain * product.astype(jnp.float32))
    return result.astype(jnp.bfloat16)


def wave_table(size):
    freq, time = np.meshgrid(np.arange(size), np.arange(size), indexing="ij")
    angle = ((2 * freq + 1) * time % (4 * size)) * (math.pi / (2 * size))
    return np.concatenate([np.cos(angle), np.sin(angle)], axis=0)


def exchange(value, axis):
    return lax.ppermute(value, axis, [(0, 1), (1, 0)])


def whole_specs(count):
    return [pl.BlockSpec(memory_space=pltpu.VMEM)] * count


def split_channels(summed, own_half):
    half = summed.shape[1] // 2
    low, high = (summed[:, :half], summed[:, half:])
    first = own_half == 0
    return (jnp.where(first, low, high), jnp.where(first, high, low))


def project_body(rows_ref, hop_ref, weight_ref, keep_ref, send_ref):
    own_half = lax.axis_index("fsdp")
    here = lax.axis_index("chan") == own_half
    rows = jnp.where(here, rows_ref[...], hop_ref[...])
    half = keep_ref.shape[1] // 3
    for branch in range(3):
        summed = jnp.dot(rows, weight_ref[branch], preferred_element_type=F32)
        keep, send = split_channels(summed, own_half)
        keep_ref[:, branch * half : (branch + 1) * half] = keep
        send_ref[:, branch * half : (branch + 1) * half] = send.astype(BF16)


def project_first_body(rows_ref, hop_ref, halo_ref, halo_hop_ref, weight_ref, keep_ref, send_ref):
    own_half = lax.axis_index("fsdp")
    here = lax.axis_index("chan") == own_half
    rows = jnp.where(here, rows_ref[...], hop_ref[...])
    halo = jnp.where(here, halo_ref[...], halo_hop_ref[...])
    rows = jnp.concatenate([halo, rows], axis=0)
    half = keep_ref.shape[1] // 3
    for branch in range(3):
        summed = jnp.dot(rows, weight_ref[branch], preferred_element_type=F32)
        keep, send = split_channels(summed, own_half)
        keep_ref[:, branch * half : (branch + 1) * half] = keep
        send_ref[:, branch * half : (branch + 1) * half] = send.astype(BF16)


def taps_body(table_ref, *refs):
    tap_refs = refs[:4]
    real_ref, imag_ref, ordered = refs[4:]
    position = lax.axis_index("seq")
    blocks = len(tap_refs)
    size = table_ref.shape[1]
    for step in range(blocks):
        ordered[lax.rem(position - step + blocks, blocks)] = tap_refs[step][...]
    sign = 1.0 - 2.0 * (lax.broadcasted_iota(jnp.int32, (size, 1), 0) % 2).astype(F32)
    sign = sign * (1.0 / size)
    before_real = before_imag = None
    for block in range(blocks):
        waves = jnp.dot(table_ref[...], ordered[block], preferred_element_type=F32)
        real, imag = (waves[:size], -waves[size:])
        if block == 0:
            real_ref[block] = real * (1.0 / size)
            imag_ref[block] = imag * (1.0 / size)
        else:
            real_ref[block] = real * (1.0 / size) - sign * before_imag
            imag_ref[block] = imag * (1.0 / size) + sign * before_real
        before_real, before_imag = (real, imag)


def mix_body(keep_first, keep_second, got_first, got_second, short_ref, product_ref, query_ref, joined):
    own = lax.axis_index("fsdp")
    rows = keep_second.shape[0]
    half = keep_second.shape[1] // 3
    joined[:HALO, :] = keep_first[:HALO, :] + got_first[:HALO, :].astype(F32)
    own_start = pl.multiple_of(HALO + own * rows, HALO)
    other_start = pl.multiple_of(HALO + (1 - own) * rows, HALO)
    joined[pl.ds(own_start, rows), :] = keep_first[HALO:, :] + got_second[...].astype(F32)
    joined[pl.ds(other_start, rows), :] = keep_second[...] + got_first[HALO:, :].astype(F32)
    count = 2 * rows
    mixed = []
    for branch in range(3):
        lanes = slice(branch * half, (branch + 1) * half)
        total = None
        for tap in range(3):
            term = short_ref[tap, branch][None, :] * joined[pl.ds(HALO - tap, count), lanes]
            total = term if total is None else total + term
        mixed.append(total)
    query_ref[...] = mixed[0]
    product_ref[...] = (mixed[1] * mixed[2]).astype(BF16)


def conv_body(own_ref, one_ref, two_ref, three_ref, real_ref, imag_ref, table_ref, turned_ref,
              query_ref, gain_ref, stay_ref, go_ref, result):
    position = lax.axis_index("seq")
    own = lax.axis_index("fsdp")
    size = table_ref.shape[1]
    total_real = total_imag = None
    for step, block_ref in enumerate((own_ref, one_ref, two_ref, three_ref)):
        block = block_ref[...]
        if step:
            block = jnp.where(position >= step, block, jnp.zeros_like(block))
        waves = jnp.dot(table_ref[...], block, preferred_element_type=F32)
        real, imag = (waves[:size], -waves[size:])
        term_real = real * real_ref[step] - imag * imag_ref[step]
        term_imag = real * imag_ref[step] + imag * real_ref[step]
        total_real = term_real if total_real is None else total_real + term_real
        total_imag = term_imag if total_imag is None else total_imag + term_imag
    stacked = jnp.concatenate([total_real, -total_imag], axis=0).astype(BF16)
    conv = jnp.dot(turned_ref[...], stacked, preferred_element_type=F32)
    gated = query_ref[...] * (conv + gain_ref[...] * own_ref[...].astype(F32))
    result[...] = gated.astype(BF16)
    rows = stay_ref.shape[0]
    stay_ref[...] = result[pl.ds(pl.multiple_of(own * rows, rows), rows), :]
    go_ref[...] = result[pl.ds(pl.multiple_of((1 - own) * rows, rows), rows), :]


def join_body(stay_ref, got_ref, out_ref):
    first = lax.axis_index("fsdp") == 0
    half = stay_ref.shape[1]
    out_ref[:, :half] = jnp.where(first, stay_ref[...], got_ref[...])
    out_ref[:, half:] = jnp.where(first, got_ref[...], stay_ref[...])


def shape(dims, kind):
    return jax.ShapeDtypeStruct(dims, kind)


def pair_mesh(tokens, proj_weight, short_weight, skip_gain, filter_taps):
    rows = tokens.shape[0]
    features = proj_weight.shape[0]
    width = proj_weight.shape[2]
    half = width // 2
    size = 2 * rows
    blocks = lax.axis_size("seq")
    fsdp = lax.axis_index("fsdp")
    weight = jnp.transpose(proj_weight, (1, 0, 2))
    call = functools.partial(
        pl.pallas_call, compiler_params=pltpu.CompilerParams(vmem_limit_bytes=32 * 1024 * 1024)
    )

    got = lax.ppermute(tokens, ("fsdp", "chan"), [(1, 3), (2, 0)])
    own_hop = exchange(tokens, "chan")
    halo = lax.ppermute(
        tokens[rows - HALO :],
        ("seq", "fsdp", "chan"),
        [(4 * s + 2 + c, 4 * (s + 1) + 2 * c + c) for s in range(blocks - 1) for c in range(2)],
    )
    halo_hop = exchange(halo, "chan")

    keep_first, send_first = call(
        project_first_body,
        in_specs=whole_specs(5),
        out_specs=whole_specs(2),
        out_shape=(shape((HALO + rows, 3 * half), F32), shape((HALO + rows, 3 * half), BF16)),
    )(tokens, own_hop, halo, halo_hop, weight)

    table = wave_table(size)
    forward = jnp.asarray(table, dtype=BF16)
    inverse = jnp.asarray(table.T, dtype=BF16)
    tap_low, tap_high = (filter_taps[:, :half], filter_taps[:, half:])
    first = fsdp == 0
    tap_keep = jnp.where(first, tap_low, tap_high)
    tap_got = exchange(jnp.where(first, tap_high, tap_low), "fsdp")
    taps = jnp.where(
        first,
        jnp.concatenate([tap_keep, tap_got], axis=0),
        jnp.concatenate([tap_got, tap_keep], axis=0),
    )
    ring = [
        [(s, (s + step) % blocks) for s in range(blocks)] for step in range(blocks)
    ]
    tap_blocks = [taps] + [lax.ppermute(taps, "seq", ring[step]) for step in range(1, blocks)]
    tap_real, tap_imag = call(
        taps_body,
        in_specs=whole_specs(1 + blocks),
        out_specs=whole_specs(2),
        out_shape=(shape((blocks, size, half), F32), shape((blocks, size, half), F32)),
        scratch_shapes=[pltpu.VMEM((blocks, size, half), BF16)],
    )(forward, *tap_blocks)

    got_first = exchange(send_first, "fsdp")
    got_hop = exchange(got, "chan")
    keep_second, send_second = call(
        project_body,
        in_specs=whole_specs(3),
        out_specs=whole_specs(2),
        out_shape=(shape((rows, 3 * half), F32), shape((rows, 3 * half), BF16)),
    )(got, got_hop, weight)
    got_second = exchange(send_second, "fsdp")

    short_half = lax.dynamic_slice_in_dim(short_weight, fsdp * half, half, axis=2)
    gain_half = lax.dynamic_slice_in_dim(skip_gain, fsdp * half, half, axis=0)[None, :]
    product, query = call(
        mix_body,
        in_specs=whole_specs(5),
        out_specs=whole_specs(2),
        out_shape=(shape((size, half), BF16), shape((size, half), F32)),
        scratch_shapes=[pltpu.VMEM((HALO + size, 3 * half), F32)],
    )(keep_first, keep_second, got_first, got_second, short_half)

    products = [product] + [lax.ppermute(product, "seq", ring[step]) for step in range(1, blocks)]
    stay, go = call(
        conv_body,
        in_specs=whole_specs(10),
        out_specs=whole_specs(2),
        out_shape=(shape((rows, half), BF16), shape((rows, half), BF16)),
        scratch_shapes=[pltpu.VMEM((size, half), BF16)],
    )(*products, tap_real, tap_imag, forward, inverse, query, gain_half)
    back = exchange(go, "fsdp")
    return call(
        join_body,
        in_specs=whole_specs(2),
        out_specs=whole_specs(1)[0],
        out_shape=shape((rows, width), BF16),
    )(stay, back)


def solution(mesh):
    in_specs = (
        P(("grp", "seq", "fsdp"), "chan"),
        P("fsdp", None, "chan"),
        P(None, None, "chan"),
        P("chan"),
        P(("seq", "fsdp"), "chan"),
    )
    out_specs = P(("grp", "seq", "fsdp"), "chan")
    sizes = mesh.shape
    paired = sizes["fsdp"] == 2 and sizes["chan"] == 2 and sizes["seq"] == 4
    per_device = pair_mesh if paired else any_mesh
    return jax.shard_map(
        per_device, mesh=mesh, in_specs=in_specs, out_specs=out_specs, check_vma=False
    )
```

```python
import functools
import math

import jax
import jax.numpy as jnp
import numpy as np
from jax import lax
from jax.experimental import pallas as pl
from jax.experimental.pallas import tpu as pltpu
from jax.sharding import PartitionSpec as P

HALO = 16
LOAD_MIB = 48
F32 = jnp.float32
BF16 = jnp.bfloat16


def shifted(value, axis, steps):
    count = lax.axis_size(axis)
    initial, last = (max(0, -steps), min(count, count - steps))
    return lax.ppermute(value, axis, [(source, source + steps) for source in range(initial, last)])


def index_grid(row_count, col_count):
    return (
        lax.broadcasted_iota(jnp.int32, (row_count, col_count), 0),
        lax.broadcasted_iota(jnp.int32, (row_count, col_count), 1),
    )


def phase_pair(row_ids, col_ids, period):
    wrapped = row_ids * col_ids % period
    phase = wrapped.astype(jnp.float32) * (2.0 * math.pi / period)
    return (jnp.cos(phase), jnp.sin(phase))


def multiply(real_x, imag_x):
    sig_real = real_x[0].astype(jnp.float32)
    sig_imag = imag_x[0].astype(jnp.float32)
    tap_real = real_x[1].astype(jnp.float32)
    tap_imag = imag_x[1].astype(jnp.float32)
    real_z = (sig_real * tap_real - sig_imag * tap_imag).astype(jnp.bfloat16)
    imag_z = (sig_real * tap_imag + sig_imag * tap_real).astype(jnp.bfloat16)
    return (real_z, imag_z)


def spread(stacked, groups, inner_shape):
    shaped = stacked.reshape((2, groups, 1) + inner_shape)
    moved = lax.all_to_all(shaped, ("seq", "fsdp"), split_axis=1, concat_axis=2, tiled=True)
    return moved.reshape((2, groups) + inner_shape)


def any_mesh(tokens, proj_weight, short_weight, skip_gain, filter_taps):
    whole = lax.all_gather(tokens, "chan", axis=1, tiled=True)
    row_count = whole.shape[0]
    width = proj_weight.shape[2]
    flat_width = 3 * width
    piece = lax.all_gather(proj_weight, "fsdp", axis=0, tiled=True)
    summed = jnp.dot(
        whole, piece.reshape(piece.shape[0], flat_width), preferred_element_type=jnp.float32
    )
    projected = summed.astype(jnp.bfloat16).reshape(row_count, 3, width)
    earlier = shifted(projected[row_count - 2 :], ("seq", "fsdp"), 1)
    extended = jnp.concatenate([earlier, projected], axis=0).astype(jnp.float32)
    mixed = (
        short_weight[0] * extended[2:]
        + short_weight[1] * extended[1:-1]
        + short_weight[2] * extended[:-2]
    )
    query = mixed[:, 0]
    product = (mixed[:, 1] * mixed[:, 2]).astype(jnp.bfloat16)
    groups = lax.axis_size(("seq", "fsdp"))
    position = lax.axis_index(("seq", "fsdp"))
    period_rows = 2 * groups
    length = period_rows * row_count
    scale = 1.0 / length
    bin_ids, tap_ids = index_grid(period_rows, groups)
    first_cos, first_sin = phase_pair(bin_ids, tap_ids, period_rows)
    first_cos = first_cos.astype(jnp.bfloat16)
    first_sin = first_sin.astype(jnp.bfloat16)
    col_ids, freq_ids = index_grid(row_count, row_count)
    last_cos, last_sin = phase_pair(col_ids, freq_ids, row_count)
    last_cos = last_cos.astype(jnp.bfloat16)
    last_sin = last_sin.astype(jnp.bfloat16)
    stacked = jnp.stack([product, filter_taps])
    f32 = jnp.float32
    per_dev = row_count // groups
    per_bins = period_rows // groups
    arrived = spread(stacked.reshape(2, groups, per_dev, width), groups, (per_dev, width))
    real_a = jnp.einsum("qp,kpmc->kqmc", first_cos, arrived, preferred_element_type=f32)
    imag_a = -jnp.einsum("qp,kpmc->kqmc", first_sin, arrived, preferred_element_type=f32)
    row_ids, mid_ids = index_grid(period_rows, per_dev)
    twist_cos, twist_sin = phase_pair(row_ids, mid_ids + position * per_dev, length)
    twist_cos = twist_cos[:, :, None]
    twist_sin = twist_sin[:, :, None]
    real_b = (real_a * twist_cos + imag_a * twist_sin).astype(jnp.bfloat16)
    imag_b = (imag_a * twist_cos - real_a * twist_sin).astype(jnp.bfloat16)
    outgoing = jnp.stack([real_b, imag_b]).reshape(2, 2, groups, per_bins, 1, per_dev, width)
    turned = lax.all_to_all(outgoing, ("seq", "fsdp"), split_axis=2, concat_axis=4, tiled=True)
    turned = turned.reshape(2, 2, per_bins, row_count, width)
    real_b = turned[0]
    imag_b = turned[1]
    real_x = (
        jnp.einsum("kqmc,mr->kqrc", real_b, last_cos, preferred_element_type=f32)
        + jnp.einsum("kqmc,mr->kqrc", imag_b, last_sin, preferred_element_type=f32)
    ).astype(jnp.bfloat16)
    imag_x = (
        jnp.einsum("kqmc,mr->kqrc", imag_b, last_cos, preferred_element_type=f32)
        - jnp.einsum("kqmc,mr->kqrc", real_b, last_sin, preferred_element_type=f32)
    ).astype(jnp.bfloat16)
    real_z, imag_z = multiply(real_x, imag_x)
    real_v = jnp.einsum("qrc,mr->qmc", real_z, last_cos, preferred_element_type=f32) - jnp.einsum(
        "qrc,mr->qmc", imag_z, last_sin, preferred_element_type=f32
    )
    imag_v = jnp.einsum("qrc,mr->qmc", imag_z, last_cos, preferred_element_type=f32) + jnp.einsum(
        "qrc,mr->qmc", real_z, last_sin, preferred_element_type=f32
    )
    row_ids, mid_ids = index_grid(per_bins, row_count)
    twist_cos, twist_sin = phase_pair(row_ids + position * per_bins, mid_ids, length)
    twist_cos = twist_cos[:, :, None]
    twist_sin = twist_sin[:, :, None]
    real_w = (real_v * twist_cos - imag_v * twist_sin).astype(jnp.bfloat16)
    imag_w = (imag_v * twist_cos + real_v * twist_sin).astype(jnp.bfloat16)
    backward = jnp.stack([real_w, imag_w]).reshape(2, 1, per_bins, groups, per_dev, width)
    returned = lax.all_to_all(backward, ("seq", "fsdp"), split_axis=3, concat_axis=1, tiled=True)
    returned = returned.reshape(2, period_rows, per_dev, width)
    conv_rows = jnp.einsum(
        "qp,qmc->pmc", first_cos, returned[0], preferred_element_type=f32
    ) - jnp.einsum("qp,qmc->pmc", first_sin, returned[1], preferred_element_type=f32)
    conv_rows = (conv_rows * scale).astype(jnp.bfloat16)
    homed = lax.all_to_all(
        conv_rows.reshape(groups, 1, per_dev, width),
        ("seq", "fsdp"),
        split_axis=0,
        concat_axis=1,
        tiled=True,
    )
    conv = homed.reshape(row_count, width)
    result = query * (conv.astype(jnp.float32) + skip_gain * product.astype(jnp.float32))
    return result.astype(jnp.bfloat16)


def wave_table(size):
    freq, time = np.meshgrid(np.arange(size), np.arange(size), indexing="ij")
    angle = ((2 * freq + 1) * time % (4 * size)) * (math.pi / (2 * size))
    return np.concatenate([np.cos(angle), np.sin(angle)], axis=0)


def exchange(value, axis):
    return lax.ppermute(value, axis, [(0, 1), (1, 0)])


def whole_specs(count):
    return [pl.BlockSpec(memory_space=pltpu.VMEM)] * count


def split_channels(summed, own_half):
    half = summed.shape[1] // 2
    low, high = (summed[:, :half], summed[:, half:])
    first = own_half == 0
    return (jnp.where(first, low, high), jnp.where(first, high, low))


def pick_rows(source, target):
    lines = lax.broadcasted_iota(jnp.int32, (HALO, HALO), 0)
    places = lax.broadcasted_iota(jnp.int32, (HALO, HALO), 1)
    wanted = (lines - target == places - source) & (places >= source) & (places < source + 2)
    return wanted.astype(F32).astype(BF16)


def pack_body(rows_ref, pack_ref, done_ref):
    width = pack_ref.shape[1]
    last = rows_ref[rows_ref.shape[0] - HALO :, :]
    total = jnp.zeros((HALO, width), F32)
    for piece in range(last.shape[1] // width):
        part = last[:, piece * width : (piece + 1) * width]
        total += jnp.dot(pick_rows(HALO - 2, 2 * piece), part, preferred_element_type=F32)
    pack_ref[...] = total.astype(BF16)
    done_ref[...] = jnp.zeros_like(done_ref)


def unpack_halo(pieces, count):
    parts = [
        jnp.dot(pick_rows(2 * piece, HALO - 2), pieces, preferred_element_type=F32).astype(BF16)
        for piece in range(count)
    ]
    return jnp.concatenate(parts, axis=1)


def choose_body(rows_ref, hop_ref, order_ref, send_ref):
    core = lax.axis_index("chan")
    count = send_ref.shape[0]
    lines = pl.ds(pl.multiple_of(core * count, count), count)
    here = core != lax.axis_index("fsdp")
    send_ref[...] = jnp.where(here, rows_ref[lines, :], hop_ref[lines, :])


def load_body(weight_ref, order_ref, weight_out, sems):
    copies = [
        pltpu.make_async_copy(weight_ref.at[branch], weight_out.at[branch], sems.at[branch])
        for branch in range(3)
    ]
    for copy in copies:
        copy.start()
    for copy in copies:
        copy.wait()


def project(rows, weight_ref, own_half, keep_ref, send_ref):
    half = keep_ref.shape[1] // 3
    for branch in range(3):
        summed = jnp.dot(rows, weight_ref[branch], preferred_element_type=F32)
        keep, send = split_channels(summed, own_half)
        keep_ref[:, branch * half : (branch + 1) * half] = keep
        send_ref[:, branch * half : (branch + 1) * half] = send.astype(BF16)


def project_first_body(
    rows_ref, hop_ref, pack_ref, pack_hop_ref, weight_ref, keep_ref, send_ref, done_ref
):
    own_half = lax.axis_index("fsdp")
    here = lax.axis_index("chan") == own_half
    pieces = rows_ref.shape[1] // pack_ref.shape[1]
    rows = jnp.where(here, rows_ref[...], hop_ref[...])
    halo = unpack_halo(jnp.where(here, pack_ref[...], pack_hop_ref[...]), pieces)
    halo = jnp.where(lax.axis_index("seq") > 0, halo, jnp.zeros_like(halo))
    rows = jnp.concatenate([halo, rows], axis=0)
    project(rows, weight_ref, own_half, keep_ref, send_ref)
    done_ref[...] = jnp.zeros_like(done_ref)


def project_second_body(got_ref, hop_ref, weight_ref, keep_ref, send_ref, done_ref):
    own_half = lax.axis_index("fsdp")
    first = lax.axis_index("chan") == 0
    got, hop = (got_ref[...], hop_ref[...])
    rows = jnp.concatenate([jnp.where(first, got, hop), jnp.where(first, hop, got)], axis=0)
    project(rows, weight_ref, own_half, keep_ref, send_ref)
    done_ref[...] = jnp.zeros_like(done_ref)


def pair_taps_body(own_ref, got_ref, *refs):
    pair_ref = refs[-1]
    pair_ref[0] = own_ref[...]
    pair_ref[1] = got_ref[...]


def sort_taps_body(pair_ref, far_ref, *refs):
    keep_ref, send_ref, done_ref = refs[-3:]
    position = lax.axis_index("seq")
    first = lax.axis_index("fsdp") == 0
    blocks, rows, half = keep_ref.shape
    for step in range(blocks):
        block = lax.rem(position - step + blocks, blocks)
        taps = (pair_ref if step < 2 else far_ref)[step % 2]
        low, high = (taps[:, :half], taps[:, half:])
        keep_ref[block] = jnp.where(first, low, high)
        send_ref[block] = jnp.where(first, high, low)
    done_ref[...] = jnp.zeros_like(done_ref)


def after_body(*refs):
    pass


def after(value, *orders):
    return pl.pallas_call(
        after_body,
        in_specs=whole_specs(1 + len(orders)),
        out_specs=whole_specs(1)[0],
        out_shape=shape(value.shape, value.dtype),
        input_output_aliases={0: 0},
        compiler_params=pltpu.CompilerParams(vmem_limit_bytes=32 * 1024 * 1024),
    )(value, *orders)


def taps_body(table_ref, keep_ref, got_ref, real_ref, imag_ref):
    first = lax.axis_index("fsdp") == 0
    blocks = keep_ref.shape[0]
    size = table_ref.shape[1]
    sign = 1.0 - 2.0 * (lax.broadcasted_iota(jnp.int32, (size, 1), 0) % 2).astype(F32)
    sign = sign * (1.0 / size)
    before_real = before_imag = None
    for block in range(blocks):
        keep, got = (keep_ref[block], got_ref[block])
        taps = jnp.concatenate(
            [jnp.where(first, keep, got), jnp.where(first, got, keep)], axis=0
        )
        waves = jnp.dot(table_ref[...], taps, preferred_element_type=F32)
        real, imag = (waves[:size], -waves[size:])
        if block == 0:
            real_ref[block] = real * (1.0 / size)
            imag_ref[block] = imag * (1.0 / size)
        else:
            real_ref[block] = real * (1.0 / size) - sign * before_imag
            imag_ref[block] = imag * (1.0 / size) + sign * before_real
        before_real, before_imag = (real, imag)


def mix_body(keep_first, keep_second, got_first, got_second, short_ref, *refs):
    product_ref, query_ref, joined = refs[-3:]
    own = lax.axis_index("fsdp")
    rows = got_second.shape[0]
    half = got_second.shape[1] // 3
    joined[:HALO, :] = keep_first[:HALO, :] + got_first[:HALO, :].astype(F32)
    own_start = pl.multiple_of(HALO + own * rows, HALO)
    other_start = pl.multiple_of(HALO + (1 - own) * rows, HALO)
    joined[pl.ds(own_start, rows), :] = keep_first[HALO:, :] + got_second[:, :].astype(F32)
    joined[pl.ds(other_start, rows), :] = keep_second[:, :] + got_first[HALO:, :].astype(F32)
    count = 2 * rows
    mixed = []
    for branch in range(3):
        lanes = slice(branch * half, (branch + 1) * half)
        total = None
        for tap in range(3):
            taps = short_ref[tap, branch : branch + 1, :]
            taps = jnp.where(own == 0, taps[:, :half], taps[:, half:])
            term = taps * joined[pl.ds(HALO - tap, count), lanes]
            total = term if total is None else total + term
        mixed.append(total)
    query_ref[...] = mixed[0]
    product_ref[...] = (mixed[1] * mixed[2]).astype(BF16)


def conv_body(own_ref, one_ref, two_ref, three_ref, real_ref, imag_ref, table_ref, turned_ref,
              query_ref, gain_ref, stay_ref, go_ref, result):
    position = lax.axis_index("seq")
    own = lax.axis_index("fsdp")
    size = table_ref.shape[1]
    total_real = total_imag = None
    for step, block_ref in enumerate((own_ref, one_ref, two_ref, three_ref)):
        block = block_ref[...]
        if step:
            block = jnp.where(position >= step, block, jnp.zeros_like(block))
        waves = jnp.dot(table_ref[...], block, preferred_element_type=F32)
        real, imag = (waves[:size], -waves[size:])
        term_real = real * real_ref[step] - imag * imag_ref[step]
        term_imag = real * imag_ref[step] + imag * real_ref[step]
        total_real = term_real if total_real is None else total_real + term_real
        total_imag = term_imag if total_imag is None else total_imag + term_imag
    stacked = jnp.concatenate([total_real, -total_imag], axis=0).astype(BF16)
    conv = jnp.dot(turned_ref[...], stacked, preferred_element_type=F32)
    half = own_ref.shape[1]
    gain = jnp.where(own == 0, gain_ref[:, :half], gain_ref[:, half:])
    gated = query_ref[...] * (conv + gain * own_ref[...].astype(F32))
    result[...] = gated.astype(BF16)
    rows = stay_ref.shape[0]
    stay_ref[...] = result[pl.ds(pl.multiple_of(own * rows, rows), rows), :]
    go_ref[...] = result[pl.ds(pl.multiple_of((1 - own) * rows, rows), rows), :]


def join_body(stay_ref, got_ref, out_ref):
    first = lax.axis_index("fsdp") == 0
    half = stay_ref.shape[1]
    out_ref[:, :half] = jnp.where(first, stay_ref[...], got_ref[...])
    out_ref[:, half:] = jnp.where(first, got_ref[...], stay_ref[...])


def shape(dims, kind):
    return jax.ShapeDtypeStruct(dims, kind)


def pair_mesh(tokens, proj_weight, short_weight, skip_gain, filter_taps):
    rows = tokens.shape[0]
    features = proj_weight.shape[0]
    width = proj_weight.shape[2]
    half = width // 2
    size = 2 * rows
    blocks = lax.axis_size("seq")
    weight = jnp.transpose(proj_weight, (1, 0, 2))
    ring = [[(s, (s + step) % blocks) for s in range(blocks)] for step in range(blocks)]
    call = functools.partial(
        pl.pallas_call, compiler_params=pltpu.CompilerParams(vmem_limit_bytes=32 * 1024 * 1024)
    )

    own_hop = exchange(tokens, "chan")
    token = shape((8, 128), F32)
    pack, pack_done = call(
        pack_body,
        in_specs=whole_specs(1),
        out_specs=whole_specs(2),
        out_shape=(shape((HALO, width), BF16), token),
    )(tokens)
    token_send = call(
        choose_body,
        in_specs=whole_specs(3),
        out_specs=whole_specs(1)[0],
        out_shape=shape((rows // 2, features), BF16),
    )(tokens, own_hop, pack_done)
    got = exchange(token_send, "fsdp")
    tap_near = lax.ppermute(filter_taps, "seq", ring[1])
    weight = pl.pallas_call(
        load_body,
        in_specs=[pl.BlockSpec(memory_space=pltpu.HBM), *whole_specs(1)],
        out_specs=whole_specs(1)[0],
        out_shape=shape(weight.shape, BF16),
        scratch_shapes=[pltpu.SemaphoreType.DMA((3,))],
        compiler_params=pltpu.CompilerParams(vmem_limit_bytes=LOAD_MIB * 1024 * 1024),
    )(weight, pack_done)
    pack_got = lax.ppermute(
        pack,
        ("seq", "fsdp", "chan"),
        [
            (4 * s + 2 * f + c, 4 * ((s + 1) % blocks) + 2 * (f ^ (1 - c)) + c)
            for s in range(blocks)
            for f in range(2)
            for c in range(2)
        ],
    )
    tap_pair = call(
        pair_taps_body,
        in_specs=whole_specs(2),
        out_specs=whole_specs(1)[0],
        out_shape=shape((2, rows, width), BF16),
    )(filter_taps, tap_near)
    pack_got = after(pack_got, weight)
    pack_hop = exchange(pack_got, "chan")
    keep_first, send_first, first_done = call(
        project_first_body,
        in_specs=whole_specs(5),
        out_specs=whole_specs(3),
        out_shape=(
            shape((HALO + rows, 3 * half), F32),
            shape((HALO + rows, 3 * half), BF16),
            token,
        ),
    )(tokens, own_hop, pack_got, pack_hop, weight)
    got = after(got, first_done, tap_pair)
    got_hop = exchange(got, "chan")
    got_first = exchange(send_first, "fsdp")
    keep_second, send_second, second_done = call(
        project_second_body,
        in_specs=whole_specs(3),
        out_specs=whole_specs(3),
        out_shape=(shape((rows, 3 * half), F32), shape((rows, 3 * half), BF16), token),
    )(got, got_hop, weight)
    got_second = exchange(send_second, "fsdp")
    tap_far = lax.ppermute(tap_pair, "seq", ring[2])

    tap_keep, tap_send, tap_done = call(
        sort_taps_body,
        in_specs=whole_specs(2 + 1),
        out_specs=whole_specs(3),
        out_shape=(
            shape((blocks, rows, half), BF16),
            shape((blocks, rows, half), BF16),
            token,
        ),
    )(tap_pair, tap_far, second_done)
    tap_got = exchange(tap_send, "fsdp")
    table = wave_table(size)
    forward = jnp.asarray(table, dtype=BF16)
    inverse = jnp.asarray(table.T, dtype=BF16)
    product, query = call(
        mix_body,
        in_specs=whole_specs(6),
        out_specs=whole_specs(2),
        out_shape=(shape((size, half), BF16), shape((size, half), F32)),
        scratch_shapes=[pltpu.VMEM((HALO + size, 3 * half), F32)],
    )(keep_first, keep_second, got_first, got_second, short_weight, tap_done)

    products = [product] + [lax.ppermute(product, "seq", ring[step]) for step in range(1, blocks)]
    tap_real, tap_imag = call(
        taps_body,
        in_specs=whole_specs(3),
        out_specs=whole_specs(2),
        out_shape=(shape((blocks, size, half), F32), shape((blocks, size, half), F32)),
    )(forward, tap_keep, tap_got)
    stay, go = call(
        conv_body,
        in_specs=whole_specs(10),
        out_specs=whole_specs(2),
        out_shape=(shape((rows, half), BF16), shape((rows, half), BF16)),
        scratch_shapes=[pltpu.VMEM((size, half), BF16)],
    )(*products, tap_real, tap_imag, forward, inverse, query, skip_gain.reshape(1, width))
    back = exchange(go, "fsdp")
    return call(
        join_body,
        in_specs=whole_specs(2),
        out_specs=whole_specs(1)[0],
        out_shape=shape((rows, width), BF16),
    )(stay, back)


def solution(mesh):
    in_specs = (
        P(("grp", "seq", "fsdp"), "chan"),
        P("fsdp", None, "chan"),
        P(None, None, "chan"),
        P("chan"),
        P(("seq", "fsdp"), "chan"),
    )
    out_specs = P(("grp", "seq", "fsdp"), "chan")
    sizes = mesh.shape
    paired = sizes["fsdp"] == 2 and sizes["chan"] == 2 and sizes["seq"] == 4
    per_device = pair_mesh if paired else any_mesh
    return jax.shard_map(
        per_device, mesh=mesh, in_specs=in_specs, out_specs=out_specs, check_vma=False
    )
```

```python
import functools
import math

import jax
import jax.numpy as jnp
import numpy as np
from jax import lax
from jax.experimental import pallas as pl
from jax.experimental.pallas import tpu as pltpu
from jax.sharding import PartitionSpec as P

HALO = 16
PAD = 32
F32 = jnp.float32
BF16 = jnp.bfloat16


def shifted(value, axis, steps):
    count = lax.axis_size(axis)
    initial, last = (max(0, -steps), min(count, count - steps))
    return lax.ppermute(value, axis, [(source, source + steps) for source in range(initial, last)])


def index_grid(row_count, col_count):
    return (
        lax.broadcasted_iota(jnp.int32, (row_count, col_count), 0),
        lax.broadcasted_iota(jnp.int32, (row_count, col_count), 1),
    )


def phase_pair(row_ids, col_ids, period):
    wrapped = row_ids * col_ids % period
    phase = wrapped.astype(jnp.float32) * (2.0 * math.pi / period)
    return (jnp.cos(phase), jnp.sin(phase))


def multiply(real_x, imag_x):
    sig_real = real_x[0].astype(jnp.float32)
    sig_imag = imag_x[0].astype(jnp.float32)
    tap_real = real_x[1].astype(jnp.float32)
    tap_imag = imag_x[1].astype(jnp.float32)
    real_z = (sig_real * tap_real - sig_imag * tap_imag).astype(jnp.bfloat16)
    imag_z = (sig_real * tap_imag + sig_imag * tap_real).astype(jnp.bfloat16)
    return (real_z, imag_z)


def spread(stacked, groups, inner_shape):
    shaped = stacked.reshape((2, groups, 1) + inner_shape)
    moved = lax.all_to_all(shaped, ("seq", "fsdp"), split_axis=1, concat_axis=2, tiled=True)
    return moved.reshape((2, groups) + inner_shape)


def any_mesh(tokens, proj_weight, short_weight, skip_gain, filter_taps):
    whole = lax.all_gather(tokens, "chan", axis=1, tiled=True)
    row_count = whole.shape[0]
    width = proj_weight.shape[2]
    flat_width = 3 * width
    piece = lax.all_gather(proj_weight, "fsdp", axis=0, tiled=True)
    summed = jnp.dot(
        whole, piece.reshape(piece.shape[0], flat_width), preferred_element_type=jnp.float32
    )
    projected = summed.astype(jnp.bfloat16).reshape(row_count, 3, width)
    earlier = shifted(projected[row_count - 2 :], ("seq", "fsdp"), 1)
    extended = jnp.concatenate([earlier, projected], axis=0).astype(jnp.float32)
    mixed = (
        short_weight[0] * extended[2:]
        + short_weight[1] * extended[1:-1]
        + short_weight[2] * extended[:-2]
    )
    query = mixed[:, 0]
    product = (mixed[:, 1] * mixed[:, 2]).astype(jnp.bfloat16)
    groups = lax.axis_size(("seq", "fsdp"))
    position = lax.axis_index(("seq", "fsdp"))
    period_rows = 2 * groups
    length = period_rows * row_count
    scale = 1.0 / length
    bin_ids, tap_ids = index_grid(period_rows, groups)
    first_cos, first_sin = phase_pair(bin_ids, tap_ids, period_rows)
    first_cos = first_cos.astype(jnp.bfloat16)
    first_sin = first_sin.astype(jnp.bfloat16)
    col_ids, freq_ids = index_grid(row_count, row_count)
    last_cos, last_sin = phase_pair(col_ids, freq_ids, row_count)
    last_cos = last_cos.astype(jnp.bfloat16)
    last_sin = last_sin.astype(jnp.bfloat16)
    stacked = jnp.stack([product, filter_taps])
    f32 = jnp.float32
    per_dev = row_count // groups
    per_bins = period_rows // groups
    arrived = spread(stacked.reshape(2, groups, per_dev, width), groups, (per_dev, width))
    real_a = jnp.einsum("qp,kpmc->kqmc", first_cos, arrived, preferred_element_type=f32)
    imag_a = -jnp.einsum("qp,kpmc->kqmc", first_sin, arrived, preferred_element_type=f32)
    row_ids, mid_ids = index_grid(period_rows, per_dev)
    twist_cos, twist_sin = phase_pair(row_ids, mid_ids + position * per_dev, length)
    twist_cos = twist_cos[:, :, None]
    twist_sin = twist_sin[:, :, None]
    real_b = (real_a * twist_cos + imag_a * twist_sin).astype(jnp.bfloat16)
    imag_b = (imag_a * twist_cos - real_a * twist_sin).astype(jnp.bfloat16)
    outgoing = jnp.stack([real_b, imag_b]).reshape(2, 2, groups, per_bins, 1, per_dev, width)
    turned = lax.all_to_all(outgoing, ("seq", "fsdp"), split_axis=2, concat_axis=4, tiled=True)
    turned = turned.reshape(2, 2, per_bins, row_count, width)
    real_b = turned[0]
    imag_b = turned[1]
    real_x = (
        jnp.einsum("kqmc,mr->kqrc", real_b, last_cos, preferred_element_type=f32)
        + jnp.einsum("kqmc,mr->kqrc", imag_b, last_sin, preferred_element_type=f32)
    ).astype(jnp.bfloat16)
    imag_x = (
        jnp.einsum("kqmc,mr->kqrc", imag_b, last_cos, preferred_element_type=f32)
        - jnp.einsum("kqmc,mr->kqrc", real_b, last_sin, preferred_element_type=f32)
    ).astype(jnp.bfloat16)
    real_z, imag_z = multiply(real_x, imag_x)
    real_v = jnp.einsum("qrc,mr->qmc", real_z, last_cos, preferred_element_type=f32) - jnp.einsum(
        "qrc,mr->qmc", imag_z, last_sin, preferred_element_type=f32
    )
    imag_v = jnp.einsum("qrc,mr->qmc", imag_z, last_cos, preferred_element_type=f32) + jnp.einsum(
        "qrc,mr->qmc", real_z, last_sin, preferred_element_type=f32
    )
    row_ids, mid_ids = index_grid(per_bins, row_count)
    twist_cos, twist_sin = phase_pair(row_ids + position * per_bins, mid_ids, length)
    twist_cos = twist_cos[:, :, None]
    twist_sin = twist_sin[:, :, None]
    real_w = (real_v * twist_cos - imag_v * twist_sin).astype(jnp.bfloat16)
    imag_w = (imag_v * twist_cos + real_v * twist_sin).astype(jnp.bfloat16)
    backward = jnp.stack([real_w, imag_w]).reshape(2, 1, per_bins, groups, per_dev, width)
    returned = lax.all_to_all(backward, ("seq", "fsdp"), split_axis=3, concat_axis=1, tiled=True)
    returned = returned.reshape(2, period_rows, per_dev, width)
    conv_rows = jnp.einsum(
        "qp,qmc->pmc", first_cos, returned[0], preferred_element_type=f32
    ) - jnp.einsum("qp,qmc->pmc", first_sin, returned[1], preferred_element_type=f32)
    conv_rows = (conv_rows * scale).astype(jnp.bfloat16)
    homed = lax.all_to_all(
        conv_rows.reshape(groups, 1, per_dev, width),
        ("seq", "fsdp"),
        split_axis=0,
        concat_axis=1,
        tiled=True,
    )
    conv = homed.reshape(row_count, width)
    result = query * (conv.astype(jnp.float32) + skip_gain * product.astype(jnp.float32))
    return result.astype(jnp.bfloat16)


def wave_table(size):
    freq, time = np.meshgrid(np.arange(size), np.arange(size), indexing="ij")
    angle = ((2 * freq + 1) * time % (4 * size)) * (math.pi / (2 * size))
    return np.concatenate([np.cos(angle), np.sin(angle)], axis=0)


def exchange(value, axis):
    return lax.ppermute(value, axis, [(0, 1), (1, 0)])


def whole_specs(count):
    return [pl.BlockSpec(memory_space=pltpu.VMEM)] * count


def split_channels(summed, own_half):
    half = summed.shape[1] // 2
    low, high = (summed[:, :half], summed[:, half:])
    first = own_half == 0
    return (jnp.where(first, low, high), jnp.where(first, high, low))


def pick_rows(source, target):
    lines = lax.broadcasted_iota(jnp.int32, (HALO, HALO), 0)
    places = lax.broadcasted_iota(jnp.int32, (HALO, HALO), 1)
    wanted = (lines - target == places - source) & (places >= source) & (places < source + 2)
    return wanted.astype(F32).astype(BF16)


def pack_body(rows_ref, pack_ref):
    width = pack_ref.shape[1]
    last = rows_ref[rows_ref.shape[0] - HALO :, :]
    total = jnp.zeros((HALO, width), F32)
    for piece in range(last.shape[1] // width):
        part = last[:, piece * width : (piece + 1) * width]
        total += jnp.dot(pick_rows(HALO - 2, 2 * piece), part, preferred_element_type=F32)
    pack_ref[...] = total.astype(BF16)


def unpack_halo(pieces, count):
    parts = [
        jnp.dot(pick_rows(2 * piece, HALO - 2), pieces, preferred_element_type=F32).astype(BF16)
        for piece in range(count)
    ]
    return jnp.concatenate(parts, axis=1)


def project(rows, weight_ref, own_half, keep_ref, send_ref):
    half = keep_ref.shape[1] // 3
    for branch in range(3):
        summed = jnp.dot(rows, weight_ref[branch], preferred_element_type=F32)
        keep, send = split_channels(summed, own_half)
        lanes = slice(branch * half, (branch + 1) * half)
        keep_ref[:, lanes] = keep
        send_ref[: send.shape[0], lanes] = send.astype(BF16)


def project_first_body(rows_ref, cycled_ref, weight_ref, keep_ref, send_ref):
    own_half = lax.axis_index("fsdp")
    here = lax.axis_index("chan") == own_half
    rows = jnp.where(here, rows_ref[...], cycled_ref[...])
    project(rows, weight_ref, own_half, keep_ref, send_ref)


def project_second_body(
    cycled_ref, hop_ref, pack_ref, pack_hop_ref, weight_ref, keep_ref, send_ref, done_ref
):
    own_half = lax.axis_index("fsdp")
    here = lax.axis_index("chan") == own_half
    pieces = cycled_ref.shape[1] // pack_ref.shape[1]
    rows = jnp.where(here, cycled_ref[...], hop_ref[...])
    halo = unpack_halo(jnp.where(here, pack_ref[...], pack_hop_ref[...]), pieces)
    halo = jnp.where(lax.axis_index("seq") > 0, halo, jnp.zeros_like(halo))
    rows = jnp.concatenate([halo, rows], axis=0)
    project(rows, weight_ref, own_half, keep_ref, send_ref)
    done_ref[...] = jnp.zeros_like(done_ref)


def sort_taps_body(*refs):
    keep_ref, send_ref, done_ref = refs[-3:]
    position = lax.axis_index("seq")
    first = lax.axis_index("fsdp") == 0
    blocks, _, half = keep_ref.shape
    for step in range(blocks):
        block = lax.rem(position - step + blocks, blocks)
        taps = refs[step][...]
        low, high = (taps[:, :half], taps[:, half:])
        keep_ref[block] = jnp.where(first, low, high)
        send_ref[block] = jnp.where(first, high, low)
    done_ref[...] = jnp.zeros_like(done_ref)


def after_body(*refs):
    pass


def after(value, *orders):
    return pl.pallas_call(
        after_body,
        in_specs=whole_specs(1 + len(orders)),
        out_specs=whole_specs(1)[0],
        out_shape=shape(value.shape, value.dtype),
        input_output_aliases={0: 0},
        compiler_params=pltpu.CompilerParams(vmem_limit_bytes=32 * 1024 * 1024),
    )(value, *orders)


def taps_body(table_ref, keep_ref, got_ref, real_ref, imag_ref):
    first = lax.axis_index("fsdp") == 0
    blocks = keep_ref.shape[0]
    size = table_ref.shape[1]
    sign = 1.0 - 2.0 * (lax.broadcasted_iota(jnp.int32, (size, 1), 0) % 2).astype(F32)
    sign = sign * (1.0 / size)
    before_real = before_imag = None
    for block in range(blocks):
        keep, got = (keep_ref[block], got_ref[block])
        taps = jnp.concatenate(
            [jnp.where(first, keep, got), jnp.where(first, got, keep)], axis=0
        )
        waves = jnp.dot(table_ref[...], taps, preferred_element_type=F32)
        real, imag = (waves[:size], -waves[size:])
        if block == 0:
            real_ref[block] = real * (1.0 / size)
            imag_ref[block] = imag * (1.0 / size)
        else:
            real_ref[block] = real * (1.0 / size) - sign * before_imag
            imag_ref[block] = imag * (1.0 / size) + sign * before_real
        before_real, before_imag = (real, imag)


def mix_body(keep_first, keep_second, got_first, got_second, short_ref, order_ref,
             product_ref, query_ref, joined):
    own = lax.axis_index("fsdp")
    rows = keep_first.shape[0]
    half = keep_first.shape[1] // 3
    joined[:HALO, :] = keep_second[:HALO, :] + got_second[:HALO, :].astype(F32)
    own_start = pl.multiple_of(HALO + own * rows, HALO)
    other_start = pl.multiple_of(HALO + (1 - own) * rows, HALO)
    joined[pl.ds(own_start, rows), :] = keep_first[...] + got_second[HALO:, :].astype(F32)
    joined[pl.ds(other_start, rows), :] = keep_second[HALO:, :] + got_first[:rows, :].astype(F32)
    count = 2 * rows
    mixed = []
    for branch in range(3):
        lanes = slice(branch * half, (branch + 1) * half)
        total = None
        for tap in range(3):
            taps = short_ref[tap, branch : branch + 1, :]
            taps = jnp.where(own == 0, taps[:, :half], taps[:, half:])
            term = taps * joined[pl.ds(HALO - tap, count), lanes]
            total = term if total is None else total + term
        mixed.append(total)
    query_ref[...] = mixed[0]
    product_ref[...] = (mixed[1] * mixed[2]).astype(BF16)


def conv_body(own_ref, one_ref, two_ref, three_ref, real_ref, imag_ref, table_ref, turned_ref,
              query_ref, gain_ref, stay_ref, go_ref, result):
    position = lax.axis_index("seq")
    own = lax.axis_index("fsdp")
    size = table_ref.shape[1]
    total_real = total_imag = None
    for step, block_ref in enumerate((own_ref, one_ref, two_ref, three_ref)):
        block = block_ref[...]
        if step:
            block = jnp.where(position >= step, block, jnp.zeros_like(block))
        waves = jnp.dot(table_ref[...], block, preferred_element_type=F32)
        real, imag = (waves[:size], -waves[size:])
        term_real = real * real_ref[step] - imag * imag_ref[step]
        term_imag = real * imag_ref[step] + imag * real_ref[step]
        total_real = term_real if total_real is None else total_real + term_real
        total_imag = term_imag if total_imag is None else total_imag + term_imag
    stacked = jnp.concatenate([total_real, -total_imag], axis=0).astype(BF16)
    conv = jnp.dot(turned_ref[...], stacked, preferred_element_type=F32)
    half = own_ref.shape[1]
    gain = jnp.where(own == 0, gain_ref[:, :half], gain_ref[:, half:])
    gated = query_ref[...] * (conv + gain * own_ref[...].astype(F32))
    result[...] = gated.astype(BF16)
    rows = stay_ref.shape[0]
    stay_ref[...] = result[pl.ds(pl.multiple_of(own * rows, rows), rows), :]
    go_ref[...] = result[pl.ds(pl.multiple_of((1 - own) * rows, rows), rows), :]


def join_body(stay_ref, got_ref, out_ref):
    first = lax.axis_index("fsdp") == 0
    half = stay_ref.shape[1]
    out_ref[:, :half] = jnp.where(first, stay_ref[...], got_ref[...])
    out_ref[:, half:] = jnp.where(first, got_ref[...], stay_ref[...])


def shape(dims, kind):
    return jax.ShapeDtypeStruct(dims, kind)


def pair_mesh(tokens, proj_weight, short_weight, skip_gain, filter_taps):
    rows = tokens.shape[0]
    width = proj_weight.shape[2]
    half = width // 2
    size = 2 * rows
    blocks = lax.axis_size("seq")
    weight = jnp.transpose(proj_weight, (1, 0, 2))
    ring = [[(s, (s + step) % blocks) for s in range(blocks)] for step in range(blocks)]
    call = functools.partial(
        pl.pallas_call, compiler_params=pltpu.CompilerParams(vmem_limit_bytes=32 * 1024 * 1024)
    )

    cycled = lax.ppermute(tokens, ("fsdp", "chan"), [(1, 3), (3, 2), (2, 0), (0, 1)])
    token = shape((8, 128), F32)
    pack = call(
        pack_body,
        cost_estimate=pl.CostEstimate(flops=10_000_000_000, bytes_accessed=40_000_000, transcendentals=0),
        in_specs=whole_specs(1),
        out_specs=whole_specs(1)[0],
        out_shape=shape((HALO, width), BF16),
    )(tokens)
    pack_got = lax.ppermute(
        pack,
        ("seq", "fsdp", "chan"),
        [
            (4 * s + 2 * f + c, 4 * ((s + 1) % blocks) + 2 * (f ^ (1 - c)) + c)
            for s in range(blocks)
            for f in range(2)
            for c in range(2)
        ],
    )
    tap_blocks = [filter_taps] + [
        lax.ppermute(filter_taps, "seq", ring[step]) for step in range(1, blocks)
    ]
    cycled = after(cycled, pack_got)
    hop = exchange(cycled, "chan")
    pack_hop = exchange(pack_got, "chan")
    keep_first, send_first = call(
        project_first_body,
        cost_estimate=pl.CostEstimate(flops=10_000_000_000, bytes_accessed=40_000_000, transcendentals=0),
        in_specs=whole_specs(3),
        out_specs=whole_specs(2),
        out_shape=(shape((rows, 3 * half), F32), shape((rows + PAD, 3 * half), BF16)),
    )(tokens, cycled, weight)
    got_first = exchange(send_first, "fsdp")
    keep_second, send_second, second_done = call(
        project_second_body,
        in_specs=whole_specs(5),
        out_specs=whole_specs(3),
        out_shape=(
            shape((HALO + rows, 3 * half), F32),
            shape((HALO + rows, 3 * half), BF16),
            token,
        ),
    )(cycled, hop, pack_got, pack_hop, weight)
    got_second = exchange(send_second, "fsdp")
    tap_keep, tap_send, tap_done = call(
        sort_taps_body,
        in_specs=whole_specs(1 + blocks),
        out_specs=whole_specs(3),
        out_shape=(
            shape((blocks, rows, half), BF16),
            shape((blocks, rows, half), BF16),
            token,
        ),
    )(*tap_blocks, second_done)
    tap_got = exchange(tap_send, "fsdp")

    product, query = call(
        mix_body,
        in_specs=whole_specs(6),
        out_specs=whole_specs(2),
        out_shape=(shape((size, half), BF16), shape((size, half), F32)),
        scratch_shapes=[pltpu.VMEM((HALO + size, 3 * half), F32)],
    )(keep_first, keep_second, got_first, got_second, short_weight, tap_done)

    products = [product] + [lax.ppermute(product, "seq", ring[step]) for step in range(1, blocks)]
    table = wave_table(size)
    forward = jnp.asarray(table, dtype=BF16)
    inverse = jnp.asarray(table.T, dtype=BF16)
    tap_real, tap_imag = call(
        taps_body,
        in_specs=whole_specs(3),
        out_specs=whole_specs(2),
        out_shape=(shape((blocks, size, half), F32), shape((blocks, size, half), F32)),
    )(forward, tap_keep, tap_got)
    stay, go = call(
        conv_body,
        in_specs=whole_specs(10),
        out_specs=whole_specs(2),
        out_shape=(shape((rows, half), BF16), shape((rows, half), BF16)),
        scratch_shapes=[pltpu.VMEM((size, half), BF16)],
    )(*products, tap_real, tap_imag, forward, inverse, query, skip_gain.reshape(1, width))
    back = exchange(go, "fsdp")
    return call(
        join_body,
        in_specs=whole_specs(2),
        out_specs=whole_specs(1)[0],
        out_shape=shape((rows, width), BF16),
    )(stay, back)


def solution(mesh):
    in_specs = (
        P(("grp", "seq", "fsdp"), "chan"),
        P("fsdp", None, "chan"),
        P(None, None, "chan"),
        P("chan"),
        P(("seq", "fsdp"), "chan"),
    )
    out_specs = P(("grp", "seq", "fsdp"), "chan")
    sizes = mesh.shape
    paired = sizes["fsdp"] == 2 and sizes["chan"] == 2 and sizes["seq"] == 4
    per_device = pair_mesh if paired else any_mesh
    return jax.shard_map(
        per_device, mesh=mesh, in_specs=in_specs, out_specs=out_specs, check_vma=False
    )
```

```python
import functools
import math

import jax
import jax.numpy as jnp
import numpy as np
from jax import lax
from jax.experimental import pallas as pl
from jax.experimental.pallas import tpu as pltpu
from jax.sharding import PartitionSpec as P

HALO = 16
LONG = pl.CostEstimate(flops=10_000_000_000, bytes_accessed=40_000_000, transcendentals=0)
F32 = jnp.float32
BF16 = jnp.bfloat16


def shifted(value, axis, steps):
    count = lax.axis_size(axis)
    initial, last = (max(0, -steps), min(count, count - steps))
    return lax.ppermute(value, axis, [(source, source + steps) for source in range(initial, last)])


def index_grid(row_count, col_count):
    return (
        lax.broadcasted_iota(jnp.int32, (row_count, col_count), 0),
        lax.broadcasted_iota(jnp.int32, (row_count, col_count), 1),
    )


def phase_pair(row_ids, col_ids, period):
    wrapped = row_ids * col_ids % period
    phase = wrapped.astype(jnp.float32) * (2.0 * math.pi / period)
    return (jnp.cos(phase), jnp.sin(phase))


def multiply(real_x, imag_x):
    sig_real = real_x[0].astype(jnp.float32)
    sig_imag = imag_x[0].astype(jnp.float32)
    tap_real = real_x[1].astype(jnp.float32)
    tap_imag = imag_x[1].astype(jnp.float32)
    real_z = (sig_real * tap_real - sig_imag * tap_imag).astype(jnp.bfloat16)
    imag_z = (sig_real * tap_imag + sig_imag * tap_real).astype(jnp.bfloat16)
    return (real_z, imag_z)


def spread(stacked, groups, inner_shape):
    shaped = stacked.reshape((2, groups, 1) + inner_shape)
    moved = lax.all_to_all(shaped, ("seq", "fsdp"), split_axis=1, concat_axis=2, tiled=True)
    return moved.reshape((2, groups) + inner_shape)


def any_mesh(tokens, proj_weight, short_weight, skip_gain, filter_taps):
    whole = lax.all_gather(tokens, "chan", axis=1, tiled=True)
    row_count = whole.shape[0]
    width = proj_weight.shape[2]
    flat_width = 3 * width
    piece = lax.all_gather(proj_weight, "fsdp", axis=0, tiled=True)
    summed = jnp.dot(
        whole, piece.reshape(piece.shape[0], flat_width), preferred_element_type=jnp.float32
    )
    projected = summed.astype(jnp.bfloat16).reshape(row_count, 3, width)
    earlier = shifted(projected[row_count - 2 :], ("seq", "fsdp"), 1)
    extended = jnp.concatenate([earlier, projected], axis=0).astype(jnp.float32)
    mixed = (
        short_weight[0] * extended[2:]
        + short_weight[1] * extended[1:-1]
        + short_weight[2] * extended[:-2]
    )
    query = mixed[:, 0]
    product = (mixed[:, 1] * mixed[:, 2]).astype(jnp.bfloat16)
    groups = lax.axis_size(("seq", "fsdp"))
    position = lax.axis_index(("seq", "fsdp"))
    period_rows = 2 * groups
    length = period_rows * row_count
    scale = 1.0 / length
    bin_ids, tap_ids = index_grid(period_rows, groups)
    first_cos, first_sin = phase_pair(bin_ids, tap_ids, period_rows)
    first_cos = first_cos.astype(jnp.bfloat16)
    first_sin = first_sin.astype(jnp.bfloat16)
    col_ids, freq_ids = index_grid(row_count, row_count)
    last_cos, last_sin = phase_pair(col_ids, freq_ids, row_count)
    last_cos = last_cos.astype(jnp.bfloat16)
    last_sin = last_sin.astype(jnp.bfloat16)
    stacked = jnp.stack([product, filter_taps])
    f32 = jnp.float32
    per_dev = row_count // groups
    per_bins = period_rows // groups
    arrived = spread(stacked.reshape(2, groups, per_dev, width), groups, (per_dev, width))
    real_a = jnp.einsum("qp,kpmc->kqmc", first_cos, arrived, preferred_element_type=f32)
    imag_a = -jnp.einsum("qp,kpmc->kqmc", first_sin, arrived, preferred_element_type=f32)
    row_ids, mid_ids = index_grid(period_rows, per_dev)
    twist_cos, twist_sin = phase_pair(row_ids, mid_ids + position * per_dev, length)
    twist_cos = twist_cos[:, :, None]
    twist_sin = twist_sin[:, :, None]
    real_b = (real_a * twist_cos + imag_a * twist_sin).astype(jnp.bfloat16)
    imag_b = (imag_a * twist_cos - real_a * twist_sin).astype(jnp.bfloat16)
    outgoing = jnp.stack([real_b, imag_b]).reshape(2, 2, groups, per_bins, 1, per_dev, width)
    turned = lax.all_to_all(outgoing, ("seq", "fsdp"), split_axis=2, concat_axis=4, tiled=True)
    turned = turned.reshape(2, 2, per_bins, row_count, width)
    real_b = turned[0]
    imag_b = turned[1]
    real_x = (
        jnp.einsum("kqmc,mr->kqrc", real_b, last_cos, preferred_element_type=f32)
        + jnp.einsum("kqmc,mr->kqrc", imag_b, last_sin, preferred_element_type=f32)
    ).astype(jnp.bfloat16)
    imag_x = (
        jnp.einsum("kqmc,mr->kqrc", imag_b, last_cos, preferred_element_type=f32)
        - jnp.einsum("kqmc,mr->kqrc", real_b, last_sin, preferred_element_type=f32)
    ).astype(jnp.bfloat16)
    real_z, imag_z = multiply(real_x, imag_x)
    real_v = jnp.einsum("qrc,mr->qmc", real_z, last_cos, preferred_element_type=f32) - jnp.einsum(
        "qrc,mr->qmc", imag_z, last_sin, preferred_element_type=f32
    )
    imag_v = jnp.einsum("qrc,mr->qmc", imag_z, last_cos, preferred_element_type=f32) + jnp.einsum(
        "qrc,mr->qmc", real_z, last_sin, preferred_element_type=f32
    )
    row_ids, mid_ids = index_grid(per_bins, row_count)
    twist_cos, twist_sin = phase_pair(row_ids + position * per_bins, mid_ids, length)
    twist_cos = twist_cos[:, :, None]
    twist_sin = twist_sin[:, :, None]
    real_w = (real_v * twist_cos - imag_v * twist_sin).astype(jnp.bfloat16)
    imag_w = (imag_v * twist_cos + real_v * twist_sin).astype(jnp.bfloat16)
    backward = jnp.stack([real_w, imag_w]).reshape(2, 1, per_bins, groups, per_dev, width)
    returned = lax.all_to_all(backward, ("seq", "fsdp"), split_axis=3, concat_axis=1, tiled=True)
    returned = returned.reshape(2, period_rows, per_dev, width)
    conv_rows = jnp.einsum(
        "qp,qmc->pmc", first_cos, returned[0], preferred_element_type=f32
    ) - jnp.einsum("qp,qmc->pmc", first_sin, returned[1], preferred_element_type=f32)
    conv_rows = (conv_rows * scale).astype(jnp.bfloat16)
    homed = lax.all_to_all(
        conv_rows.reshape(groups, 1, per_dev, width),
        ("seq", "fsdp"),
        split_axis=0,
        concat_axis=1,
        tiled=True,
    )
    conv = homed.reshape(row_count, width)
    result = query * (conv.astype(jnp.float32) + skip_gain * product.astype(jnp.float32))
    return result.astype(jnp.bfloat16)


def wave_table(size):
    freq, time = np.meshgrid(np.arange(size), np.arange(size), indexing="ij")
    angle = ((2 * freq + 1) * time % (4 * size)) * (math.pi / (2 * size))
    return np.concatenate([np.cos(angle), np.sin(angle)], axis=0)


def exchange(value, axis):
    return lax.ppermute(value, axis, [(0, 1), (1, 0)])


def whole_specs(count):
    return [pl.BlockSpec(memory_space=pltpu.VMEM)] * count


def split_channels(summed, own_half):
    half = summed.shape[1] // 2
    low, high = (summed[:, :half], summed[:, half:])
    first = own_half == 0
    return (jnp.where(first, low, high), jnp.where(first, high, low))


def pick_rows(source, target):
    lines = lax.broadcasted_iota(jnp.int32, (HALO, HALO), 0)
    places = lax.broadcasted_iota(jnp.int32, (HALO, HALO), 1)
    wanted = (lines - target == places - source) & (places >= source) & (places < source + 2)
    return wanted.astype(F32).astype(BF16)


def pack_body(rows_ref, pack_ref):
    width = pack_ref.shape[1]
    last = rows_ref[rows_ref.shape[0] - HALO :, :]
    total = jnp.zeros((HALO, width), F32)
    for piece in range(last.shape[1] // width):
        part = last[:, piece * width : (piece + 1) * width]
        total += jnp.dot(pick_rows(HALO - 2, 2 * piece), part, preferred_element_type=F32)
    pack_ref[...] = total.astype(BF16)


def unpack_halo(pieces, count):
    parts = [
        jnp.dot(pick_rows(2 * piece, HALO - 2), pieces, preferred_element_type=F32).astype(BF16)
        for piece in range(count)
    ]
    return jnp.concatenate(parts, axis=1)


def project(rows, weight_ref, branches, keep_ref, send_ref):
    own_half = lax.axis_index("fsdp")
    half = weight_ref.shape[2] // 2
    for place, branch in enumerate(branches):
        summed = jnp.dot(rows, weight_ref[branch], preferred_element_type=F32)
        keep, send = split_channels(summed, own_half)
        lanes = slice(place * half, (place + 1) * half)
        keep_ref[:, lanes] = keep
        send_ref[:, lanes] = send.astype(BF16)


def project_first_body(rows_ref, cycled_ref, weight_ref, keep_ref, send_ref):
    here = lax.axis_index("chan") == lax.axis_index("fsdp")
    rows = jnp.where(here, rows_ref[...], cycled_ref[...])
    project(rows, weight_ref, (0, 1, 2), keep_ref, send_ref)


def project_second_body(
    branches, cycled_ref, hop_ref, pack_ref, pack_hop_ref, weight_ref, keep_ref, send_ref, *done_refs
):
    here = lax.axis_index("chan") == lax.axis_index("fsdp")
    pieces = cycled_ref.shape[1] // pack_ref.shape[1]
    rows = jnp.where(here, cycled_ref[...], hop_ref[...])
    halo = unpack_halo(jnp.where(here, pack_ref[...], pack_hop_ref[...]), pieces)
    halo = jnp.where(lax.axis_index("seq") > 0, halo, jnp.zeros_like(halo))
    rows = jnp.concatenate([halo, rows], axis=0)
    project(rows, weight_ref, branches, keep_ref, send_ref)
    for done_ref in done_refs:
        done_ref[...] = jnp.zeros_like(done_ref)


def sort_taps_body(*refs):
    keep_ref, send_ref, done_ref = refs[-3:]
    position = lax.axis_index("seq")
    first = lax.axis_index("fsdp") == 0
    blocks, _, half = keep_ref.shape
    for step in range(blocks):
        block = lax.rem(position - step + blocks, blocks)
        taps = refs[step][...]
        low, high = (taps[:, :half], taps[:, half:])
        keep_ref[block] = jnp.where(first, low, high)
        send_ref[block] = jnp.where(first, high, low)
    done_ref[...] = jnp.zeros_like(done_ref)


def after_body(*refs):
    pass


def after(value, *orders):
    return pl.pallas_call(
        after_body,
        in_specs=whole_specs(1 + len(orders)),
        out_specs=whole_specs(1)[0],
        out_shape=shape(value.shape, value.dtype),
        input_output_aliases={0: 0},
        compiler_params=pltpu.CompilerParams(vmem_limit_bytes=32 * 1024 * 1024),
    )(value, *orders)


def taps_body(table_ref, keep_ref, got_ref, real_ref, imag_ref):
    first = lax.axis_index("fsdp") == 0
    blocks = keep_ref.shape[0]
    size = table_ref.shape[1]
    sign = 1.0 - 2.0 * (lax.broadcasted_iota(jnp.int32, (size, 1), 0) % 2).astype(F32)
    sign = sign * (1.0 / size)
    before_real = before_imag = None
    for block in range(blocks):
        keep, got = (keep_ref[block], got_ref[block])
        taps = jnp.concatenate(
            [jnp.where(first, keep, got), jnp.where(first, got, keep)], axis=0
        )
        waves = jnp.dot(table_ref[...], taps, preferred_element_type=F32)
        real, imag = (waves[:size], -waves[size:])
        if block == 0:
            real_ref[block] = real * (1.0 / size)
            imag_ref[block] = imag * (1.0 / size)
        else:
            real_ref[block] = real * (1.0 / size) - sign * before_imag
            imag_ref[block] = imag * (1.0 / size) + sign * before_real
        before_real, before_imag = (real, imag)


def mixed_branches(branches, keep_first, keep_second, got_first, got_second, short_ref, joined):
    own = lax.axis_index("fsdp")
    rows = keep_first.shape[0]
    half = keep_second.shape[1] // len(branches)
    first_lanes = slice(branches[0] * half, (branches[-1] + 1) * half)
    joined[:HALO, :] = keep_second[:HALO, :] + got_second[:HALO, :].astype(F32)
    own_start = pl.multiple_of(HALO + own * rows, HALO)
    other_start = pl.multiple_of(HALO + (1 - own) * rows, HALO)
    joined[pl.ds(own_start, rows), :] = (
        keep_first[:, first_lanes] + got_second[HALO:, :].astype(F32)
    )
    joined[pl.ds(other_start, rows), :] = (
        keep_second[HALO:, :] + got_first[:, first_lanes].astype(F32)
    )
    mixed = []
    for place, branch in enumerate(branches):
        lanes = slice(place * half, (place + 1) * half)
        total = None
        for tap in range(3):
            taps = short_ref[tap, branch : branch + 1, :]
            taps = jnp.where(own == 0, taps[:, :half], taps[:, half:])
            term = taps * joined[pl.ds(HALO - tap, 2 * rows), lanes]
            total = term if total is None else total + term
        mixed.append(total)
    return mixed


def product_body(
    keep_first, keep_second, got_first, got_second, short_ref, order_ref, product_ref, joined
):
    key, value = mixed_branches(
        (1, 2), keep_first, keep_second, got_first, got_second, short_ref, joined
    )
    product_ref[...] = (key * value).astype(BF16)


def query_body(keep_first, keep_second, got_first, got_second, short_ref, query_ref, joined):
    (query,) = mixed_branches(
        (0,), keep_first, keep_second, got_first, got_second, short_ref, joined
    )
    query_ref[...] = query


def conv_body(own_ref, one_ref, two_ref, three_ref, real_ref, imag_ref, table_ref, turned_ref,
              query_ref, gain_ref, stay_ref, go_ref, result):
    position = lax.axis_index("seq")
    own = lax.axis_index("fsdp")
    size = table_ref.shape[1]
    total_real = total_imag = None
    for step, block_ref in enumerate((own_ref, one_ref, two_ref, three_ref)):
        block = block_ref[...]
        if step:
            block = jnp.where(position >= step, block, jnp.zeros_like(block))
        waves = jnp.dot(table_ref[...], block, preferred_element_type=F32)
        real, imag = (waves[:size], -waves[size:])
        term_real = real * real_ref[step] - imag * imag_ref[step]
        term_imag = real * imag_ref[step] + imag * real_ref[step]
        total_real = term_real if total_real is None else total_real + term_real
        total_imag = term_imag if total_imag is None else total_imag + term_imag
    stacked = jnp.concatenate([total_real, -total_imag], axis=0).astype(BF16)
    conv = jnp.dot(turned_ref[...], stacked, preferred_element_type=F32)
    half = own_ref.shape[1]
    gain = jnp.where(own == 0, gain_ref[:, :half], gain_ref[:, half:])
    gated = query_ref[...] * (conv + gain * own_ref[...].astype(F32))
    result[...] = gated.astype(BF16)
    rows = stay_ref.shape[0]
    stay_ref[...] = result[pl.ds(pl.multiple_of(own * rows, rows), rows), :]
    go_ref[...] = result[pl.ds(pl.multiple_of((1 - own) * rows, rows), rows), :]


def join_body(stay_ref, got_ref, out_ref):
    first = lax.axis_index("fsdp") == 0
    half = stay_ref.shape[1]
    out_ref[:, :half] = jnp.where(first, stay_ref[...], got_ref[...])
    out_ref[:, half:] = jnp.where(first, got_ref[...], stay_ref[...])


def shape(dims, kind):
    return jax.ShapeDtypeStruct(dims, kind)


def pair_mesh(tokens, proj_weight, short_weight, skip_gain, filter_taps):
    rows = tokens.shape[0]
    width = proj_weight.shape[2]
    half = width // 2
    size = 2 * rows
    blocks = lax.axis_size("seq")
    weight = jnp.transpose(proj_weight, (1, 0, 2))
    ring = [[(s, (s + step) % blocks) for s in range(blocks)] for step in range(blocks)]
    call = functools.partial(
        pl.pallas_call, compiler_params=pltpu.CompilerParams(vmem_limit_bytes=32 * 1024 * 1024)
    )

    cycled = lax.ppermute(tokens, ("fsdp", "chan"), [(1, 3), (3, 2), (2, 0), (0, 1)])
    token = shape((8, 128), F32)
    pack = call(
        pack_body,
        cost_estimate=LONG,
        in_specs=whole_specs(1),
        out_specs=whole_specs(1)[0],
        out_shape=shape((HALO, width), BF16),
    )(tokens)
    pack_got = lax.ppermute(
        pack,
        ("seq", "fsdp", "chan"),
        [
            (4 * s + 2 * f + c, 4 * ((s + 1) % blocks) + 2 * (f ^ (1 - c)) + c)
            for s in range(blocks)
            for f in range(2)
            for c in range(2)
        ],
    )
    tap_blocks = [filter_taps] + [
        lax.ppermute(filter_taps, "seq", ring[step]) for step in range(1, blocks)
    ]
    cycled = after(cycled, pack_got)
    hop = exchange(cycled, "chan")
    pack_hop = exchange(pack_got, "chan")
    keep_first, send_first = call(
        project_first_body,
        cost_estimate=LONG,
        in_specs=whole_specs(3),
        out_specs=whole_specs(2),
        out_shape=(shape((rows, 3 * half), F32), shape((rows, 3 * half), BF16)),
    )(tokens, cycled, weight)
    got_first = exchange(send_first, "fsdp")
    keep_product, send_product, second_done = call(
        functools.partial(project_second_body, (1, 2)),
        in_specs=whole_specs(5),
        out_specs=whole_specs(3),
        out_shape=(
            shape((HALO + rows, 2 * half), F32),
            shape((HALO + rows, 2 * half), BF16),
            token,
        ),
    )(cycled, hop, pack_got, pack_hop, weight)
    keep_query, send_query = call(
        functools.partial(project_second_body, (0,)),
        in_specs=whole_specs(5),
        out_specs=whole_specs(2),
        out_shape=(shape((HALO + rows, half), F32), shape((HALO + rows, half), BF16)),
    )(cycled, hop, pack_got, pack_hop, weight)
    tap_keep, tap_send, tap_done = call(
        sort_taps_body,
        in_specs=whole_specs(1 + blocks),
        out_specs=whole_specs(3),
        out_shape=(
            shape((blocks, rows, half), BF16),
            shape((blocks, rows, half), BF16),
            token,
        ),
    )(*tap_blocks, second_done)
    got_product = exchange(send_product, "fsdp")
    got_query = exchange(send_query, "fsdp")

    product = call(
        product_body,
        in_specs=whole_specs(6),
        out_specs=whole_specs(1)[0],
        out_shape=shape((size, half), BF16),
        scratch_shapes=[pltpu.VMEM((HALO + size, 2 * half), F32)],
    )(keep_first, keep_product, got_first, got_product, short_weight, tap_done)
    query = call(
        query_body,
        in_specs=whole_specs(5),
        out_specs=whole_specs(1)[0],
        out_shape=shape((size, half), F32),
        scratch_shapes=[pltpu.VMEM((HALO + size, half), F32)],
    )(keep_first, keep_query, got_first, got_query, short_weight)
    tap_got = exchange(tap_send, "fsdp")
    products = [product] + [lax.ppermute(product, "seq", ring[step]) for step in range(1, blocks)]
    table = wave_table(size)
    forward = jnp.asarray(table, dtype=BF16)
    inverse = jnp.asarray(table.T, dtype=BF16)
    tap_real, tap_imag = call(
        taps_body,
        in_specs=whole_specs(3),
        out_specs=whole_specs(2),
        out_shape=(shape((blocks, size, half), F32), shape((blocks, size, half), F32)),
    )(forward, tap_keep, tap_got)
    stay, go = call(
        conv_body,
        in_specs=whole_specs(10),
        out_specs=whole_specs(2),
        out_shape=(shape((rows, half), BF16), shape((rows, half), BF16)),
        scratch_shapes=[pltpu.VMEM((size, half), BF16)],
    )(*products, tap_real, tap_imag, forward, inverse, query, skip_gain.reshape(1, width))
    back = exchange(go, "fsdp")
    return call(
        join_body,
        in_specs=whole_specs(2),
        out_specs=whole_specs(1)[0],
        out_shape=shape((rows, width), BF16),
    )(stay, back)


def solution(mesh):
    in_specs = (
        P(("grp", "seq", "fsdp"), "chan"),
        P("fsdp", None, "chan"),
        P(None, None, "chan"),
        P("chan"),
        P(("seq", "fsdp"), "chan"),
    )
    out_specs = P(("grp", "seq", "fsdp"), "chan")
    sizes = mesh.shape
    paired = sizes["fsdp"] == 2 and sizes["chan"] == 2 and sizes["seq"] == 4
    per_device = pair_mesh if paired else any_mesh
    return jax.shard_map(
        per_device, mesh=mesh, in_specs=in_specs, out_specs=out_specs, check_vma=False
    )
```

```python
import functools
import math

import jax
import jax.numpy as jnp
import numpy as np
from jax import lax
from jax.experimental import pallas as pl
from jax.experimental.pallas import tpu as pltpu
from jax.sharding import PartitionSpec as P

HALO = 16
LONG = pl.CostEstimate(flops=10_000_000_000, bytes_accessed=40_000_000, transcendentals=0)
F32 = jnp.float32
BF16 = jnp.bfloat16


def shifted(value, axis, steps):
    count = lax.axis_size(axis)
    initial, last = (max(0, -steps), min(count, count - steps))
    return lax.ppermute(value, axis, [(source, source + steps) for source in range(initial, last)])


def index_grid(row_count, col_count):
    return (
        lax.broadcasted_iota(jnp.int32, (row_count, col_count), 0),
        lax.broadcasted_iota(jnp.int32, (row_count, col_count), 1),
    )


def phase_pair(row_ids, col_ids, period):
    wrapped = row_ids * col_ids % period
    phase = wrapped.astype(jnp.float32) * (2.0 * math.pi / period)
    return (jnp.cos(phase), jnp.sin(phase))


def multiply(real_x, imag_x):
    sig_real = real_x[0].astype(jnp.float32)
    sig_imag = imag_x[0].astype(jnp.float32)
    tap_real = real_x[1].astype(jnp.float32)
    tap_imag = imag_x[1].astype(jnp.float32)
    real_z = (sig_real * tap_real - sig_imag * tap_imag).astype(jnp.bfloat16)
    imag_z = (sig_real * tap_imag + sig_imag * tap_real).astype(jnp.bfloat16)
    return (real_z, imag_z)


def spread(stacked, groups, inner_shape):
    shaped = stacked.reshape((2, groups, 1) + inner_shape)
    moved = lax.all_to_all(shaped, ("seq", "fsdp"), split_axis=1, concat_axis=2, tiled=True)
    return moved.reshape((2, groups) + inner_shape)


def any_mesh(tokens, proj_weight, short_weight, skip_gain, filter_taps):
    whole = lax.all_gather(tokens, "chan", axis=1, tiled=True)
    row_count = whole.shape[0]
    width = proj_weight.shape[2]
    flat_width = 3 * width
    piece = lax.all_gather(proj_weight, "fsdp", axis=0, tiled=True)
    summed = jnp.dot(
        whole, piece.reshape(piece.shape[0], flat_width), preferred_element_type=jnp.float32
    )
    projected = summed.astype(jnp.bfloat16).reshape(row_count, 3, width)
    earlier = shifted(projected[row_count - 2 :], ("seq", "fsdp"), 1)
    extended = jnp.concatenate([earlier, projected], axis=0).astype(jnp.float32)
    mixed = (
        short_weight[0] * extended[2:]
        + short_weight[1] * extended[1:-1]
        + short_weight[2] * extended[:-2]
    )
    query = mixed[:, 0]
    product = (mixed[:, 1] * mixed[:, 2]).astype(jnp.bfloat16)
    groups = lax.axis_size(("seq", "fsdp"))
    position = lax.axis_index(("seq", "fsdp"))
    period_rows = 2 * groups
    length = period_rows * row_count
    scale = 1.0 / length
    bin_ids, tap_ids = index_grid(period_rows, groups)
    first_cos, first_sin = phase_pair(bin_ids, tap_ids, period_rows)
    first_cos = first_cos.astype(jnp.bfloat16)
    first_sin = first_sin.astype(jnp.bfloat16)
    col_ids, freq_ids = index_grid(row_count, row_count)
    last_cos, last_sin = phase_pair(col_ids, freq_ids, row_count)
    last_cos = last_cos.astype(jnp.bfloat16)
    last_sin = last_sin.astype(jnp.bfloat16)
    stacked = jnp.stack([product, filter_taps])
    f32 = jnp.float32
    per_dev = row_count // groups
    per_bins = period_rows // groups
    arrived = spread(stacked.reshape(2, groups, per_dev, width), groups, (per_dev, width))
    real_a = jnp.einsum("qp,kpmc->kqmc", first_cos, arrived, preferred_element_type=f32)
    imag_a = -jnp.einsum("qp,kpmc->kqmc", first_sin, arrived, preferred_element_type=f32)
    row_ids, mid_ids = index_grid(period_rows, per_dev)
    twist_cos, twist_sin = phase_pair(row_ids, mid_ids + position * per_dev, length)
    twist_cos = twist_cos[:, :, None]
    twist_sin = twist_sin[:, :, None]
    real_b = (real_a * twist_cos + imag_a * twist_sin).astype(jnp.bfloat16)
    imag_b = (imag_a * twist_cos - real_a * twist_sin).astype(jnp.bfloat16)
    outgoing = jnp.stack([real_b, imag_b]).reshape(2, 2, groups, per_bins, 1, per_dev, width)
    turned = lax.all_to_all(outgoing, ("seq", "fsdp"), split_axis=2, concat_axis=4, tiled=True)
    turned = turned.reshape(2, 2, per_bins, row_count, width)
    real_b = turned[0]
    imag_b = turned[1]
    real_x = (
        jnp.einsum("kqmc,mr->kqrc", real_b, last_cos, preferred_element_type=f32)
        + jnp.einsum("kqmc,mr->kqrc", imag_b, last_sin, preferred_element_type=f32)
    ).astype(jnp.bfloat16)
    imag_x = (
        jnp.einsum("kqmc,mr->kqrc", imag_b, last_cos, preferred_element_type=f32)
        - jnp.einsum("kqmc,mr->kqrc", real_b, last_sin, preferred_element_type=f32)
    ).astype(jnp.bfloat16)
    real_z, imag_z = multiply(real_x, imag_x)
    real_v = jnp.einsum("qrc,mr->qmc", real_z, last_cos, preferred_element_type=f32) - jnp.einsum(
        "qrc,mr->qmc", imag_z, last_sin, preferred_element_type=f32
    )
    imag_v = jnp.einsum("qrc,mr->qmc", imag_z, last_cos, preferred_element_type=f32) + jnp.einsum(
        "qrc,mr->qmc", real_z, last_sin, preferred_element_type=f32
    )
    row_ids, mid_ids = index_grid(per_bins, row_count)
    twist_cos, twist_sin = phase_pair(row_ids + position * per_bins, mid_ids, length)
    twist_cos = twist_cos[:, :, None]
    twist_sin = twist_sin[:, :, None]
    real_w = (real_v * twist_cos - imag_v * twist_sin).astype(jnp.bfloat16)
    imag_w = (imag_v * twist_cos + real_v * twist_sin).astype(jnp.bfloat16)
    backward = jnp.stack([real_w, imag_w]).reshape(2, 1, per_bins, groups, per_dev, width)
    returned = lax.all_to_all(backward, ("seq", "fsdp"), split_axis=3, concat_axis=1, tiled=True)
    returned = returned.reshape(2, period_rows, per_dev, width)
    conv_rows = jnp.einsum(
        "qp,qmc->pmc", first_cos, returned[0], preferred_element_type=f32
    ) - jnp.einsum("qp,qmc->pmc", first_sin, returned[1], preferred_element_type=f32)
    conv_rows = (conv_rows * scale).astype(jnp.bfloat16)
    homed = lax.all_to_all(
        conv_rows.reshape(groups, 1, per_dev, width),
        ("seq", "fsdp"),
        split_axis=0,
        concat_axis=1,
        tiled=True,
    )
    conv = homed.reshape(row_count, width)
    result = query * (conv.astype(jnp.float32) + skip_gain * product.astype(jnp.float32))
    return result.astype(jnp.bfloat16)


def wave_table(size):
    freq, time = np.meshgrid(np.arange(size), np.arange(size), indexing="ij")
    angle = ((2 * freq + 1) * time % (4 * size)) * (math.pi / (2 * size))
    return np.concatenate([np.cos(angle), np.sin(angle)], axis=0)


def exchange(value, axis):
    return lax.ppermute(value, axis, [(0, 1), (1, 0)])


def whole_specs(count):
    return [pl.BlockSpec(memory_space=pltpu.VMEM)] * count


def split_channels(summed, own_half):
    half = summed.shape[1] // 2
    low, high = (summed[:, :half], summed[:, half:])
    first = own_half == 0
    return (jnp.where(first, low, high), jnp.where(first, high, low))


def pick_rows(source, target):
    lines = lax.broadcasted_iota(jnp.int32, (HALO, HALO), 0)
    places = lax.broadcasted_iota(jnp.int32, (HALO, HALO), 1)
    wanted = (lines - target == places - source) & (places >= source) & (places < source + 2)
    return wanted.astype(F32).astype(BF16)


def pack_body(rows_ref, pack_ref):
    width = pack_ref.shape[1]
    last = rows_ref[rows_ref.shape[0] - HALO :, :]
    total = jnp.zeros((HALO, width), F32)
    for piece in range(last.shape[1] // width):
        part = last[:, piece * width : (piece + 1) * width]
        total += jnp.dot(pick_rows(HALO - 2, 2 * piece), part, preferred_element_type=F32)
    pack_ref[...] = total.astype(BF16)


def unpack_halo(pieces, count):
    parts = [
        jnp.dot(pick_rows(2 * piece, HALO - 2), pieces, preferred_element_type=F32).astype(BF16)
        for piece in range(count)
    ]
    return jnp.concatenate(parts, axis=1)


def project(rows, weight_ref, branches, keep_ref, send_ref):
    own_half = lax.axis_index("fsdp")
    half = weight_ref.shape[2] // 2
    for place, branch in enumerate(branches):
        summed = jnp.dot(rows, weight_ref[branch], preferred_element_type=F32)
        keep, send = split_channels(summed, own_half)
        lanes = slice(place * half, (place + 1) * half)
        keep_ref[:, lanes] = keep
        send_ref[:, lanes] = send.astype(send_ref.dtype)


def project_first_body(rows_ref, cycled_ref, weight_ref, keep_ref, send_ref):
    here = lax.axis_index("chan") == lax.axis_index("fsdp")
    rows = jnp.where(here, rows_ref[...], cycled_ref[...])
    project(rows, weight_ref, (0, 1, 2), keep_ref, send_ref)


def project_second_body(
    branches, cycled_ref, hop_ref, pack_ref, pack_hop_ref, weight_ref, keep_ref, send_ref, *done_refs
):
    here = lax.axis_index("chan") == lax.axis_index("fsdp")
    pieces = cycled_ref.shape[1] // pack_ref.shape[1]
    rows = jnp.where(here, cycled_ref[...], hop_ref[...])
    halo = unpack_halo(jnp.where(here, pack_ref[...], pack_hop_ref[...]), pieces)
    halo = jnp.where(lax.axis_index("seq") > 0, halo, jnp.zeros_like(halo))
    rows = jnp.concatenate([halo, rows], axis=0)
    project(rows, weight_ref, branches, keep_ref, send_ref)
    for done_ref in done_refs:
        done_ref[...] = jnp.zeros_like(done_ref)


def sort_taps_body(*refs):
    keep_ref, send_ref, done_ref = refs[-3:]
    position = lax.axis_index("seq")
    first = lax.axis_index("fsdp") == 0
    blocks, _, half = keep_ref.shape
    for step in range(blocks):
        block = lax.rem(position - step + blocks, blocks)
        taps = refs[step][...]
        low, high = (taps[:, :half], taps[:, half:])
        keep_ref[block] = jnp.where(first, low, high)
        send_ref[block] = jnp.where(first, high, low)
    done_ref[...] = jnp.zeros_like(done_ref)


def after_body(*refs):
    pass


def after(value, *orders):
    return pl.pallas_call(
        after_body,
        in_specs=whole_specs(1 + len(orders)),
        out_specs=whole_specs(1)[0],
        out_shape=shape(value.shape, value.dtype),
        input_output_aliases={0: 0},
        compiler_params=pltpu.CompilerParams(vmem_limit_bytes=32 * 1024 * 1024),
    )(value, *orders)


def taps_body(table_ref, keep_ref, got_ref, real_ref, imag_ref):
    first = lax.axis_index("fsdp") == 0
    blocks = keep_ref.shape[0]
    size = table_ref.shape[1]
    sign = 1.0 - 2.0 * (lax.broadcasted_iota(jnp.int32, (size, 1), 0) % 2).astype(F32)
    sign = sign * (1.0 / size)
    before_real = before_imag = None
    for block in range(blocks):
        keep, got = (keep_ref[block], got_ref[block])
        taps = jnp.concatenate(
            [jnp.where(first, keep, got), jnp.where(first, got, keep)], axis=0
        )
        waves = jnp.dot(table_ref[...], taps, preferred_element_type=F32)
        real, imag = (waves[:size], -waves[size:])
        if block == 0:
            real_ref[block] = real * (1.0 / size)
            imag_ref[block] = imag * (1.0 / size)
        else:
            real_ref[block] = real * (1.0 / size) - sign * before_imag
            imag_ref[block] = imag * (1.0 / size) + sign * before_real
        before_real, before_imag = (real, imag)


def mixed_branches(branches, keep_first, keep_second, got_first, got_second, short_ref, joined):
    own = lax.axis_index("fsdp")
    rows = keep_first.shape[0]
    half = keep_second.shape[1] // len(branches)
    first_lanes = slice(branches[0] * half, (branches[-1] + 1) * half)
    joined[:HALO, :] = keep_second[:HALO, :] + got_second[:HALO, :].astype(F32)
    own_start = pl.multiple_of(HALO + own * rows, HALO)
    other_start = pl.multiple_of(HALO + (1 - own) * rows, HALO)
    joined[pl.ds(own_start, rows), :] = (
        keep_first[:, first_lanes] + got_second[HALO:, :].astype(F32)
    )
    joined[pl.ds(other_start, rows), :] = (
        keep_second[HALO:, :] + got_first[:, first_lanes].astype(F32)
    )
    mixed = []
    for place, branch in enumerate(branches):
        lanes = slice(place * half, (place + 1) * half)
        total = None
        for tap in range(3):
            taps = short_ref[tap, branch : branch + 1, :]
            taps = jnp.where(own == 0, taps[:, :half], taps[:, half:])
            term = taps * joined[pl.ds(HALO - tap, 2 * rows), lanes]
            total = term if total is None else total + term
        mixed.append(total)
    return mixed


def product_body(
    keep_first, keep_second, got_first, got_second, short_ref, order_ref, product_ref, joined
):
    key, value = mixed_branches(
        (1, 2), keep_first, keep_second, got_first, got_second, short_ref, joined
    )
    product_ref[...] = (key * value).astype(BF16)


def query_body(keep_first, keep_second, got_first, got_second, short_ref, query_ref, joined):
    (query,) = mixed_branches(
        (0,), keep_first, keep_second, got_first, got_second, short_ref, joined
    )
    query_ref[...] = query


def conv_body(own_ref, one_ref, two_ref, three_ref, real_ref, imag_ref, table_ref, turned_ref,
              query_ref, gain_ref, stay_ref, go_ref, result):
    position = lax.axis_index("seq")
    own = lax.axis_index("fsdp")
    size = table_ref.shape[1]
    total_real = total_imag = None
    for step, block_ref in enumerate((own_ref, one_ref, two_ref, three_ref)):
        block = block_ref[...]
        source = position ^ step
        back = jnp.maximum(position - source, 0)
        if step:
            block = jnp.where(source < position, block, jnp.zeros_like(block))
        waves = jnp.dot(table_ref[...], block, preferred_element_type=F32)
        real, imag = (waves[:size], -waves[size:])
        term_real = real * real_ref[back] - imag * imag_ref[back]
        term_imag = real * imag_ref[back] + imag * real_ref[back]
        total_real = term_real if total_real is None else total_real + term_real
        total_imag = term_imag if total_imag is None else total_imag + term_imag
    stacked = jnp.concatenate([total_real, -total_imag], axis=0).astype(BF16)
    conv = jnp.dot(turned_ref[...], stacked, preferred_element_type=F32)
    half = own_ref.shape[1]
    gain = jnp.where(own == 0, gain_ref[:, :half], gain_ref[:, half:])
    gated = query_ref[...] * (conv + gain * own_ref[...].astype(F32))
    result[...] = gated.astype(BF16)
    rows = stay_ref.shape[0]
    stay_ref[...] = result[pl.ds(pl.multiple_of(own * rows, rows), rows), :]
    go_ref[...] = result[pl.ds(pl.multiple_of((1 - own) * rows, rows), rows), :]


def join_body(stay_ref, got_ref, out_ref):
    first = lax.axis_index("fsdp") == 0
    half = stay_ref.shape[1]
    out_ref[:, :half] = jnp.where(first, stay_ref[...], got_ref[...])
    out_ref[:, half:] = jnp.where(first, got_ref[...], stay_ref[...])


def shape(dims, kind):
    return jax.ShapeDtypeStruct(dims, kind)


def pair_mesh(tokens, proj_weight, short_weight, skip_gain, filter_taps):
    rows = tokens.shape[0]
    width = proj_weight.shape[2]
    half = width // 2
    size = 2 * rows
    blocks = lax.axis_size("seq")
    weight = jnp.transpose(proj_weight, (1, 0, 2))
    ring = [[(s, (s + step) % blocks) for s in range(blocks)] for step in range(blocks)]
    call = functools.partial(
        pl.pallas_call, compiler_params=pltpu.CompilerParams(vmem_limit_bytes=32 * 1024 * 1024)
    )

    cycled = lax.ppermute(tokens, ("fsdp", "chan"), [(1, 3), (3, 2), (2, 0), (0, 1)])
    token = shape((8, 128), F32)
    pack = call(
        pack_body,
        cost_estimate=LONG,
        in_specs=whole_specs(1),
        out_specs=whole_specs(1)[0],
        out_shape=shape((HALO, width), BF16),
    )(tokens)
    pack_got = lax.ppermute(
        pack,
        ("seq", "fsdp", "chan"),
        [
            (4 * s + 2 * f + c, 4 * ((s + 1) % blocks) + 2 * (f ^ (1 - c)) + c)
            for s in range(blocks)
            for f in range(2)
            for c in range(2)
        ],
    )
    tap_blocks = [filter_taps] + [
        lax.ppermute(filter_taps, "seq", ring[step]) for step in range(1, blocks)
    ]
    cycled = after(cycled, pack_got)
    hop = exchange(cycled, "chan")
    pack_hop = exchange(pack_got, "chan")
    keep_first, send_first = call(
        project_first_body,
        cost_estimate=LONG,
        in_specs=whole_specs(3),
        out_specs=whole_specs(2),
        out_shape=(shape((rows, 3 * half), F32), shape((rows, 3 * half), BF16)),
    )(tokens, cycled, weight)
    got_first = exchange(send_first, "fsdp")
    keep_product, send_product, second_done = call(
        functools.partial(project_second_body, (1, 2)),
        in_specs=whole_specs(5),
        out_specs=whole_specs(3),
        out_shape=(
            shape((HALO + rows, 2 * half), F32),
            shape((HALO + rows, 2 * half), BF16),
            token,
        ),
    )(cycled, hop, pack_got, pack_hop, weight)
    keep_query, send_query = call(
        functools.partial(project_second_body, (0,)),
        in_specs=whole_specs(5),
        out_specs=whole_specs(2),
        out_shape=(shape((HALO + rows, half), F32), shape((HALO + rows, half), F32)),
    )(cycled, hop, pack_got, pack_hop, weight)
    tap_keep, tap_send, tap_done = call(
        sort_taps_body,
        in_specs=whole_specs(1 + blocks),
        out_specs=whole_specs(3),
        out_shape=(
            shape((blocks, rows, half), BF16),
            shape((blocks, rows, half), BF16),
            token,
        ),
    )(*tap_blocks, second_done)
    got_product = exchange(send_product, "fsdp")
    got_query = exchange(send_query, "fsdp")

    product = call(
        product_body,
        in_specs=whole_specs(6),
        out_specs=whole_specs(1)[0],
        out_shape=shape((size, half), BF16),
        scratch_shapes=[pltpu.VMEM((HALO + size, 2 * half), F32)],
    )(keep_first, keep_product, got_first, got_product, short_weight, tap_done)
    query = call(
        query_body,
        in_specs=whole_specs(5),
        out_specs=whole_specs(1)[0],
        out_shape=shape((size, half), F32),
        scratch_shapes=[pltpu.VMEM((HALO + size, half), F32)],
    )(keep_first, keep_query, got_first, got_query, short_weight)
    tap_got = exchange(tap_send, "fsdp")
    products = [product] + [lax.ppermute(product, "seq", [(s, s ^ step) for s in range(blocks)]) for step in range(1, blocks)]
    table = wave_table(size)
    forward = jnp.asarray(table, dtype=BF16)
    inverse = jnp.asarray(table.T, dtype=BF16)
    tap_real, tap_imag = call(
        taps_body,
        in_specs=whole_specs(3),
        out_specs=whole_specs(2),
        out_shape=(shape((blocks, size, half), F32), shape((blocks, size, half), F32)),
    )(forward, tap_keep, tap_got)
    stay, go = call(
        conv_body,
        in_specs=whole_specs(10),
        out_specs=whole_specs(2),
        out_shape=(shape((rows, half), BF16), shape((rows, half), BF16)),
        scratch_shapes=[pltpu.VMEM((size, half), BF16)],
    )(*products, tap_real, tap_imag, forward, inverse, query, skip_gain.reshape(1, width))
    back = exchange(go, "fsdp")
    return call(
        join_body,
        in_specs=whole_specs(2),
        out_specs=whole_specs(1)[0],
        out_shape=shape((rows, width), BF16),
    )(stay, back)


def solution(mesh):
    in_specs = (
        P(("grp", "seq", "fsdp"), "chan"),
        P("fsdp", None, "chan"),
        P(None, None, "chan"),
        P("chan"),
        P(("seq", "fsdp"), "chan"),
    )
    out_specs = P(("grp", "seq", "fsdp"), "chan")
    sizes = mesh.shape
    paired = sizes["fsdp"] == 2 and sizes["chan"] == 2 and sizes["seq"] == 4
    per_device = pair_mesh if paired else any_mesh
    return jax.shard_map(
        per_device, mesh=mesh, in_specs=in_specs, out_specs=out_specs, check_vma=False
    )
```

```python
import functools
import math

import jax
import jax.numpy as jnp
import numpy as np
from jax import lax
from jax.experimental import pallas as pl
from jax.experimental.pallas import tpu as pltpu
from jax.sharding import PartitionSpec as P

HALO = 16
LONG = pl.CostEstimate(flops=10_000_000_000, bytes_accessed=40_000_000, transcendentals=0)
F32 = jnp.float32
BF16 = jnp.bfloat16


def shifted(value, axis, steps):
    count = lax.axis_size(axis)
    initial, last = (max(0, -steps), min(count, count - steps))
    return lax.ppermute(value, axis, [(source, source + steps) for source in range(initial, last)])


def index_grid(row_count, col_count):
    return (
        lax.broadcasted_iota(jnp.int32, (row_count, col_count), 0),
        lax.broadcasted_iota(jnp.int32, (row_count, col_count), 1),
    )


def phase_pair(row_ids, col_ids, period):
    wrapped = row_ids * col_ids % period
    phase = wrapped.astype(jnp.float32) * (2.0 * math.pi / period)
    return (jnp.cos(phase), jnp.sin(phase))


def multiply(real_x, imag_x):
    sig_real = real_x[0].astype(jnp.float32)
    sig_imag = imag_x[0].astype(jnp.float32)
    tap_real = real_x[1].astype(jnp.float32)
    tap_imag = imag_x[1].astype(jnp.float32)
    real_z = (sig_real * tap_real - sig_imag * tap_imag).astype(jnp.bfloat16)
    imag_z = (sig_real * tap_imag + sig_imag * tap_real).astype(jnp.bfloat16)
    return (real_z, imag_z)


def spread(stacked, groups, inner_shape):
    shaped = stacked.reshape((2, groups, 1) + inner_shape)
    moved = lax.all_to_all(shaped, ("seq", "fsdp"), split_axis=1, concat_axis=2, tiled=True)
    return moved.reshape((2, groups) + inner_shape)


def any_mesh(tokens, proj_weight, short_weight, skip_gain, filter_taps):
    whole = lax.all_gather(tokens, "chan", axis=1, tiled=True)
    row_count = whole.shape[0]
    width = proj_weight.shape[2]
    flat_width = 3 * width
    piece = lax.all_gather(proj_weight, "fsdp", axis=0, tiled=True)
    summed = jnp.dot(
        whole, piece.reshape(piece.shape[0], flat_width), preferred_element_type=jnp.float32
    )
    projected = summed.astype(jnp.bfloat16).reshape(row_count, 3, width)
    earlier = shifted(projected[row_count - 2 :], ("seq", "fsdp"), 1)
    extended = jnp.concatenate([earlier, projected], axis=0).astype(jnp.float32)
    mixed = (
        short_weight[0] * extended[2:]
        + short_weight[1] * extended[1:-1]
        + short_weight[2] * extended[:-2]
    )
    query = mixed[:, 0]
    product = (mixed[:, 1] * mixed[:, 2]).astype(jnp.bfloat16)
    groups = lax.axis_size(("seq", "fsdp"))
    position = lax.axis_index(("seq", "fsdp"))
    period_rows = 2 * groups
    length = period_rows * row_count
    scale = 1.0 / length
    bin_ids, tap_ids = index_grid(period_rows, groups)
    first_cos, first_sin = phase_pair(bin_ids, tap_ids, period_rows)
    first_cos = first_cos.astype(jnp.bfloat16)
    first_sin = first_sin.astype(jnp.bfloat16)
    col_ids, freq_ids = index_grid(row_count, row_count)
    last_cos, last_sin = phase_pair(col_ids, freq_ids, row_count)
    last_cos = last_cos.astype(jnp.bfloat16)
    last_sin = last_sin.astype(jnp.bfloat16)
    stacked = jnp.stack([product, filter_taps])
    f32 = jnp.float32
    per_dev = row_count // groups
    per_bins = period_rows // groups
    arrived = spread(stacked.reshape(2, groups, per_dev, width), groups, (per_dev, width))
    real_a = jnp.einsum("qp,kpmc->kqmc", first_cos, arrived, preferred_element_type=f32)
    imag_a = -jnp.einsum("qp,kpmc->kqmc", first_sin, arrived, preferred_element_type=f32)
    row_ids, mid_ids = index_grid(period_rows, per_dev)
    twist_cos, twist_sin = phase_pair(row_ids, mid_ids + position * per_dev, length)
    twist_cos = twist_cos[:, :, None]
    twist_sin = twist_sin[:, :, None]
    real_b = (real_a * twist_cos + imag_a * twist_sin).astype(jnp.bfloat16)
    imag_b = (imag_a * twist_cos - real_a * twist_sin).astype(jnp.bfloat16)
    outgoing = jnp.stack([real_b, imag_b]).reshape(2, 2, groups, per_bins, 1, per_dev, width)
    turned = lax.all_to_all(outgoing, ("seq", "fsdp"), split_axis=2, concat_axis=4, tiled=True)
    turned = turned.reshape(2, 2, per_bins, row_count, width)
    real_b = turned[0]
    imag_b = turned[1]
    real_x = (
        jnp.einsum("kqmc,mr->kqrc", real_b, last_cos, preferred_element_type=f32)
        + jnp.einsum("kqmc,mr->kqrc", imag_b, last_sin, preferred_element_type=f32)
    ).astype(jnp.bfloat16)
    imag_x = (
        jnp.einsum("kqmc,mr->kqrc", imag_b, last_cos, preferred_element_type=f32)
        - jnp.einsum("kqmc,mr->kqrc", real_b, last_sin, preferred_element_type=f32)
    ).astype(jnp.bfloat16)
    real_z, imag_z = multiply(real_x, imag_x)
    real_v = jnp.einsum("qrc,mr->qmc", real_z, last_cos, preferred_element_type=f32) - jnp.einsum(
        "qrc,mr->qmc", imag_z, last_sin, preferred_element_type=f32
    )
    imag_v = jnp.einsum("qrc,mr->qmc", imag_z, last_cos, preferred_element_type=f32) + jnp.einsum(
        "qrc,mr->qmc", real_z, last_sin, preferred_element_type=f32
    )
    row_ids, mid_ids = index_grid(per_bins, row_count)
    twist_cos, twist_sin = phase_pair(row_ids + position * per_bins, mid_ids, length)
    twist_cos = twist_cos[:, :, None]
    twist_sin = twist_sin[:, :, None]
    real_w = (real_v * twist_cos - imag_v * twist_sin).astype(jnp.bfloat16)
    imag_w = (imag_v * twist_cos + real_v * twist_sin).astype(jnp.bfloat16)
    backward = jnp.stack([real_w, imag_w]).reshape(2, 1, per_bins, groups, per_dev, width)
    returned = lax.all_to_all(backward, ("seq", "fsdp"), split_axis=3, concat_axis=1, tiled=True)
    returned = returned.reshape(2, period_rows, per_dev, width)
    conv_rows = jnp.einsum(
        "qp,qmc->pmc", first_cos, returned[0], preferred_element_type=f32
    ) - jnp.einsum("qp,qmc->pmc", first_sin, returned[1], preferred_element_type=f32)
    conv_rows = (conv_rows * scale).astype(jnp.bfloat16)
    homed = lax.all_to_all(
        conv_rows.reshape(groups, 1, per_dev, width),
        ("seq", "fsdp"),
        split_axis=0,
        concat_axis=1,
        tiled=True,
    )
    conv = homed.reshape(row_count, width)
    result = query * (conv.astype(jnp.float32) + skip_gain * product.astype(jnp.float32))
    return result.astype(jnp.bfloat16)


def wave_table(size):
    freq, time = np.meshgrid(np.arange(size), np.arange(size), indexing="ij")
    angle = ((2 * freq + 1) * time % (4 * size)) * (math.pi / (2 * size))
    return np.concatenate([np.cos(angle), np.sin(angle)], axis=0)


def exchange(value, axis):
    return lax.ppermute(value, axis, [(0, 1), (1, 0)])


def whole_specs(count):
    return [pl.BlockSpec(memory_space=pltpu.VMEM)] * count


def split_channels(summed, own_half):
    half = summed.shape[1] // 2
    low, high = (summed[:, :half], summed[:, half:])
    first = own_half == 0
    return (jnp.where(first, low, high), jnp.where(first, high, low))


def pick_rows(source, target):
    lines = lax.broadcasted_iota(jnp.int32, (HALO, HALO), 0)
    places = lax.broadcasted_iota(jnp.int32, (HALO, HALO), 1)
    wanted = (lines - target == places - source) & (places >= source) & (places < source + 2)
    return wanted.astype(F32).astype(BF16)


def pack_body(rows_ref, pack_ref):
    width = pack_ref.shape[1]
    last = rows_ref[rows_ref.shape[0] - HALO :, :]
    total = jnp.zeros((HALO, width), F32)
    for piece in range(last.shape[1] // width):
        part = last[:, piece * width : (piece + 1) * width]
        total += jnp.dot(pick_rows(HALO - 2, 2 * piece), part, preferred_element_type=F32)
    pack_ref[...] = total.astype(BF16)


def unpack_halo(pieces, count):
    parts = [
        jnp.dot(pick_rows(2 * piece, HALO - 2), pieces, preferred_element_type=F32).astype(BF16)
        for piece in range(count)
    ]
    return jnp.concatenate(parts, axis=1)


def project(rows, weight_ref, branches, keep_ref, send_ref):
    own_half = lax.axis_index("fsdp")
    half = weight_ref.shape[2] // 2
    for place, branch in enumerate(branches):
        summed = jnp.dot(rows, weight_ref[branch], preferred_element_type=F32)
        keep, send = split_channels(summed, own_half)
        lanes = slice(place * half, (place + 1) * half)
        keep_ref[:, lanes] = keep
        send_ref[:, lanes] = send.astype(send_ref.dtype)


def project_first_body(rows_ref, cycled_ref, weight_ref, keep_ref, send_ref):
    here = lax.axis_index("chan") == lax.axis_index("fsdp")
    rows = jnp.where(here, rows_ref[...], cycled_ref[...])
    project(rows, weight_ref, (0, 1, 2), keep_ref, send_ref)


def project_second_body(
    branches, cycled_ref, hop_ref, pack_ref, pack_hop_ref, weight_ref, keep_ref, send_ref, *done_refs
):
    here = lax.axis_index("chan") == lax.axis_index("fsdp")
    pieces = cycled_ref.shape[1] // pack_ref.shape[1]
    rows = jnp.where(here, cycled_ref[...], hop_ref[...])
    halo = unpack_halo(jnp.where(here, pack_ref[...], pack_hop_ref[...]), pieces)
    halo = jnp.where(lax.axis_index("seq") > 0, halo, jnp.zeros_like(halo))
    rows = jnp.concatenate([halo, rows], axis=0)
    project(rows, weight_ref, branches, keep_ref, send_ref)
    for done_ref in done_refs:
        done_ref[...] = jnp.zeros_like(done_ref)


def sort_taps_body(*refs):
    keep_ref, send_ref, done_ref = refs[-3:]
    position = lax.axis_index("seq")
    first = lax.axis_index("fsdp") == 0
    blocks, _, half = keep_ref.shape
    for step in range(blocks):
        block = position ^ step
        taps = refs[step][...]
        low, high = (taps[:, :half], taps[:, half:])
        keep_ref[block] = jnp.where(first, low, high)
        send_ref[block] = jnp.where(first, high, low)
    done_ref[...] = jnp.zeros_like(done_ref)


def after_body(*refs):
    pass


def after(value, *orders):
    return pl.pallas_call(
        after_body,
        in_specs=whole_specs(1 + len(orders)),
        out_specs=whole_specs(1)[0],
        out_shape=shape(value.shape, value.dtype),
        input_output_aliases={0: 0},
        compiler_params=pltpu.CompilerParams(vmem_limit_bytes=32 * 1024 * 1024),
    )(value, *orders)


def taps_body(table_ref, keep_ref, got_ref, real_ref, imag_ref):
    first = lax.axis_index("fsdp") == 0
    blocks = keep_ref.shape[0]
    size = table_ref.shape[1]
    sign = 1.0 - 2.0 * (lax.broadcasted_iota(jnp.int32, (size, 1), 0) % 2).astype(F32)
    sign = sign * (1.0 / size)
    before_real = before_imag = None
    for block in range(blocks):
        keep, got = (keep_ref[block], got_ref[block])
        taps = jnp.concatenate(
            [jnp.where(first, keep, got), jnp.where(first, got, keep)], axis=0
        )
        waves = jnp.dot(table_ref[...], taps, preferred_element_type=F32)
        real, imag = (waves[:size], -waves[size:])
        if block == 0:
            real_ref[block] = real * (1.0 / size)
            imag_ref[block] = imag * (1.0 / size)
        else:
            real_ref[block] = real * (1.0 / size) - sign * before_imag
            imag_ref[block] = imag * (1.0 / size) + sign * before_real
        before_real, before_imag = (real, imag)


def mixed_branches(branches, keep_first, keep_second, got_first, got_second, short_ref, joined):
    own = lax.axis_index("fsdp")
    rows = keep_first.shape[0]
    half = keep_second.shape[1] // len(branches)
    first_lanes = slice(branches[0] * half, (branches[-1] + 1) * half)
    joined[:HALO, :] = keep_second[:HALO, :] + got_second[:HALO, :].astype(F32)
    own_start = pl.multiple_of(HALO + own * rows, HALO)
    other_start = pl.multiple_of(HALO + (1 - own) * rows, HALO)
    joined[pl.ds(own_start, rows), :] = (
        keep_first[:, first_lanes] + got_second[HALO:, :].astype(F32)
    )
    joined[pl.ds(other_start, rows), :] = (
        keep_second[HALO:, :] + got_first[:, first_lanes].astype(F32)
    )
    mixed = []
    for place, branch in enumerate(branches):
        lanes = slice(place * half, (place + 1) * half)
        total = None
        for tap in range(3):
            taps = short_ref[tap, branch : branch + 1, :]
            taps = jnp.where(own == 0, taps[:, :half], taps[:, half:])
            term = taps * joined[pl.ds(HALO - tap, 2 * rows), lanes]
            total = term if total is None else total + term
        mixed.append(total)
    return mixed


def product_body(
    keep_first, keep_second, got_first, got_second, short_ref, order_ref, product_ref, joined
):
    key, value = mixed_branches(
        (1, 2), keep_first, keep_second, got_first, got_second, short_ref, joined
    )
    product_ref[...] = (key * value).astype(BF16)


def query_body(keep_first, keep_second, got_first, got_second, short_ref, query_ref, joined):
    (query,) = mixed_branches(
        (0,), keep_first, keep_second, got_first, got_second, short_ref, joined
    )
    query_ref[...] = query


def spectrum_term(step, block_ref, real_ref, imag_ref, table_ref):
    position = lax.axis_index("seq")
    size = table_ref.shape[1]
    source = position ^ step
    back = jnp.maximum(position - source, 0)
    block = block_ref[...]
    if step:
        block = jnp.where(source < position, block, jnp.zeros_like(block))
    waves = jnp.dot(table_ref[...], block, preferred_element_type=F32)
    real, imag = (waves[:size], -waves[size:])
    tap_real, tap_imag = (real_ref[back], imag_ref[back])
    return (real * tap_real - imag * tap_imag, real * tap_imag + imag * tap_real)


def conv_early_body(own_ref, far_ref, near_ref, real_ref, imag_ref, table_ref, total_ref):
    total_ref[0], total_ref[1] = spectrum_term(0, own_ref, real_ref, imag_ref, table_ref)
    for step, block_ref in ((3, far_ref), (1, near_ref)):
        real, imag = spectrum_term(step, block_ref, real_ref, imag_ref, table_ref)
        total_ref[0] += real
        total_ref[1] += imag


def gated_rows(place, rows, stacked, turned_ref, query_ref, gain_ref, own_ref):
    half = own_ref.shape[1]
    lines = pl.ds(pl.multiple_of(place * rows, rows), rows)
    conv = jnp.dot(turned_ref[lines, :], stacked, preferred_element_type=F32)
    first = lax.axis_index("fsdp") == 0
    gain = jnp.where(first, gain_ref[:, :half], gain_ref[:, half:])
    gated = query_ref[lines, :] * (conv + gain * own_ref[lines, :].astype(F32))
    return gated.astype(BF16)


def conv_last_body(
    last_ref, total_ref, real_ref, imag_ref, table_ref, turned_ref, query_ref, gain_ref, own_ref,
    go_ref, stacked_ref
):
    real, imag = spectrum_term(2, last_ref, real_ref, imag_ref, table_ref)
    stacked = jnp.concatenate([total_ref[0] + real, -(total_ref[1] + imag)], axis=0).astype(BF16)
    stacked_ref[...] = stacked
    other = 1 - lax.axis_index("fsdp")
    go_ref[...] = gated_rows(
        other, go_ref.shape[0], stacked, turned_ref, query_ref, gain_ref, own_ref
    )


def conv_stay_body(stacked_ref, turned_ref, query_ref, gain_ref, own_ref, stay_ref):
    own = lax.axis_index("fsdp")
    stay_ref[...] = gated_rows(
        own, stay_ref.shape[0], stacked_ref[...], turned_ref, query_ref, gain_ref, own_ref
    )


def join_body(stay_ref, got_ref, out_ref):
    first = lax.axis_index("fsdp") == 0
    half = stay_ref.shape[1]
    out_ref[:, :half] = jnp.where(first, stay_ref[...], got_ref[...])
    out_ref[:, half:] = jnp.where(first, got_ref[...], stay_ref[...])


def shape(dims, kind):
    return jax.ShapeDtypeStruct(dims, kind)


def pair_mesh(tokens, proj_weight, short_weight, skip_gain, filter_taps):
    rows = tokens.shape[0]
    width = proj_weight.shape[2]
    half = width // 2
    size = 2 * rows
    blocks = lax.axis_size("seq")
    weight = jnp.transpose(proj_weight, (1, 0, 2))
    pairs = [[(s, s ^ step) for s in range(blocks)] for step in range(blocks)]
    call = functools.partial(
        pl.pallas_call, compiler_params=pltpu.CompilerParams(vmem_limit_bytes=32 * 1024 * 1024)
    )

    cycled = lax.ppermute(tokens, ("fsdp", "chan"), [(1, 3), (3, 2), (2, 0), (0, 1)])
    token = shape((8, 128), F32)
    pack = call(
        pack_body,
        cost_estimate=LONG,
        in_specs=whole_specs(1),
        out_specs=whole_specs(1)[0],
        out_shape=shape((HALO, width), BF16),
    )(tokens)
    pack_got = lax.ppermute(
        pack,
        ("seq", "fsdp", "chan"),
        [
            (4 * s + 2 * f + c, 4 * ((s + 1) % blocks) + 2 * (f ^ (1 - c)) + c)
            for s in range(blocks)
            for f in range(2)
            for c in range(2)
        ],
    )
    tap_blocks = [filter_taps] + [
        lax.ppermute(filter_taps, "seq", pairs[step]) for step in range(1, blocks)
    ]
    cycled = after(cycled, pack_got)
    hop = exchange(cycled, "chan")
    pack_hop = exchange(pack_got, "chan")
    keep_first, send_first = call(
        project_first_body,
        cost_estimate=LONG,
        in_specs=whole_specs(3),
        out_specs=whole_specs(2),
        out_shape=(shape((rows, 3 * half), F32), shape((rows, 3 * half), BF16)),
    )(tokens, cycled, weight)
    got_first = exchange(send_first, "fsdp")
    keep_product, send_product, second_done = call(
        functools.partial(project_second_body, (1, 2)),
        in_specs=whole_specs(5),
        out_specs=whole_specs(3),
        out_shape=(
            shape((HALO + rows, 2 * half), F32),
            shape((HALO + rows, 2 * half), BF16),
            token,
        ),
    )(cycled, hop, pack_got, pack_hop, weight)
    keep_query, send_query = call(
        functools.partial(project_second_body, (0,)),
        in_specs=whole_specs(5),
        out_specs=whole_specs(2),
        out_shape=(shape((HALO + rows, half), F32), shape((HALO + rows, half), F32)),
    )(cycled, hop, pack_got, pack_hop, weight)
    tap_keep, tap_send, tap_done = call(
        sort_taps_body,
        in_specs=whole_specs(1 + blocks),
        out_specs=whole_specs(3),
        out_shape=(
            shape((blocks, rows, half), BF16),
            shape((blocks, rows, half), BF16),
            token,
        ),
    )(*tap_blocks, second_done)
    got_product = exchange(send_product, "fsdp")
    got_query = exchange(send_query, "fsdp")

    product = call(
        product_body,
        in_specs=whole_specs(6),
        out_specs=whole_specs(1)[0],
        out_shape=shape((size, half), BF16),
        scratch_shapes=[pltpu.VMEM((HALO + size, 2 * half), F32)],
    )(keep_first, keep_product, got_first, got_product, short_weight, tap_done)
    query = call(
        query_body,
        in_specs=whole_specs(5),
        out_specs=whole_specs(1)[0],
        out_shape=shape((size, half), F32),
        scratch_shapes=[pltpu.VMEM((HALO + size, half), F32)],
    )(keep_first, keep_query, got_first, got_query, short_weight)
    tap_got = exchange(tap_send, "fsdp")
    last, far, near = (lax.ppermute(product, "seq", pairs[step]) for step in (2, 3, 1))
    table = wave_table(size)
    forward = jnp.asarray(table, dtype=BF16)
    inverse = jnp.asarray(table.T, dtype=BF16)
    tap_real, tap_imag = call(
        taps_body,
        in_specs=whole_specs(3),
        out_specs=whole_specs(2),
        out_shape=(shape((blocks, size, half), F32), shape((blocks, size, half), F32)),
    )(forward, tap_keep, tap_got)
    total = call(
        conv_early_body,
        in_specs=whole_specs(6),
        out_specs=whole_specs(1)[0],
        out_shape=shape((2, size, half), F32),
    )(product, far, near, tap_real, tap_imag, forward)
    ending = (inverse, query, skip_gain.reshape(1, width), product)
    go, stacked = call(
        conv_last_body,
        in_specs=whole_specs(9),
        out_specs=whole_specs(2),
        out_shape=(shape((rows, half), BF16), shape((2 * size, half), BF16)),
    )(last, total, tap_real, tap_imag, forward, *ending)
    stay = call(
        conv_stay_body,
        in_specs=whole_specs(5),
        out_specs=whole_specs(1)[0],
        out_shape=shape((rows, half), BF16),
    )(stacked, *ending)
    back = exchange(go, "fsdp")
    return call(
        join_body,
        in_specs=whole_specs(2),
        out_specs=whole_specs(1)[0],
        out_shape=shape((rows, width), BF16),
    )(stay, back)


def solution(mesh):
    in_specs = (
        P(("grp", "seq", "fsdp"), "chan"),
        P("fsdp", None, "chan"),
        P(None, None, "chan"),
        P("chan"),
        P(("seq", "fsdp"), "chan"),
    )
    out_specs = P(("grp", "seq", "fsdp"), "chan")
    sizes = mesh.shape
    paired = sizes["fsdp"] == 2 and sizes["chan"] == 2 and sizes["seq"] == 4
    per_device = pair_mesh if paired else any_mesh
    return jax.shard_map(
        per_device, mesh=mesh, in_specs=in_specs, out_specs=out_specs, check_vma=False
    )
```

```python
import functools
import math

import jax
import jax.numpy as jnp
import numpy as np
from jax import lax
from jax.experimental import pallas as pl
from jax.experimental.pallas import tpu as pltpu
from jax.sharding import PartitionSpec as P

HALO = 16
LONG = pl.CostEstimate(flops=10_000_000_000, bytes_accessed=40_000_000, transcendentals=0)
F32 = jnp.float32
BF16 = jnp.bfloat16


def shifted(value, axis, steps):
    count = lax.axis_size(axis)
    initial, last = (max(0, -steps), min(count, count - steps))
    return lax.ppermute(value, axis, [(source, source + steps) for source in range(initial, last)])


def index_grid(row_count, col_count):
    return (
        lax.broadcasted_iota(jnp.int32, (row_count, col_count), 0),
        lax.broadcasted_iota(jnp.int32, (row_count, col_count), 1),
    )


def phase_pair(row_ids, col_ids, period):
    wrapped = row_ids * col_ids % period
    phase = wrapped.astype(jnp.float32) * (2.0 * math.pi / period)
    return (jnp.cos(phase), jnp.sin(phase))


def multiply(real_x, imag_x):
    sig_real = real_x[0].astype(jnp.float32)
    sig_imag = imag_x[0].astype(jnp.float32)
    tap_real = real_x[1].astype(jnp.float32)
    tap_imag = imag_x[1].astype(jnp.float32)
    real_z = (sig_real * tap_real - sig_imag * tap_imag).astype(jnp.bfloat16)
    imag_z = (sig_real * tap_imag + sig_imag * tap_real).astype(jnp.bfloat16)
    return (real_z, imag_z)


def spread(stacked, groups, inner_shape):
    shaped = stacked.reshape((2, groups, 1) + inner_shape)
    moved = lax.all_to_all(shaped, ("seq", "fsdp"), split_axis=1, concat_axis=2, tiled=True)
    return moved.reshape((2, groups) + inner_shape)


def any_mesh(tokens, proj_weight, short_weight, skip_gain, filter_taps):
    whole = lax.all_gather(tokens, "chan", axis=1, tiled=True)
    row_count = whole.shape[0]
    width = proj_weight.shape[2]
    flat_width = 3 * width
    piece = lax.all_gather(proj_weight, "fsdp", axis=0, tiled=True)
    summed = jnp.dot(
        whole, piece.reshape(piece.shape[0], flat_width), preferred_element_type=jnp.float32
    )
    projected = summed.astype(jnp.bfloat16).reshape(row_count, 3, width)
    earlier = shifted(projected[row_count - 2 :], ("seq", "fsdp"), 1)
    extended = jnp.concatenate([earlier, projected], axis=0).astype(jnp.float32)
    mixed = (
        short_weight[0] * extended[2:]
        + short_weight[1] * extended[1:-1]
        + short_weight[2] * extended[:-2]
    )
    query = mixed[:, 0]
    product = (mixed[:, 1] * mixed[:, 2]).astype(jnp.bfloat16)
    groups = lax.axis_size(("seq", "fsdp"))
    position = lax.axis_index(("seq", "fsdp"))
    period_rows = 2 * groups
    length = period_rows * row_count
    scale = 1.0 / length
    bin_ids, tap_ids = index_grid(period_rows, groups)
    first_cos, first_sin = phase_pair(bin_ids, tap_ids, period_rows)
    first_cos = first_cos.astype(jnp.bfloat16)
    first_sin = first_sin.astype(jnp.bfloat16)
    col_ids, freq_ids = index_grid(row_count, row_count)
    last_cos, last_sin = phase_pair(col_ids, freq_ids, row_count)
    last_cos = last_cos.astype(jnp.bfloat16)
    last_sin = last_sin.astype(jnp.bfloat16)
    stacked = jnp.stack([product, filter_taps])
    f32 = jnp.float32
    per_dev = row_count // groups
    per_bins = period_rows // groups
    arrived = spread(stacked.reshape(2, groups, per_dev, width), groups, (per_dev, width))
    real_a = jnp.einsum("qp,kpmc->kqmc", first_cos, arrived, preferred_element_type=f32)
    imag_a = -jnp.einsum("qp,kpmc->kqmc", first_sin, arrived, preferred_element_type=f32)
    row_ids, mid_ids = index_grid(period_rows, per_dev)
    twist_cos, twist_sin = phase_pair(row_ids, mid_ids + position * per_dev, length)
    twist_cos = twist_cos[:, :, None]
    twist_sin = twist_sin[:, :, None]
    real_b = (real_a * twist_cos + imag_a * twist_sin).astype(jnp.bfloat16)
    imag_b = (imag_a * twist_cos - real_a * twist_sin).astype(jnp.bfloat16)
    outgoing = jnp.stack([real_b, imag_b]).reshape(2, 2, groups, per_bins, 1, per_dev, width)
    turned = lax.all_to_all(outgoing, ("seq", "fsdp"), split_axis=2, concat_axis=4, tiled=True)
    turned = turned.reshape(2, 2, per_bins, row_count, width)
    real_b = turned[0]
    imag_b = turned[1]
    real_x = (
        jnp.einsum("kqmc,mr->kqrc", real_b, last_cos, preferred_element_type=f32)
        + jnp.einsum("kqmc,mr->kqrc", imag_b, last_sin, preferred_element_type=f32)
    ).astype(jnp.bfloat16)
    imag_x = (
        jnp.einsum("kqmc,mr->kqrc", imag_b, last_cos, preferred_element_type=f32)
        - jnp.einsum("kqmc,mr->kqrc", real_b, last_sin, preferred_element_type=f32)
    ).astype(jnp.bfloat16)
    real_z, imag_z = multiply(real_x, imag_x)
    real_v = jnp.einsum("qrc,mr->qmc", real_z, last_cos, preferred_element_type=f32) - jnp.einsum(
        "qrc,mr->qmc", imag_z, last_sin, preferred_element_type=f32
    )
    imag_v = jnp.einsum("qrc,mr->qmc", imag_z, last_cos, preferred_element_type=f32) + jnp.einsum(
        "qrc,mr->qmc", real_z, last_sin, preferred_element_type=f32
    )
    row_ids, mid_ids = index_grid(per_bins, row_count)
    twist_cos, twist_sin = phase_pair(row_ids + position * per_bins, mid_ids, length)
    twist_cos = twist_cos[:, :, None]
    twist_sin = twist_sin[:, :, None]
    real_w = (real_v * twist_cos - imag_v * twist_sin).astype(jnp.bfloat16)
    imag_w = (imag_v * twist_cos + real_v * twist_sin).astype(jnp.bfloat16)
    backward = jnp.stack([real_w, imag_w]).reshape(2, 1, per_bins, groups, per_dev, width)
    returned = lax.all_to_all(backward, ("seq", "fsdp"), split_axis=3, concat_axis=1, tiled=True)
    returned = returned.reshape(2, period_rows, per_dev, width)
    conv_rows = jnp.einsum(
        "qp,qmc->pmc", first_cos, returned[0], preferred_element_type=f32
    ) - jnp.einsum("qp,qmc->pmc", first_sin, returned[1], preferred_element_type=f32)
    conv_rows = (conv_rows * scale).astype(jnp.bfloat16)
    homed = lax.all_to_all(
        conv_rows.reshape(groups, 1, per_dev, width),
        ("seq", "fsdp"),
        split_axis=0,
        concat_axis=1,
        tiled=True,
    )
    conv = homed.reshape(row_count, width)
    result = query * (conv.astype(jnp.float32) + skip_gain * product.astype(jnp.float32))
    return result.astype(jnp.bfloat16)


def wave_table(size):
    freq, time = np.meshgrid(np.arange(size), np.arange(size), indexing="ij")
    angle = ((2 * freq + 1) * time % (4 * size)) * (math.pi / (2 * size))
    return np.concatenate([np.cos(angle), np.sin(angle)], axis=0)


def exchange(value, axis):
    return lax.ppermute(value, axis, [(0, 1), (1, 0)])


def whole_specs(count):
    return [pl.BlockSpec(memory_space=pltpu.VMEM)] * count


def split_channels(summed, own_half):
    half = summed.shape[1] // 2
    low, high = (summed[:, :half], summed[:, half:])
    first = own_half == 0
    return (jnp.where(first, low, high), jnp.where(first, high, low))


def pick_rows(source, target):
    lines = lax.broadcasted_iota(jnp.int32, (HALO, HALO), 0)
    places = lax.broadcasted_iota(jnp.int32, (HALO, HALO), 1)
    wanted = (lines - target == places - source) & (places >= source) & (places < source + 2)
    return wanted.astype(F32).astype(BF16)


def pack_body(rows_ref, pack_ref):
    width = pack_ref.shape[1]
    last = rows_ref[rows_ref.shape[0] - HALO :, :]
    total = jnp.zeros((HALO, width), F32)
    for piece in range(last.shape[1] // width):
        part = last[:, piece * width : (piece + 1) * width]
        total += jnp.dot(pick_rows(HALO - 2, 2 * piece), part, preferred_element_type=F32)
    pack_ref[...] = total.astype(BF16)


def unpack_halo(pieces, count):
    parts = [
        jnp.dot(pick_rows(2 * piece, HALO - 2), pieces, preferred_element_type=F32).astype(BF16)
        for piece in range(count)
    ]
    return jnp.concatenate(parts, axis=1)


def project(rows, weight_ref, branches, keep_ref, send_ref):
    own_half = lax.axis_index("fsdp")
    half = weight_ref.shape[2] // 2
    for place, branch in enumerate(branches):
        summed = jnp.dot(rows, weight_ref[branch], preferred_element_type=F32)
        keep, send = split_channels(summed, own_half)
        lanes = slice(place * half, (place + 1) * half)
        keep_ref[:, lanes] = keep
        send_ref[:, lanes] = send.astype(BF16)


def project_first_body(
    rows_ref, cycled_ref, weight_ref, keep_product, send_product, keep_query, send_query
):
    here = lax.axis_index("chan") == lax.axis_index("fsdp")
    rows = jnp.where(here, rows_ref[...], cycled_ref[...])
    project(rows, weight_ref, (1, 2), keep_product, send_product)
    project(rows, weight_ref, (0,), keep_query, send_query)


def arrived_rows(cycled_ref, hop_ref, pack_ref, pack_hop_ref):
    here = lax.axis_index("chan") == lax.axis_index("fsdp")
    pieces = cycled_ref.shape[1] // pack_ref.shape[1]
    rows = jnp.where(here, cycled_ref[...], hop_ref[...])
    halo = unpack_halo(jnp.where(here, pack_ref[...], pack_hop_ref[...]), pieces)
    halo = jnp.where(lax.axis_index("seq") > 0, halo, jnp.zeros_like(halo))
    return jnp.concatenate([halo, rows], axis=0)


def project_product_body(
    cycled_ref, hop_ref, pack_ref, pack_hop_ref, weight_ref, keep_ref, send_ref, done_ref
):
    rows = arrived_rows(cycled_ref, hop_ref, pack_ref, pack_hop_ref)
    project(rows, weight_ref, (1, 2), keep_ref, send_ref)
    done_ref[...] = jnp.zeros_like(done_ref)


def project_query_body(
    cycled_ref, hop_ref, pack_ref, pack_hop_ref, weight_ref, first_ref, keep_ref, send_ref
):
    rows = arrived_rows(cycled_ref, hop_ref, pack_ref, pack_hop_ref)
    count = first_ref.shape[0]
    send_ref[:count, :] = first_ref[...]
    project(rows, weight_ref, (0,), keep_ref, send_ref.at[count:, :])


def sort_taps_body(*refs):
    keep_ref, send_ref, done_ref = refs[-3:]
    position = lax.axis_index("seq")
    first = lax.axis_index("fsdp") == 0
    blocks, _, half = keep_ref.shape
    for step in range(blocks):
        block = position ^ step
        taps = refs[step][...]
        low, high = (taps[:, :half], taps[:, half:])
        keep_ref[block] = jnp.where(first, low, high)
        send_ref[block] = jnp.where(first, high, low)
    done_ref[...] = jnp.zeros_like(done_ref)


def after_body(*refs):
    pass


def after(value, *orders):
    return pl.pallas_call(
        after_body,
        in_specs=whole_specs(1 + len(orders)),
        out_specs=whole_specs(1)[0],
        out_shape=shape(value.shape, value.dtype),
        input_output_aliases={0: 0},
        compiler_params=pltpu.CompilerParams(vmem_limit_bytes=32 * 1024 * 1024),
    )(value, *orders)


def taps_body(table_ref, keep_ref, got_ref, real_ref, imag_ref):
    first = lax.axis_index("fsdp") == 0
    blocks = keep_ref.shape[0]
    size = table_ref.shape[1]
    sign = 1.0 - 2.0 * (lax.broadcasted_iota(jnp.int32, (size, 1), 0) % 2).astype(F32)
    sign = sign * (1.0 / size)
    before_real = before_imag = None
    for block in range(blocks):
        keep, got = (keep_ref[block], got_ref[block])
        taps = jnp.concatenate(
            [jnp.where(first, keep, got), jnp.where(first, got, keep)], axis=0
        )
        waves = jnp.dot(table_ref[...], taps, preferred_element_type=F32)
        real, imag = (waves[:size], -waves[size:])
        if block == 0:
            real_ref[block] = real * (1.0 / size)
            imag_ref[block] = imag * (1.0 / size)
        else:
            real_ref[block] = real * (1.0 / size) - sign * before_imag
            imag_ref[block] = imag * (1.0 / size) + sign * before_real
        before_real, before_imag = (real, imag)


def mixed_branches(branches, keep_first, keep_second, got_first, got_second, short_ref, joined):
    own = lax.axis_index("fsdp")
    rows = keep_first.shape[0]
    half = keep_second.shape[1] // len(branches)
    joined[:HALO, :] = keep_second[:HALO, :] + got_second[:HALO, :].astype(F32)
    own_start = pl.multiple_of(HALO + own * rows, HALO)
    other_start = pl.multiple_of(HALO + (1 - own) * rows, HALO)
    joined[pl.ds(own_start, rows), :] = keep_first[...] + got_second[HALO:, :].astype(F32)
    joined[pl.ds(other_start, rows), :] = keep_second[HALO:, :] + got_first[...].astype(F32)
    mixed = []
    for place, branch in enumerate(branches):
        lanes = slice(place * half, (place + 1) * half)
        total = None
        for tap in range(3):
            taps = short_ref[tap, branch : branch + 1, :]
            taps = jnp.where(own == 0, taps[:, :half], taps[:, half:])
            term = taps * joined[pl.ds(HALO - tap, 2 * rows), lanes]
            total = term if total is None else total + term
        mixed.append(total)
    return mixed


def product_body(
    keep_first, keep_second, got_first, got_second, short_ref, order_ref, product_ref, joined
):
    key, value = mixed_branches(
        (1, 2), keep_first, keep_second, got_first, got_second, short_ref, joined
    )
    product_ref[...] = (key * value).astype(BF16)


def query_body(keep_first, keep_second, got_ref, short_ref, query_ref, joined):
    rows = keep_first.shape[0]
    (query,) = mixed_branches(
        (0,), keep_first, keep_second, got_ref.at[:rows, :], got_ref.at[rows:, :], short_ref, joined
    )
    query_ref[...] = query


def spectrum_term(step, block_ref, real_ref, imag_ref, table_ref):
    position = lax.axis_index("seq")
    size = table_ref.shape[1]
    source = position ^ step
    back = jnp.maximum(position - source, 0)
    block = block_ref[...]
    if step:
        block = jnp.where(source < position, block, jnp.zeros_like(block))
    waves = jnp.dot(table_ref[...], block, preferred_element_type=F32)
    real, imag = (waves[:size], -waves[size:])
    tap_real, tap_imag = (real_ref[back], imag_ref[back])
    return (real * tap_real - imag * tap_imag, real * tap_imag + imag * tap_real)


def conv_early_body(own_ref, far_ref, near_ref, real_ref, imag_ref, table_ref, total_ref):
    total_ref[0], total_ref[1] = spectrum_term(0, own_ref, real_ref, imag_ref, table_ref)
    for step, block_ref in ((3, far_ref), (1, near_ref)):
        real, imag = spectrum_term(step, block_ref, real_ref, imag_ref, table_ref)
        total_ref[0] += real
        total_ref[1] += imag


def gated_rows(place, rows, stacked, turned_ref, query_ref, gain_ref, own_ref):
    half = own_ref.shape[1]
    lines = pl.ds(pl.multiple_of(place * rows, rows), rows)
    conv = jnp.dot(turned_ref[lines, :], stacked, preferred_element_type=F32)
    first = lax.axis_index("fsdp") == 0
    gain = jnp.where(first, gain_ref[:, :half], gain_ref[:, half:])
    gated = query_ref[lines, :] * (conv + gain * own_ref[lines, :].astype(F32))
    return gated.astype(BF16)


def conv_last_body(
    last_ref, total_ref, real_ref, imag_ref, table_ref, turned_ref, query_ref, gain_ref, own_ref,
    go_ref, stacked_ref
):
    real, imag = spectrum_term(2, last_ref, real_ref, imag_ref, table_ref)
    stacked = jnp.concatenate([total_ref[0] + real, -(total_ref[1] + imag)], axis=0).astype(BF16)
    stacked_ref[...] = stacked
    other = 1 - lax.axis_index("fsdp")
    go_ref[...] = gated_rows(
        other, go_ref.shape[0], stacked, turned_ref, query_ref, gain_ref, own_ref
    )


def conv_stay_body(stacked_ref, turned_ref, query_ref, gain_ref, own_ref, stay_ref):
    own = lax.axis_index("fsdp")
    stay_ref[...] = gated_rows(
        own, stay_ref.shape[0], stacked_ref[...], turned_ref, query_ref, gain_ref, own_ref
    )


def join_body(stay_ref, got_ref, out_ref):
    first = lax.axis_index("fsdp") == 0
    half = stay_ref.shape[1]
    out_ref[:, :half] = jnp.where(first, stay_ref[...], got_ref[...])
    out_ref[:, half:] = jnp.where(first, got_ref[...], stay_ref[...])


def shape(dims, kind):
    return jax.ShapeDtypeStruct(dims, kind)


def pair_mesh(tokens, proj_weight, short_weight, skip_gain, filter_taps):
    rows = tokens.shape[0]
    width = proj_weight.shape[2]
    half = width // 2
    size = 2 * rows
    blocks = lax.axis_size("seq")
    weight = jnp.transpose(proj_weight, (1, 0, 2))
    pairs = [[(s, s ^ step) for s in range(blocks)] for step in range(blocks)]
    call = functools.partial(
        pl.pallas_call, compiler_params=pltpu.CompilerParams(vmem_limit_bytes=32 * 1024 * 1024)
    )

    cycled = lax.ppermute(tokens, ("fsdp", "chan"), [(1, 3), (3, 2), (2, 0), (0, 1)])
    token = shape((8, 128), F32)
    pack = call(
        pack_body,
        cost_estimate=LONG,
        in_specs=whole_specs(1),
        out_specs=whole_specs(1)[0],
        out_shape=shape((HALO, width), BF16),
    )(tokens)
    pack_got = lax.ppermute(
        pack,
        ("seq", "fsdp", "chan"),
        [
            (4 * s + 2 * f + c, 4 * ((s + 1) % blocks) + 2 * (f ^ (1 - c)) + c)
            for s in range(blocks)
            for f in range(2)
            for c in range(2)
        ],
    )
    tap_blocks = [filter_taps] + [
        lax.ppermute(filter_taps, "seq", pairs[step]) for step in range(1, blocks)
    ]
    cycled = after(cycled, pack_got)
    hop = exchange(cycled, "chan")
    pack_hop = exchange(pack_got, "chan")
    keep_first, send_first, keep_first_query, send_first_query = call(
        project_first_body,
        cost_estimate=LONG,
        in_specs=whole_specs(3),
        out_specs=whole_specs(4),
        out_shape=(
            shape((rows, 2 * half), F32),
            shape((rows, 2 * half), BF16),
            shape((rows, half), F32),
            shape((rows, half), BF16),
        ),
    )(tokens, cycled, weight)
    got_first = exchange(send_first, "fsdp")
    arrived = (cycled, hop, pack_got, pack_hop, weight)
    keep_second, send_second, second_done = call(
        project_product_body,
        in_specs=whole_specs(5),
        out_specs=whole_specs(3),
        out_shape=(
            shape((HALO + rows, 2 * half), F32),
            shape((HALO + rows, 2 * half), BF16),
            token,
        ),
    )(*arrived)
    keep_second_query, send_query = call(
        project_query_body,
        in_specs=whole_specs(6),
        out_specs=whole_specs(2),
        out_shape=(
            shape((HALO + rows, half), F32),
            shape((rows + HALO + rows, half), BF16),
        ),
    )(*arrived, send_first_query)
    tap_keep, tap_send, tap_done = call(
        sort_taps_body,
        in_specs=whole_specs(1 + blocks),
        out_specs=whole_specs(3),
        out_shape=(
            shape((blocks, rows, half), BF16),
            shape((blocks, rows, half), BF16),
            token,
        ),
    )(*tap_blocks, second_done)
    got_second = exchange(send_second, "fsdp")
    got_query = exchange(send_query, "fsdp")

    product = call(
        product_body,
        in_specs=whole_specs(6),
        out_specs=whole_specs(1)[0],
        out_shape=shape((size, half), BF16),
        scratch_shapes=[pltpu.VMEM((HALO + size, 2 * half), F32)],
    )(keep_first, keep_second, got_first, got_second, short_weight, tap_done)
    query = call(
        query_body,
        in_specs=whole_specs(4),
        out_specs=whole_specs(1)[0],
        out_shape=shape((size, half), F32),
        scratch_shapes=[pltpu.VMEM((HALO + size, half), F32)],
    )(keep_first_query, keep_second_query, got_query, short_weight)
    tap_got = exchange(after(tap_send, got_first, keep_second_query), "fsdp")
    last, far, near = (lax.ppermute(product, "seq", pairs[step]) for step in (2, 3, 1))
    table = wave_table(size)
    forward = jnp.asarray(table, dtype=BF16)
    inverse = jnp.asarray(table.T, dtype=BF16)
    tap_real, tap_imag = call(
        taps_body,
        in_specs=whole_specs(3),
        out_specs=whole_specs(2),
        out_shape=(shape((blocks, size, half), F32), shape((blocks, size, half), F32)),
    )(forward, tap_keep, tap_got)
    total = call(
        conv_early_body,
        in_specs=whole_specs(6),
        out_specs=whole_specs(1)[0],
        out_shape=shape((2, size, half), F32),
    )(product, far, near, tap_real, tap_imag, forward)
    ending = (inverse, query, skip_gain.reshape(1, width), product)
    go, stacked = call(
        conv_last_body,
        in_specs=whole_specs(9),
        out_specs=whole_specs(2),
        out_shape=(shape((rows, half), BF16), shape((2 * size, half), BF16)),
    )(last, total, tap_real, tap_imag, forward, *ending)
    stay = call(
        conv_stay_body,
        in_specs=whole_specs(5),
        out_specs=whole_specs(1)[0],
        out_shape=shape((rows, half), BF16),
    )(stacked, *ending)
    back = exchange(go, "fsdp")
    return call(
        join_body,
        in_specs=whole_specs(2),
        out_specs=whole_specs(1)[0],
        out_shape=shape((rows, width), BF16),
    )(stay, back)


def solution(mesh):
    in_specs = (
        P(("grp", "seq", "fsdp"), "chan"),
        P("fsdp", None, "chan"),
        P(None, None, "chan"),
        P("chan"),
        P(("seq", "fsdp"), "chan"),
    )
    out_specs = P(("grp", "seq", "fsdp"), "chan")
    sizes = mesh.shape
    paired = sizes["fsdp"] == 2 and sizes["chan"] == 2 and sizes["seq"] == 4
    per_device = pair_mesh if paired else any_mesh
    return jax.shard_map(
        per_device, mesh=mesh, in_specs=in_specs, out_specs=out_specs, check_vma=False
    )
```

```python
import functools
import math

import jax
import jax.numpy as jnp
import numpy as np
from jax import lax
from jax.experimental import pallas as pl
from jax.experimental.pallas import tpu as pltpu
from jax.sharding import PartitionSpec as P

HALO = 16
LONG = pl.CostEstimate(flops=10_000_000_000, bytes_accessed=40_000_000, transcendentals=0)
F32 = jnp.float32
BF16 = jnp.bfloat16


def shifted(value, axis, steps):
    count = lax.axis_size(axis)
    initial, last = (max(0, -steps), min(count, count - steps))
    return lax.ppermute(value, axis, [(source, source + steps) for source in range(initial, last)])


def index_grid(row_count, col_count):
    return (
        lax.broadcasted_iota(jnp.int32, (row_count, col_count), 0),
        lax.broadcasted_iota(jnp.int32, (row_count, col_count), 1),
    )


def phase_pair(row_ids, col_ids, period):
    wrapped = row_ids * col_ids % period
    phase = wrapped.astype(jnp.float32) * (2.0 * math.pi / period)
    return (jnp.cos(phase), jnp.sin(phase))


def multiply(real_x, imag_x):
    sig_real = real_x[0].astype(jnp.float32)
    sig_imag = imag_x[0].astype(jnp.float32)
    tap_real = real_x[1].astype(jnp.float32)
    tap_imag = imag_x[1].astype(jnp.float32)
    real_z = (sig_real * tap_real - sig_imag * tap_imag).astype(jnp.bfloat16)
    imag_z = (sig_real * tap_imag + sig_imag * tap_real).astype(jnp.bfloat16)
    return (real_z, imag_z)


def spread(stacked, groups, inner_shape):
    shaped = stacked.reshape((2, groups, 1) + inner_shape)
    moved = lax.all_to_all(shaped, ("seq", "fsdp"), split_axis=1, concat_axis=2, tiled=True)
    return moved.reshape((2, groups) + inner_shape)


def any_mesh(tokens, proj_weight, short_weight, skip_gain, filter_taps):
    whole = lax.all_gather(tokens, "chan", axis=1, tiled=True)
    row_count = whole.shape[0]
    width = proj_weight.shape[2]
    flat_width = 3 * width
    piece = lax.all_gather(proj_weight, "fsdp", axis=0, tiled=True)
    summed = jnp.dot(
        whole, piece.reshape(piece.shape[0], flat_width), preferred_element_type=jnp.float32
    )
    projected = summed.astype(jnp.bfloat16).reshape(row_count, 3, width)
    earlier = shifted(projected[row_count - 2 :], ("seq", "fsdp"), 1)
    extended = jnp.concatenate([earlier, projected], axis=0).astype(jnp.float32)
    mixed = (
        short_weight[0] * extended[2:]
        + short_weight[1] * extended[1:-1]
        + short_weight[2] * extended[:-2]
    )
    query = mixed[:, 0]
    product = (mixed[:, 1] * mixed[:, 2]).astype(jnp.bfloat16)
    groups = lax.axis_size(("seq", "fsdp"))
    position = lax.axis_index(("seq", "fsdp"))
    period_rows = 2 * groups
    length = period_rows * row_count
    scale = 1.0 / length
    bin_ids, tap_ids = index_grid(period_rows, groups)
    first_cos, first_sin = phase_pair(bin_ids, tap_ids, period_rows)
    first_cos = first_cos.astype(jnp.bfloat16)
    first_sin = first_sin.astype(jnp.bfloat16)
    col_ids, freq_ids = index_grid(row_count, row_count)
    last_cos, last_sin = phase_pair(col_ids, freq_ids, row_count)
    last_cos = last_cos.astype(jnp.bfloat16)
    last_sin = last_sin.astype(jnp.bfloat16)
    stacked = jnp.stack([product, filter_taps])
    f32 = jnp.float32
    per_dev = row_count // groups
    per_bins = period_rows // groups
    arrived = spread(stacked.reshape(2, groups, per_dev, width), groups, (per_dev, width))
    real_a = jnp.einsum("qp,kpmc->kqmc", first_cos, arrived, preferred_element_type=f32)
    imag_a = -jnp.einsum("qp,kpmc->kqmc", first_sin, arrived, preferred_element_type=f32)
    row_ids, mid_ids = index_grid(period_rows, per_dev)
    twist_cos, twist_sin = phase_pair(row_ids, mid_ids + position * per_dev, length)
    twist_cos = twist_cos[:, :, None]
    twist_sin = twist_sin[:, :, None]
    real_b = (real_a * twist_cos + imag_a * twist_sin).astype(jnp.bfloat16)
    imag_b = (imag_a * twist_cos - real_a * twist_sin).astype(jnp.bfloat16)
    outgoing = jnp.stack([real_b, imag_b]).reshape(2, 2, groups, per_bins, 1, per_dev, width)
    turned = lax.all_to_all(outgoing, ("seq", "fsdp"), split_axis=2, concat_axis=4, tiled=True)
    turned = turned.reshape(2, 2, per_bins, row_count, width)
    real_b = turned[0]
    imag_b = turned[1]
    real_x = (
        jnp.einsum("kqmc,mr->kqrc", real_b, last_cos, preferred_element_type=f32)
        + jnp.einsum("kqmc,mr->kqrc", imag_b, last_sin, preferred_element_type=f32)
    ).astype(jnp.bfloat16)
    imag_x = (
        jnp.einsum("kqmc,mr->kqrc", imag_b, last_cos, preferred_element_type=f32)
        - jnp.einsum("kqmc,mr->kqrc", real_b, last_sin, preferred_element_type=f32)
    ).astype(jnp.bfloat16)
    real_z, imag_z = multiply(real_x, imag_x)
    real_v = jnp.einsum("qrc,mr->qmc", real_z, last_cos, preferred_element_type=f32) - jnp.einsum(
        "qrc,mr->qmc", imag_z, last_sin, preferred_element_type=f32
    )
    imag_v = jnp.einsum("qrc,mr->qmc", imag_z, last_cos, preferred_element_type=f32) + jnp.einsum(
        "qrc,mr->qmc", real_z, last_sin, preferred_element_type=f32
    )
    row_ids, mid_ids = index_grid(per_bins, row_count)
    twist_cos, twist_sin = phase_pair(row_ids + position * per_bins, mid_ids, length)
    twist_cos = twist_cos[:, :, None]
    twist_sin = twist_sin[:, :, None]
    real_w = (real_v * twist_cos - imag_v * twist_sin).astype(jnp.bfloat16)
    imag_w = (imag_v * twist_cos + real_v * twist_sin).astype(jnp.bfloat16)
    backward = jnp.stack([real_w, imag_w]).reshape(2, 1, per_bins, groups, per_dev, width)
    returned = lax.all_to_all(backward, ("seq", "fsdp"), split_axis=3, concat_axis=1, tiled=True)
    returned = returned.reshape(2, period_rows, per_dev, width)
    conv_rows = jnp.einsum(
        "qp,qmc->pmc", first_cos, returned[0], preferred_element_type=f32
    ) - jnp.einsum("qp,qmc->pmc", first_sin, returned[1], preferred_element_type=f32)
    conv_rows = (conv_rows * scale).astype(jnp.bfloat16)
    homed = lax.all_to_all(
        conv_rows.reshape(groups, 1, per_dev, width),
        ("seq", "fsdp"),
        split_axis=0,
        concat_axis=1,
        tiled=True,
    )
    conv = homed.reshape(row_count, width)
    result = query * (conv.astype(jnp.float32) + skip_gain * product.astype(jnp.float32))
    return result.astype(jnp.bfloat16)


def wave_table(size):
    freq, time = np.meshgrid(np.arange(size), np.arange(size), indexing="ij")
    angle = ((2 * freq + 1) * time % (4 * size)) * (math.pi / (2 * size))
    return np.concatenate([np.cos(angle), np.sin(angle)], axis=0)


def exchange(value, axis):
    return lax.ppermute(value, axis, [(0, 1), (1, 0)])


def whole_specs(count):
    return [pl.BlockSpec(memory_space=pltpu.VMEM)] * count


def split_channels(summed, own_half):
    half = summed.shape[1] // 2
    low, high = (summed[:, :half], summed[:, half:])
    first = own_half == 0
    return (jnp.where(first, low, high), jnp.where(first, high, low))


def pick_rows(source, target):
    lines = lax.broadcasted_iota(jnp.int32, (HALO, HALO), 0)
    places = lax.broadcasted_iota(jnp.int32, (HALO, HALO), 1)
    wanted = (lines - target == places - source) & (places >= source) & (places < source + 2)
    return wanted.astype(F32).astype(BF16)


def pack_body(rows_ref, pack_ref):
    width = pack_ref.shape[1]
    last = rows_ref[rows_ref.shape[0] - HALO :, :]
    total = jnp.zeros((HALO, width), F32)
    for piece in range(last.shape[1] // width):
        part = last[:, piece * width : (piece + 1) * width]
        total += jnp.dot(pick_rows(HALO - 2, 2 * piece), part, preferred_element_type=F32)
    pack_ref[...] = total.astype(BF16)


def unpack_halo(pieces, count):
    parts = [
        jnp.dot(pick_rows(2 * piece, HALO - 2), pieces, preferred_element_type=F32).astype(BF16)
        for piece in range(count)
    ]
    return jnp.concatenate(parts, axis=1)


def project(rows, weight_ref, branches, keep_ref, send_ref):
    own_half = lax.axis_index("fsdp")
    half = weight_ref.shape[2] // 2
    for place, branch in enumerate(branches):
        summed = jnp.dot(rows, weight_ref[branch], preferred_element_type=F32)
        keep, send = split_channels(summed, own_half)
        lanes = slice(place * half, (place + 1) * half)
        keep_ref[:, lanes] = keep
        send_ref[:, lanes] = send.astype(BF16)


def project_first_body(
    rows_ref, cycled_ref, weight_ref, keep_product, send_product, keep_query, send_query
):
    here = lax.axis_index("chan") == lax.axis_index("fsdp")
    rows = jnp.where(here, rows_ref[...], cycled_ref[...])
    project(rows, weight_ref, (1, 2), keep_product, send_product)
    project(rows, weight_ref, (0,), keep_query, send_query)


def arrived_rows(cycled_ref, hop_ref, pack_ref, pack_hop_ref):
    here = lax.axis_index("chan") == lax.axis_index("fsdp")
    pieces = cycled_ref.shape[1] // pack_ref.shape[1]
    rows = jnp.where(here, cycled_ref[...], hop_ref[...])
    halo = unpack_halo(jnp.where(here, pack_ref[...], pack_hop_ref[...]), pieces)
    halo = jnp.where(lax.axis_index("seq") > 0, halo, jnp.zeros_like(halo))
    return jnp.concatenate([halo, rows], axis=0)


def project_product_body(
    cycled_ref, hop_ref, pack_ref, pack_hop_ref, weight_ref, keep_ref, send_ref, done_ref
):
    rows = arrived_rows(cycled_ref, hop_ref, pack_ref, pack_hop_ref)
    project(rows, weight_ref, (1, 2), keep_ref, send_ref)
    done_ref[...] = jnp.zeros_like(done_ref)


def project_query_body(
    cycled_ref, hop_ref, pack_ref, pack_hop_ref, weight_ref, first_ref, order_ref,
    own_ref, one_ref, two_ref, three_ref, keep_ref, taps_ref, send_ref, done_ref
):
    rows = arrived_rows(cycled_ref, hop_ref, pack_ref, pack_hop_ref)
    count = first_ref.shape[0]
    send_ref[:count, :] = first_ref[...]
    after_query = count + rows.shape[0]
    project(rows, weight_ref, (0,), keep_ref, send_ref.at[count:after_query, :])
    position = lax.axis_index("seq")
    first = lax.axis_index("fsdp") == 0
    _, tap_rows, half = taps_ref.shape
    for step, tap_ref in enumerate((own_ref, one_ref, two_ref, three_ref)):
        block = position ^ step
        low, high = (tap_ref[:, :half], tap_ref[:, half:])
        taps_ref[block] = jnp.where(first, low, high)
        start = pl.multiple_of(after_query + block * tap_rows, HALO)
        send_ref[pl.ds(start, tap_rows), :] = jnp.where(first, high, low)
    done_ref[...] = jnp.zeros_like(done_ref)


def after_body(*refs):
    pass


def after(value, *orders, cost_estimate=None):
    return pl.pallas_call(
        after_body,
        in_specs=whole_specs(1 + len(orders)),
        out_specs=whole_specs(1)[0],
        out_shape=shape(value.shape, value.dtype),
        input_output_aliases={0: 0},
        cost_estimate=cost_estimate,
        compiler_params=pltpu.CompilerParams(vmem_limit_bytes=32 * 1024 * 1024),
    )(value, *orders)


def taps_body(table_ref, keep_ref, got_ref, real_ref, imag_ref):
    first = lax.axis_index("fsdp") == 0
    blocks = keep_ref.shape[0]
    size = table_ref.shape[1]
    sign = 1.0 - 2.0 * (lax.broadcasted_iota(jnp.int32, (size, 1), 0) % 2).astype(F32)
    sign = sign * (1.0 / size)
    before_real = before_imag = None
    for block in range(blocks):
        start = got_ref.shape[0] - (blocks - block) * keep_ref.shape[1]
        keep, got = (keep_ref[block], got_ref[start : start + keep_ref.shape[1], :])
        taps = jnp.concatenate(
            [jnp.where(first, keep, got), jnp.where(first, got, keep)], axis=0
        )
        waves = jnp.dot(table_ref[...], taps, preferred_element_type=F32)
        real, imag = (waves[:size], -waves[size:])
        if block == 0:
            real_ref[block] = real * (1.0 / size)
            imag_ref[block] = imag * (1.0 / size)
        else:
            real_ref[block] = real * (1.0 / size) - sign * before_imag
            imag_ref[block] = imag * (1.0 / size) + sign * before_real
        before_real, before_imag = (real, imag)


def mixed_branches(branches, keep_first, keep_second, got_first, got_second, short_ref, joined):
    own = lax.axis_index("fsdp")
    rows = keep_first.shape[0]
    half = keep_second.shape[1] // len(branches)
    joined[:HALO, :] = keep_second[:HALO, :] + got_second[:HALO, :].astype(F32)
    own_start = pl.multiple_of(HALO + own * rows, HALO)
    other_start = pl.multiple_of(HALO + (1 - own) * rows, HALO)
    joined[pl.ds(own_start, rows), :] = keep_first[...] + got_second[HALO:, :].astype(F32)
    joined[pl.ds(other_start, rows), :] = keep_second[HALO:, :] + got_first[...].astype(F32)
    mixed = []
    for place, branch in enumerate(branches):
        lanes = slice(place * half, (place + 1) * half)
        total = None
        for tap in range(3):
            taps = short_ref[tap, branch : branch + 1, :]
            taps = jnp.where(own == 0, taps[:, :half], taps[:, half:])
            term = taps * joined[pl.ds(HALO - tap, 2 * rows), lanes]
            total = term if total is None else total + term
        mixed.append(total)
    return mixed


def product_body(
    keep_first, keep_second, got_first, got_second, short_ref, order_ref, product_ref, joined
):
    key, value = mixed_branches(
        (1, 2), keep_first, keep_second, got_first, got_second, short_ref, joined
    )
    product_ref[...] = (key * value).astype(BF16)


def query_body(keep_first, keep_second, got_ref, short_ref, query_ref, joined):
    rows = keep_first.shape[0]
    (query,) = mixed_branches(
        (0,), keep_first, keep_second, got_ref.at[:rows, :], got_ref.at[rows : 2 * rows + HALO, :], short_ref, joined
    )
    query_ref[...] = query


def spectrum_term(step, block_ref, real_ref, imag_ref, table_ref):
    position = lax.axis_index("seq")
    size = table_ref.shape[1]
    source = position ^ step
    back = jnp.maximum(position - source, 0)
    block = block_ref[...]
    if step:
        block = jnp.where(source < position, block, jnp.zeros_like(block))
    waves = jnp.dot(table_ref[...], block, preferred_element_type=F32)
    real, imag = (waves[:size], -waves[size:])
    tap_real, tap_imag = (real_ref[back], imag_ref[back])
    return (real * tap_real - imag * tap_imag, real * tap_imag + imag * tap_real)


def conv_early_body(own_ref, near_ref, far_ref, real_ref, imag_ref, table_ref, total_ref):
    total_ref[0], total_ref[1] = spectrum_term(0, own_ref, real_ref, imag_ref, table_ref)
    for step, block_ref in ((1, near_ref), (3, far_ref)):
        real, imag = spectrum_term(step, block_ref, real_ref, imag_ref, table_ref)
        total_ref[0] += real
        total_ref[1] += imag


def gated_rows(place, rows, stacked, turned_ref, query_ref, gain_ref, own_ref):
    half = own_ref.shape[1]
    lines = pl.ds(pl.multiple_of(place * rows, rows), rows)
    conv = jnp.dot(turned_ref[lines, :], stacked, preferred_element_type=F32)
    first = lax.axis_index("fsdp") == 0
    gain = jnp.where(first, gain_ref[:, :half], gain_ref[:, half:])
    gated = query_ref[lines, :] * (conv + gain * own_ref[lines, :].astype(F32))
    return gated.astype(BF16)


def conv_last_body(
    last_ref, total_ref, real_ref, imag_ref, table_ref, turned_ref, query_ref, gain_ref, own_ref,
    go_ref, stacked_ref
):
    real, imag = spectrum_term(2, last_ref, real_ref, imag_ref, table_ref)
    stacked = jnp.concatenate([total_ref[0] + real, -(total_ref[1] + imag)], axis=0).astype(BF16)
    stacked_ref[...] = stacked
    other = 1 - lax.axis_index("fsdp")
    go_ref[...] = gated_rows(
        other, go_ref.shape[0], stacked, turned_ref, query_ref, gain_ref, own_ref
    )


def conv_stay_body(stacked_ref, turned_ref, query_ref, gain_ref, own_ref, stay_ref):
    own = lax.axis_index("fsdp")
    stay_ref[...] = gated_rows(
        own, stay_ref.shape[0], stacked_ref[...], turned_ref, query_ref, gain_ref, own_ref
    )


def join_body(stay_ref, got_ref, out_ref):
    first = lax.axis_index("fsdp") == 0
    half = stay_ref.shape[1]
    out_ref[:, :half] = jnp.where(first, stay_ref[...], got_ref[...])
    out_ref[:, half:] = jnp.where(first, got_ref[...], stay_ref[...])


def shape(dims, kind):
    return jax.ShapeDtypeStruct(dims, kind)


def pair_mesh(tokens, proj_weight, short_weight, skip_gain, filter_taps):
    rows = tokens.shape[0]
    width = proj_weight.shape[2]
    half = width // 2
    size = 2 * rows
    blocks = lax.axis_size("seq")
    weight = jnp.transpose(proj_weight, (1, 0, 2))
    pairs = [[(s, s ^ step) for s in range(blocks)] for step in range(blocks)]
    call = functools.partial(
        pl.pallas_call, compiler_params=pltpu.CompilerParams(vmem_limit_bytes=32 * 1024 * 1024)
    )

    cycled = lax.ppermute(tokens, ("fsdp", "chan"), [(1, 3), (3, 2), (2, 0), (0, 1)])
    token = shape((8, 128), F32)
    pack = call(
        pack_body,
        cost_estimate=LONG,
        in_specs=whole_specs(1),
        out_specs=whole_specs(1)[0],
        out_shape=shape((HALO, width), BF16),
    )(tokens)
    pack_got = lax.ppermute(
        pack,
        ("seq", "fsdp", "chan"),
        [
            (4 * s + 2 * f + c, 4 * ((s + 1) % blocks) + 2 * (f ^ (1 - c)) + c)
            for s in range(blocks)
            for f in range(2)
            for c in range(2)
        ],
    )
    tap_blocks = [filter_taps] + [
        lax.ppermute(filter_taps, "seq", pairs[step]) for step in range(1, blocks)
    ]
    cycled = after(cycled, pack_got)
    hop = exchange(cycled, "chan")
    pack_hop = exchange(pack_got, "chan")
    keep_first, send_first, keep_first_query, send_first_query = call(
        project_first_body,
        cost_estimate=LONG,
        in_specs=whole_specs(3),
        out_specs=whole_specs(4),
        out_shape=(
            shape((rows, 2 * half), F32),
            shape((rows, 2 * half), BF16),
            shape((rows, half), F32),
            shape((rows, half), BF16),
        ),
    )(tokens, cycled, weight)
    got_first = exchange(send_first, "fsdp")
    arrived = (cycled, hop, pack_got, pack_hop, weight)
    keep_second, send_second, second_done = call(
        project_product_body,
        in_specs=whole_specs(5),
        out_specs=whole_specs(3),
        out_shape=(
            shape((HALO + rows, 2 * half), F32),
            shape((HALO + rows, 2 * half), BF16),
            token,
        ),
    )(*arrived)
    keep_second_query, tap_keep, send_late, late_done = call(
        project_query_body,
        in_specs=whole_specs(7 + blocks),
        out_specs=whole_specs(4),
        out_shape=(
            shape((HALO + rows, half), F32),
            shape((blocks, rows, half), BF16),
            shape((rows + HALO + rows + blocks * rows, half), BF16),
            token,
        ),
    )(*arrived, send_first_query, second_done, *tap_blocks)
    got_second = exchange(send_second, "fsdp")

    product = call(
        product_body,
        cost_estimate=LONG,
        in_specs=whole_specs(6),
        out_specs=whole_specs(1)[0],
        out_shape=shape((size, half), BF16),
        scratch_shapes=[pltpu.VMEM((HALO + size, 2 * half), F32)],
    )(keep_first, keep_second, got_first, got_second, short_weight, late_done)
    got_late = exchange(after(send_late, got_first, cost_estimate=LONG), "fsdp")
    query = call(
        query_body,
        in_specs=whole_specs(4),
        out_specs=whole_specs(1)[0],
        out_shape=shape((size, half), F32),
        scratch_shapes=[pltpu.VMEM((HALO + size, half), F32)],
    )(keep_first_query, keep_second_query, got_late, short_weight)
    last, near, far = (lax.ppermute(product, "seq", pairs[step]) for step in (2, 1, 3))
    table = wave_table(size)
    forward = jnp.asarray(table, dtype=BF16)
    inverse = jnp.asarray(table.T, dtype=BF16)
    tap_real, tap_imag = call(
        taps_body,
        in_specs=whole_specs(3),
        out_specs=whole_specs(2),
        out_shape=(shape((blocks, size, half), F32), shape((blocks, size, half), F32)),
    )(forward, tap_keep, got_late)
    total = call(
        conv_early_body,
        in_specs=whole_specs(6),
        out_specs=whole_specs(1)[0],
        out_shape=shape((2, size, half), F32),
    )(product, near, far, tap_real, tap_imag, forward)
    ending = (inverse, query, skip_gain.reshape(1, width), product)
    go, stacked = call(
        conv_last_body,
        in_specs=whole_specs(9),
        out_specs=whole_specs(2),
        out_shape=(shape((rows, half), BF16), shape((2 * size, half), BF16)),
    )(last, total, tap_real, tap_imag, forward, *ending)
    stay = call(
        conv_stay_body,
        in_specs=whole_specs(5),
        out_specs=whole_specs(1)[0],
        out_shape=shape((rows, half), BF16),
    )(stacked, *ending)
    back = exchange(go, "fsdp")
    return call(
        join_body,
        in_specs=whole_specs(2),
        out_specs=whole_specs(1)[0],
        out_shape=shape((rows, width), BF16),
    )(stay, back)


def solution(mesh):
    in_specs = (
        P(("grp", "seq", "fsdp"), "chan"),
        P("fsdp", None, "chan"),
        P(None, None, "chan"),
        P("chan"),
        P(("seq", "fsdp"), "chan"),
    )
    out_specs = P(("grp", "seq", "fsdp"), "chan")
    sizes = mesh.shape
    paired = sizes["fsdp"] == 2 and sizes["chan"] == 2 and sizes["seq"] == 4
    per_device = pair_mesh if paired else any_mesh
    return jax.shard_map(
        per_device, mesh=mesh, in_specs=in_specs, out_specs=out_specs, check_vma=False
    )
```

```python
import functools
import math

import jax
import jax.numpy as jnp
import numpy as np
from jax import lax
from jax.experimental import pallas as pl
from jax.experimental.pallas import tpu as pltpu
from jax.sharding import PartitionSpec as P

HALO = 16
LONG = pl.CostEstimate(flops=10_000_000_000, bytes_accessed=40_000_000, transcendentals=0)
F32 = jnp.float32
BF16 = jnp.bfloat16


def shifted(value, axis, steps):
    count = lax.axis_size(axis)
    initial, last = (max(0, -steps), min(count, count - steps))
    return lax.ppermute(value, axis, [(source, source + steps) for source in range(initial, last)])


def index_grid(row_count, col_count):
    return (
        lax.broadcasted_iota(jnp.int32, (row_count, col_count), 0),
        lax.broadcasted_iota(jnp.int32, (row_count, col_count), 1),
    )


def phase_pair(row_ids, col_ids, period):
    wrapped = row_ids * col_ids % period
    phase = wrapped.astype(jnp.float32) * (2.0 * math.pi / period)
    return (jnp.cos(phase), jnp.sin(phase))


def multiply(real_x, imag_x):
    sig_real = real_x[0].astype(jnp.float32)
    sig_imag = imag_x[0].astype(jnp.float32)
    tap_real = real_x[1].astype(jnp.float32)
    tap_imag = imag_x[1].astype(jnp.float32)
    real_z = (sig_real * tap_real - sig_imag * tap_imag).astype(jnp.bfloat16)
    imag_z = (sig_real * tap_imag + sig_imag * tap_real).astype(jnp.bfloat16)
    return (real_z, imag_z)


def spread(stacked, groups, inner_shape):
    shaped = stacked.reshape((2, groups, 1) + inner_shape)
    moved = lax.all_to_all(shaped, ("seq", "fsdp"), split_axis=1, concat_axis=2, tiled=True)
    return moved.reshape((2, groups) + inner_shape)


def any_mesh(tokens, proj_weight, short_weight, skip_gain, filter_taps):
    whole = lax.all_gather(tokens, "chan", axis=1, tiled=True)
    row_count = whole.shape[0]
    width = proj_weight.shape[2]
    flat_width = 3 * width
    piece = lax.all_gather(proj_weight, "fsdp", axis=0, tiled=True)
    summed = jnp.dot(
        whole, piece.reshape(piece.shape[0], flat_width), preferred_element_type=jnp.float32
    )
    projected = summed.astype(jnp.bfloat16).reshape(row_count, 3, width)
    earlier = shifted(projected[row_count - 2 :], ("seq", "fsdp"), 1)
    extended = jnp.concatenate([earlier, projected], axis=0).astype(jnp.float32)
    mixed = (
        short_weight[0] * extended[2:]
        + short_weight[1] * extended[1:-1]
        + short_weight[2] * extended[:-2]
    )
    query = mixed[:, 0]
    product = (mixed[:, 1] * mixed[:, 2]).astype(jnp.bfloat16)
    groups = lax.axis_size(("seq", "fsdp"))
    position = lax.axis_index(("seq", "fsdp"))
    period_rows = 2 * groups
    length = period_rows * row_count
    scale = 1.0 / length
    bin_ids, tap_ids = index_grid(period_rows, groups)
    first_cos, first_sin = phase_pair(bin_ids, tap_ids, period_rows)
    first_cos = first_cos.astype(jnp.bfloat16)
    first_sin = first_sin.astype(jnp.bfloat16)
    col_ids, freq_ids = index_grid(row_count, row_count)
    last_cos, last_sin = phase_pair(col_ids, freq_ids, row_count)
    last_cos = last_cos.astype(jnp.bfloat16)
    last_sin = last_sin.astype(jnp.bfloat16)
    stacked = jnp.stack([product, filter_taps])
    f32 = jnp.float32
    per_dev = row_count // groups
    per_bins = period_rows // groups
    arrived = spread(stacked.reshape(2, groups, per_dev, width), groups, (per_dev, width))
    real_a = jnp.einsum("qp,kpmc->kqmc", first_cos, arrived, preferred_element_type=f32)
    imag_a = -jnp.einsum("qp,kpmc->kqmc", first_sin, arrived, preferred_element_type=f32)
    row_ids, mid_ids = index_grid(period_rows, per_dev)
    twist_cos, twist_sin = phase_pair(row_ids, mid_ids + position * per_dev, length)
    twist_cos = twist_cos[:, :, None]
    twist_sin = twist_sin[:, :, None]
    real_b = (real_a * twist_cos + imag_a * twist_sin).astype(jnp.bfloat16)
    imag_b = (imag_a * twist_cos - real_a * twist_sin).astype(jnp.bfloat16)
    outgoing = jnp.stack([real_b, imag_b]).reshape(2, 2, groups, per_bins, 1, per_dev, width)
    turned = lax.all_to_all(outgoing, ("seq", "fsdp"), split_axis=2, concat_axis=4, tiled=True)
    turned = turned.reshape(2, 2, per_bins, row_count, width)
    real_b = turned[0]
    imag_b = turned[1]
    real_x = (
        jnp.einsum("kqmc,mr->kqrc", real_b, last_cos, preferred_element_type=f32)
        + jnp.einsum("kqmc,mr->kqrc", imag_b, last_sin, preferred_element_type=f32)
    ).astype(jnp.bfloat16)
    imag_x = (
        jnp.einsum("kqmc,mr->kqrc", imag_b, last_cos, preferred_element_type=f32)
        - jnp.einsum("kqmc,mr->kqrc", real_b, last_sin, preferred_element_type=f32)
    ).astype(jnp.bfloat16)
    real_z, imag_z = multiply(real_x, imag_x)
    real_v = jnp.einsum("qrc,mr->qmc", real_z, last_cos, preferred_element_type=f32) - jnp.einsum(
        "qrc,mr->qmc", imag_z, last_sin, preferred_element_type=f32
    )
    imag_v = jnp.einsum("qrc,mr->qmc", imag_z, last_cos, preferred_element_type=f32) + jnp.einsum(
        "qrc,mr->qmc", real_z, last_sin, preferred_element_type=f32
    )
    row_ids, mid_ids = index_grid(per_bins, row_count)
    twist_cos, twist_sin = phase_pair(row_ids + position * per_bins, mid_ids, length)
    twist_cos = twist_cos[:, :, None]
    twist_sin = twist_sin[:, :, None]
    real_w = (real_v * twist_cos - imag_v * twist_sin).astype(jnp.bfloat16)
    imag_w = (imag_v * twist_cos + real_v * twist_sin).astype(jnp.bfloat16)
    backward = jnp.stack([real_w, imag_w]).reshape(2, 1, per_bins, groups, per_dev, width)
    returned = lax.all_to_all(backward, ("seq", "fsdp"), split_axis=3, concat_axis=1, tiled=True)
    returned = returned.reshape(2, period_rows, per_dev, width)
    conv_rows = jnp.einsum(
        "qp,qmc->pmc", first_cos, returned[0], preferred_element_type=f32
    ) - jnp.einsum("qp,qmc->pmc", first_sin, returned[1], preferred_element_type=f32)
    conv_rows = (conv_rows * scale).astype(jnp.bfloat16)
    homed = lax.all_to_all(
        conv_rows.reshape(groups, 1, per_dev, width),
        ("seq", "fsdp"),
        split_axis=0,
        concat_axis=1,
        tiled=True,
    )
    conv = homed.reshape(row_count, width)
    result = query * (conv.astype(jnp.float32) + skip_gain * product.astype(jnp.float32))
    return result.astype(jnp.bfloat16)


def wave_table(size):
    freq, time = np.meshgrid(np.arange(size), np.arange(size), indexing="ij")
    angle = ((2 * freq + 1) * time % (4 * size)) * (math.pi / (2 * size))
    return np.concatenate([np.cos(angle), np.sin(angle)], axis=0)


def exchange(value, axis):
    return lax.ppermute(value, axis, [(0, 1), (1, 0)])


def whole_specs(count):
    return [pl.BlockSpec(memory_space=pltpu.VMEM)] * count


def split_channels(summed, own_half):
    half = summed.shape[1] // 2
    low, high = (summed[:, :half], summed[:, half:])
    first = own_half == 0
    return (jnp.where(first, low, high), jnp.where(first, high, low))


def pick_rows(source, target):
    lines = lax.broadcasted_iota(jnp.int32, (HALO, HALO), 0)
    places = lax.broadcasted_iota(jnp.int32, (HALO, HALO), 1)
    wanted = (lines - target == places - source) & (places >= source) & (places < source + 2)
    return wanted.astype(F32).astype(BF16)


def pack_body(rows_ref, pack_ref):
    width = pack_ref.shape[1]
    last = rows_ref[rows_ref.shape[0] - HALO :, :]
    total = jnp.zeros((HALO, width), F32)
    for piece in range(last.shape[1] // width):
        part = last[:, piece * width : (piece + 1) * width]
        total += jnp.dot(pick_rows(HALO - 2, 2 * piece), part, preferred_element_type=F32)
    pack_ref[...] = total.astype(BF16)


def unpack_halo(pieces, count):
    parts = [
        jnp.dot(pick_rows(2 * piece, HALO - 2), pieces, preferred_element_type=F32).astype(BF16)
        for piece in range(count)
    ]
    return jnp.concatenate(parts, axis=1)


def project(rows, weight_ref, branches, keep_ref, send_ref):
    own_half = lax.axis_index("fsdp")
    half = weight_ref.shape[2] // 2
    for place, branch in enumerate(branches):
        summed = jnp.dot(rows, weight_ref[branch], preferred_element_type=F32)
        keep, send = split_channels(summed, own_half)
        lanes = slice(place * half, (place + 1) * half)
        keep_ref[:, lanes] = keep
        send_ref[:, lanes] = send.astype(BF16)


def project_first_body(
    rows_ref, cycled_ref, weight_ref, keep_product, send_product, keep_query, send_query
):
    here = lax.axis_index("chan") == lax.axis_index("fsdp")
    rows = jnp.where(here, rows_ref[...], cycled_ref[...])
    project(rows, weight_ref, (1, 2), keep_product, send_product)
    project(rows, weight_ref, (0,), keep_query, send_query)


def halo_body(pack_ref, pack_hop_ref, halo_ref):
    here = lax.axis_index("chan") == lax.axis_index("fsdp")
    pieces = halo_ref.shape[1] // pack_ref.shape[1]
    halo = unpack_halo(jnp.where(here, pack_ref[...], pack_hop_ref[...]), pieces)
    halo_ref[...] = jnp.where(lax.axis_index("seq") > 0, halo, jnp.zeros_like(halo))


def arrived_rows(cycled_ref, hop_ref, halo_ref):
    here = lax.axis_index("chan") == lax.axis_index("fsdp")
    rows = jnp.where(here, cycled_ref[...], hop_ref[...])
    return jnp.concatenate([halo_ref[...], rows], axis=0)


def project_product_body(
    cycled_ref, hop_ref, halo_ref, weight_ref, keep_ref, send_ref, done_ref
):
    rows = arrived_rows(cycled_ref, hop_ref, halo_ref)
    project(rows, weight_ref, (1, 2), keep_ref, send_ref)
    done_ref[...] = jnp.zeros_like(done_ref)


def project_query_body(
    cycled_ref, hop_ref, halo_ref, weight_ref, first_ref, order_ref,
    own_ref, one_ref, two_ref, three_ref, keep_ref, taps_ref, send_ref, done_ref
):
    rows = arrived_rows(cycled_ref, hop_ref, halo_ref)
    count = first_ref.shape[0]
    send_ref[:count, :] = first_ref[...]
    after_query = count + rows.shape[0]
    project(rows, weight_ref, (0,), keep_ref, send_ref.at[count:after_query, :])
    position = lax.axis_index("seq")
    first = lax.axis_index("fsdp") == 0
    _, tap_rows, half = taps_ref.shape
    for step, tap_ref in enumerate((own_ref, one_ref, two_ref, three_ref)):
        block = position ^ step
        low, high = (tap_ref[:, :half], tap_ref[:, half:])
        taps_ref[block] = jnp.where(first, low, high)
        start = pl.multiple_of(after_query + block * tap_rows, HALO)
        send_ref[pl.ds(start, tap_rows), :] = jnp.where(first, high, low)
    done_ref[...] = jnp.zeros_like(done_ref)


def after_body(*refs):
    pass


def after(value, *orders, cost_estimate=None):
    return pl.pallas_call(
        after_body,
        in_specs=whole_specs(1 + len(orders)),
        out_specs=whole_specs(1)[0],
        out_shape=shape(value.shape, value.dtype),
        input_output_aliases={0: 0},
        cost_estimate=cost_estimate,
        compiler_params=pltpu.CompilerParams(vmem_limit_bytes=32 * 1024 * 1024),
    )(value, *orders)


def taps_body(table_ref, keep_ref, got_ref, real_ref, imag_ref):
    first = lax.axis_index("fsdp") == 0
    blocks = keep_ref.shape[0]
    size = table_ref.shape[1]
    sign = 1.0 - 2.0 * (lax.broadcasted_iota(jnp.int32, (size, 1), 0) % 2).astype(F32)
    sign = sign * (1.0 / size)
    before_real = before_imag = None
    for block in range(blocks):
        start = got_ref.shape[0] - (blocks - block) * keep_ref.shape[1]
        keep, got = (keep_ref[block], got_ref[start : start + keep_ref.shape[1], :])
        taps = jnp.concatenate(
            [jnp.where(first, keep, got), jnp.where(first, got, keep)], axis=0
        )
        waves = jnp.dot(table_ref[...], taps, preferred_element_type=F32)
        real, imag = (waves[:size], -waves[size:])
        if block == 0:
            real_ref[block] = real * (1.0 / size)
            imag_ref[block] = imag * (1.0 / size)
        else:
            real_ref[block] = real * (1.0 / size) - sign * before_imag
            imag_ref[block] = imag * (1.0 / size) + sign * before_real
        before_real, before_imag = (real, imag)


def mixed_branches(branches, keep_first, keep_second, got_first, got_second, short_ref, joined):
    own = lax.axis_index("fsdp")
    rows = keep_first.shape[0]
    half = keep_second.shape[1] // len(branches)
    joined[:HALO, :] = keep_second[:HALO, :] + got_second[:HALO, :].astype(F32)
    own_start = pl.multiple_of(HALO + own * rows, HALO)
    other_start = pl.multiple_of(HALO + (1 - own) * rows, HALO)
    joined[pl.ds(own_start, rows), :] = keep_first[...] + got_second[HALO:, :].astype(F32)
    joined[pl.ds(other_start, rows), :] = keep_second[HALO:, :] + got_first[...].astype(F32)
    mixed = []
    for place, branch in enumerate(branches):
        lanes = slice(place * half, (place + 1) * half)
        total = None
        for tap in range(3):
            taps = short_ref[tap, branch : branch + 1, :]
            taps = jnp.where(own == 0, taps[:, :half], taps[:, half:])
            term = taps * joined[pl.ds(HALO - tap, 2 * rows), lanes]
            total = term if total is None else total + term
        mixed.append(total)
    return mixed


def product_body(
    keep_first, keep_second, got_first, got_second, short_ref, order_ref, product_ref, joined
):
    key, value = mixed_branches(
        (1, 2), keep_first, keep_second, got_first, got_second, short_ref, joined
    )
    product_ref[...] = (key * value).astype(BF16)


def query_body(keep_first, keep_second, got_ref, short_ref, query_ref, joined):
    rows = keep_first.shape[0]
    got_first = got_ref.at[:rows, :]
    got_second = got_ref.at[rows : rows + keep_second.shape[0], :]
    (query,) = mixed_branches(
        (0,), keep_first, keep_second, got_first, got_second, short_ref, joined
    )
    query_ref[...] = query


def spectrum_term(step, block_ref, real_ref, imag_ref, table_ref):
    position = lax.axis_index("seq")
    size = table_ref.shape[1]
    source = position ^ step
    back = jnp.maximum(position - source, 0)
    block = block_ref[...]
    if step:
        block = jnp.where(source < position, block, jnp.zeros_like(block))
    waves = jnp.dot(table_ref[...], block, preferred_element_type=F32)
    real, imag = (waves[:size], -waves[size:])
    tap_real, tap_imag = (real_ref[back], imag_ref[back])
    return (real * tap_real - imag * tap_imag, real * tap_imag + imag * tap_real)


def conv_early_body(own_ref, near_ref, far_ref, real_ref, imag_ref, table_ref, total_ref):
    total_ref[0], total_ref[1] = spectrum_term(0, own_ref, real_ref, imag_ref, table_ref)
    for step, block_ref in ((1, near_ref), (3, far_ref)):
        real, imag = spectrum_term(step, block_ref, real_ref, imag_ref, table_ref)
        total_ref[0] += real
        total_ref[1] += imag


def gated_rows(place, rows, stacked, turned_ref, query_ref, gain_ref, own_ref):
    half = own_ref.shape[1]
    lines = pl.ds(pl.multiple_of(place * rows, rows), rows)
    conv = jnp.dot(turned_ref[lines, :], stacked, preferred_element_type=F32)
    first = lax.axis_index("fsdp") == 0
    gain = jnp.where(first, gain_ref[:, :half], gain_ref[:, half:])
    gated = query_ref[lines, :] * (conv + gain * own_ref[lines, :].astype(F32))
    return gated.astype(BF16)


def conv_last_body(
    last_ref, total_ref, real_ref, imag_ref, table_ref, turned_ref, query_ref, gain_ref, own_ref,
    go_ref, stacked_ref
):
    real, imag = spectrum_term(2, last_ref, real_ref, imag_ref, table_ref)
    stacked = jnp.concatenate([total_ref[0] + real, -(total_ref[1] + imag)], axis=0).astype(BF16)
    stacked_ref[...] = stacked
    other = 1 - lax.axis_index("fsdp")
    go_ref[...] = gated_rows(
        other, go_ref.shape[0], stacked, turned_ref, query_ref, gain_ref, own_ref
    )


def conv_stay_body(stacked_ref, turned_ref, query_ref, gain_ref, own_ref, stay_ref):
    own = lax.axis_index("fsdp")
    stay_ref[...] = gated_rows(
        own, stay_ref.shape[0], stacked_ref[...], turned_ref, query_ref, gain_ref, own_ref
    )


def join_body(stay_ref, got_ref, out_ref):
    first = lax.axis_index("fsdp") == 0
    half = stay_ref.shape[1]
    out_ref[:, :half] = jnp.where(first, stay_ref[...], got_ref[...])
    out_ref[:, half:] = jnp.where(first, got_ref[...], stay_ref[...])


def shape(dims, kind):
    return jax.ShapeDtypeStruct(dims, kind)


def pair_mesh(tokens, proj_weight, short_weight, skip_gain, filter_taps):
    rows = tokens.shape[0]
    width = proj_weight.shape[2]
    half = width // 2
    size = 2 * rows
    blocks = lax.axis_size("seq")
    weight = jnp.transpose(proj_weight, (1, 0, 2))
    pairs = [[(s, s ^ step) for s in range(blocks)] for step in range(blocks)]
    call = functools.partial(
        pl.pallas_call, compiler_params=pltpu.CompilerParams(vmem_limit_bytes=32 * 1024 * 1024)
    )

    cycled = lax.ppermute(tokens, ("fsdp", "chan"), [(1, 3), (3, 2), (2, 0), (0, 1)])
    token = shape((8, 128), F32)
    pack = call(
        pack_body,
        cost_estimate=LONG,
        in_specs=whole_specs(1),
        out_specs=whole_specs(1)[0],
        out_shape=shape((HALO, width), BF16),
    )(tokens)
    pack_got = lax.ppermute(
        pack,
        ("seq", "fsdp", "chan"),
        [
            (4 * s + 2 * f + c, 4 * ((s + 1) % blocks) + 2 * (f ^ (1 - c)) + c)
            for s in range(blocks)
            for f in range(2)
            for c in range(2)
        ],
    )
    tap_blocks = [filter_taps] + [
        lax.ppermute(filter_taps, "seq", pairs[step]) for step in range(1, blocks)
    ]
    cycled = after(cycled, pack_got)
    hop = exchange(cycled, "chan")
    pack_hop = exchange(pack_got, "chan")
    keep_first, send_first, keep_first_query, send_first_query = call(
        project_first_body,
        cost_estimate=LONG,
        in_specs=whole_specs(3),
        out_specs=whole_specs(4),
        out_shape=(
            shape((rows, 2 * half), F32),
            shape((rows, 2 * half), BF16),
            shape((rows, half), F32),
            shape((rows, half), BF16),
        ),
    )(tokens, cycled, weight)
    got_first = exchange(send_first, "fsdp")
    halo = call(
        halo_body,
        in_specs=whole_specs(2),
        out_specs=whole_specs(1)[0],
        out_shape=shape((HALO, tokens.shape[1]), BF16),
    )(pack_got, pack_hop)
    arrived = (cycled, hop, halo, weight)
    keep_second, send_second, second_done = call(
        project_product_body,
        in_specs=whole_specs(4),
        out_specs=whole_specs(3),
        out_shape=(
            shape((HALO + rows, 2 * half), F32),
            shape((HALO + rows, 2 * half), BF16),
            token,
        ),
    )(*arrived)
    keep_second_query, tap_keep, send_late, late_done = call(
        project_query_body,
        in_specs=whole_specs(6 + blocks),
        out_specs=whole_specs(4),
        out_shape=(
            shape((HALO + rows, half), F32),
            shape((blocks, rows, half), BF16),
            shape((rows + HALO + rows + blocks * rows, half), BF16),
            token,
        ),
    )(*arrived, send_first_query, second_done, *tap_blocks)
    got_second = exchange(send_second, "fsdp")

    product = call(
        product_body,
        cost_estimate=LONG,
        in_specs=whole_specs(6),
        out_specs=whole_specs(1)[0],
        out_shape=shape((size, half), BF16),
        scratch_shapes=[pltpu.VMEM((HALO + size, 2 * half), F32)],
    )(keep_first, keep_second, got_first, got_second, short_weight, late_done)
    got_late = exchange(after(send_late, got_first, cost_estimate=LONG), "fsdp")
    query = call(
        query_body,
        in_specs=whole_specs(4),
        out_specs=whole_specs(1)[0],
        out_shape=shape((size, half), F32),
        scratch_shapes=[pltpu.VMEM((HALO + size, half), F32)],
    )(keep_first_query, keep_second_query, got_late, short_weight)
    last, near, far = (lax.ppermute(product, "seq", pairs[step]) for step in (2, 1, 3))
    table = wave_table(size)
    forward = jnp.asarray(table, dtype=BF16)
    inverse = jnp.asarray(table.T, dtype=BF16)
    tap_real, tap_imag = call(
        taps_body,
        in_specs=whole_specs(3),
        out_specs=whole_specs(2),
        out_shape=(shape((blocks, size, half), F32), shape((blocks, size, half), F32)),
    )(forward, tap_keep, got_late)
    total = call(
        conv_early_body,
        in_specs=whole_specs(6),
        out_specs=whole_specs(1)[0],
        out_shape=shape((2, size, half), F32),
    )(product, near, far, tap_real, tap_imag, forward)
    ending = (inverse, query, skip_gain.reshape(1, width), product)
    go, stacked = call(
        conv_last_body,
        in_specs=whole_specs(9),
        out_specs=whole_specs(2),
        out_shape=(shape((rows, half), BF16), shape((2 * size, half), BF16)),
    )(last, total, tap_real, tap_imag, forward, *ending)
    stay = call(
        conv_stay_body,
        in_specs=whole_specs(5),
        out_specs=whole_specs(1)[0],
        out_shape=shape((rows, half), BF16),
    )(stacked, *ending)
    back = exchange(go, "fsdp")
    return call(
        join_body,
        in_specs=whole_specs(2),
        out_specs=whole_specs(1)[0],
        out_shape=shape((rows, width), BF16),
    )(stay, back)


def solution(mesh):
    in_specs = (
        P(("grp", "seq", "fsdp"), "chan"),
        P("fsdp", None, "chan"),
        P(None, None, "chan"),
        P("chan"),
        P(("seq", "fsdp"), "chan"),
    )
    out_specs = P(("grp", "seq", "fsdp"), "chan")
    sizes = mesh.shape
    paired = sizes["fsdp"] == 2 and sizes["chan"] == 2 and sizes["seq"] == 4
    per_device = pair_mesh if paired else any_mesh
    return jax.shard_map(
        per_device, mesh=mesh, in_specs=in_specs, out_specs=out_specs, check_vma=False
    )
```

```python
import functools
import math

import jax
import jax.numpy as jnp
import numpy as np
from jax import lax
from jax.experimental import pallas as pl
from jax.experimental.pallas import tpu as pltpu
from jax.sharding import PartitionSpec as P

HALO = 16
LONG = pl.CostEstimate(flops=10_000_000_000, bytes_accessed=40_000_000, transcendentals=0)
F32 = jnp.float32
BF16 = jnp.bfloat16


def shifted(value, axis, steps):
    count = lax.axis_size(axis)
    initial, last = (max(0, -steps), min(count, count - steps))
    return lax.ppermute(value, axis, [(source, source + steps) for source in range(initial, last)])


def index_grid(row_count, col_count):
    return (
        lax.broadcasted_iota(jnp.int32, (row_count, col_count), 0),
        lax.broadcasted_iota(jnp.int32, (row_count, col_count), 1),
    )


def phase_pair(row_ids, col_ids, period):
    wrapped = row_ids * col_ids % period
    phase = wrapped.astype(jnp.float32) * (2.0 * math.pi / period)
    return (jnp.cos(phase), jnp.sin(phase))


def multiply(real_x, imag_x):
    sig_real = real_x[0].astype(jnp.float32)
    sig_imag = imag_x[0].astype(jnp.float32)
    tap_real = real_x[1].astype(jnp.float32)
    tap_imag = imag_x[1].astype(jnp.float32)
    real_z = (sig_real * tap_real - sig_imag * tap_imag).astype(jnp.bfloat16)
    imag_z = (sig_real * tap_imag + sig_imag * tap_real).astype(jnp.bfloat16)
    return (real_z, imag_z)


def spread(stacked, groups, inner_shape):
    shaped = stacked.reshape((2, groups, 1) + inner_shape)
    moved = lax.all_to_all(shaped, ("seq", "fsdp"), split_axis=1, concat_axis=2, tiled=True)
    return moved.reshape((2, groups) + inner_shape)


def any_mesh(tokens, proj_weight, short_weight, skip_gain, filter_taps):
    whole = lax.all_gather(tokens, "chan", axis=1, tiled=True)
    row_count = whole.shape[0]
    width = proj_weight.shape[2]
    flat_width = 3 * width
    piece = lax.all_gather(proj_weight, "fsdp", axis=0, tiled=True)
    summed = jnp.dot(
        whole, piece.reshape(piece.shape[0], flat_width), preferred_element_type=jnp.float32
    )
    projected = summed.astype(jnp.bfloat16).reshape(row_count, 3, width)
    earlier = shifted(projected[row_count - 2 :], ("seq", "fsdp"), 1)
    extended = jnp.concatenate([earlier, projected], axis=0).astype(jnp.float32)
    mixed = (
        short_weight[0] * extended[2:]
        + short_weight[1] * extended[1:-1]
        + short_weight[2] * extended[:-2]
    )
    query = mixed[:, 0]
    product = (mixed[:, 1] * mixed[:, 2]).astype(jnp.bfloat16)
    groups = lax.axis_size(("seq", "fsdp"))
    position = lax.axis_index(("seq", "fsdp"))
    period_rows = 2 * groups
    length = period_rows * row_count
    scale = 1.0 / length
    bin_ids, tap_ids = index_grid(period_rows, groups)
    first_cos, first_sin = phase_pair(bin_ids, tap_ids, period_rows)
    first_cos = first_cos.astype(jnp.bfloat16)
    first_sin = first_sin.astype(jnp.bfloat16)
    col_ids, freq_ids = index_grid(row_count, row_count)
    last_cos, last_sin = phase_pair(col_ids, freq_ids, row_count)
    last_cos = last_cos.astype(jnp.bfloat16)
    last_sin = last_sin.astype(jnp.bfloat16)
    stacked = jnp.stack([product, filter_taps])
    f32 = jnp.float32
    per_dev = row_count // groups
    per_bins = period_rows // groups
    arrived = spread(stacked.reshape(2, groups, per_dev, width), groups, (per_dev, width))
    real_a = jnp.einsum("qp,kpmc->kqmc", first_cos, arrived, preferred_element_type=f32)
    imag_a = -jnp.einsum("qp,kpmc->kqmc", first_sin, arrived, preferred_element_type=f32)
    row_ids, mid_ids = index_grid(period_rows, per_dev)
    twist_cos, twist_sin = phase_pair(row_ids, mid_ids + position * per_dev, length)
    twist_cos = twist_cos[:, :, None]
    twist_sin = twist_sin[:, :, None]
    real_b = (real_a * twist_cos + imag_a * twist_sin).astype(jnp.bfloat16)
    imag_b = (imag_a * twist_cos - real_a * twist_sin).astype(jnp.bfloat16)
    outgoing = jnp.stack([real_b, imag_b]).reshape(2, 2, groups, per_bins, 1, per_dev, width)
    turned = lax.all_to_all(outgoing, ("seq", "fsdp"), split_axis=2, concat_axis=4, tiled=True)
    turned = turned.reshape(2, 2, per_bins, row_count, width)
    real_b = turned[0]
    imag_b = turned[1]
    real_x = (
        jnp.einsum("kqmc,mr->kqrc", real_b, last_cos, preferred_element_type=f32)
        + jnp.einsum("kqmc,mr->kqrc", imag_b, last_sin, preferred_element_type=f32)
    ).astype(jnp.bfloat16)
    imag_x = (
        jnp.einsum("kqmc,mr->kqrc", imag_b, last_cos, preferred_element_type=f32)
        - jnp.einsum("kqmc,mr->kqrc", real_b, last_sin, preferred_element_type=f32)
    ).astype(jnp.bfloat16)
    real_z, imag_z = multiply(real_x, imag_x)
    real_v = jnp.einsum("qrc,mr->qmc", real_z, last_cos, preferred_element_type=f32) - jnp.einsum(
        "qrc,mr->qmc", imag_z, last_sin, preferred_element_type=f32
    )
    imag_v = jnp.einsum("qrc,mr->qmc", imag_z, last_cos, preferred_element_type=f32) + jnp.einsum(
        "qrc,mr->qmc", real_z, last_sin, preferred_element_type=f32
    )
    row_ids, mid_ids = index_grid(per_bins, row_count)
    twist_cos, twist_sin = phase_pair(row_ids + position * per_bins, mid_ids, length)
    twist_cos = twist_cos[:, :, None]
    twist_sin = twist_sin[:, :, None]
    real_w = (real_v * twist_cos - imag_v * twist_sin).astype(jnp.bfloat16)
    imag_w = (imag_v * twist_cos + real_v * twist_sin).astype(jnp.bfloat16)
    backward = jnp.stack([real_w, imag_w]).reshape(2, 1, per_bins, groups, per_dev, width)
    returned = lax.all_to_all(backward, ("seq", "fsdp"), split_axis=3, concat_axis=1, tiled=True)
    returned = returned.reshape(2, period_rows, per_dev, width)
    conv_rows = jnp.einsum(
        "qp,qmc->pmc", first_cos, returned[0], preferred_element_type=f32
    ) - jnp.einsum("qp,qmc->pmc", first_sin, returned[1], preferred_element_type=f32)
    conv_rows = (conv_rows * scale).astype(jnp.bfloat16)
    homed = lax.all_to_all(
        conv_rows.reshape(groups, 1, per_dev, width),
        ("seq", "fsdp"),
        split_axis=0,
        concat_axis=1,
        tiled=True,
    )
    conv = homed.reshape(row_count, width)
    result = query * (conv.astype(jnp.float32) + skip_gain * product.astype(jnp.float32))
    return result.astype(jnp.bfloat16)


def wave_table(size):
    freq, time = np.meshgrid(np.arange(size), np.arange(size), indexing="ij")
    angle = ((2 * freq + 1) * time % (4 * size)) * (math.pi / (2 * size))
    return np.concatenate([np.cos(angle), np.sin(angle)], axis=0)


def exchange(value, axis):
    return lax.ppermute(value, axis, [(0, 1), (1, 0)])


def whole_specs(count):
    return [pl.BlockSpec(memory_space=pltpu.VMEM)] * count


def split_channels(summed, own_half):
    half = summed.shape[1] // 2
    low, high = (summed[:, :half], summed[:, half:])
    first = own_half == 0
    return (jnp.where(first, low, high), jnp.where(first, high, low))


def pick_rows(source, target):
    lines = lax.broadcasted_iota(jnp.int32, (HALO, HALO), 0)
    places = lax.broadcasted_iota(jnp.int32, (HALO, HALO), 1)
    wanted = (lines - target == places - source) & (places >= source) & (places < source + 2)
    return wanted.astype(F32).astype(BF16)


def pack_body(rows_ref, pack_ref):
    width = pack_ref.shape[1]
    last = rows_ref[rows_ref.shape[0] - HALO :, :]
    total = jnp.zeros((HALO, width), F32)
    for piece in range(last.shape[1] // width):
        part = last[:, piece * width : (piece + 1) * width]
        total += jnp.dot(pick_rows(HALO - 2, 2 * piece), part, preferred_element_type=F32)
    pack_ref[...] = total.astype(BF16)


def unpack_halo(pieces, count):
    parts = [
        jnp.dot(pick_rows(2 * piece, HALO - 2), pieces, preferred_element_type=F32).astype(BF16)
        for piece in range(count)
    ]
    return jnp.concatenate(parts, axis=1)


def project(rows, weight_ref, branches, keep_ref, send_ref):
    own_half = lax.axis_index("fsdp")
    half = weight_ref.shape[2] // 2
    for place, branch in enumerate(branches):
        depth = rows.shape[1] // 2
        summed = jnp.dot(rows[:, :depth], weight_ref[branch, :depth, :], preferred_element_type=F32)
        summed += jnp.dot(rows[:, depth:], weight_ref[branch, depth:, :], preferred_element_type=F32)
        keep, send = split_channels(summed, own_half)
        lanes = slice(place * half, (place + 1) * half)
        keep_ref[:, lanes] = keep
        send_ref[:, lanes] = send.astype(BF16)


def project_first_body(
    rows_ref, cycled_ref, weight_ref, keep_product, send_product, keep_query, send_query
):
    here = lax.axis_index("chan") == lax.axis_index("fsdp")
    rows = jnp.where(here, rows_ref[...], cycled_ref[...])
    project(rows, weight_ref, (1, 2), keep_product, send_product)
    project(rows, weight_ref, (0,), keep_query, send_query)


def halo_body(pack_ref, pack_hop_ref, halo_ref):
    here = lax.axis_index("chan") == lax.axis_index("fsdp")
    pieces = halo_ref.shape[1] // pack_ref.shape[1]
    halo = unpack_halo(jnp.where(here, pack_ref[...], pack_hop_ref[...]), pieces)
    halo_ref[...] = jnp.where(lax.axis_index("seq") > 0, halo, jnp.zeros_like(halo))


def arrived_rows(cycled_ref, hop_ref, halo_ref):
    here = lax.axis_index("chan") == lax.axis_index("fsdp")
    rows = jnp.where(here, cycled_ref[...], hop_ref[...])
    return jnp.concatenate([halo_ref[...], rows], axis=0)


def project_product_body(
    cycled_ref, hop_ref, halo_ref, weight_ref, keep_ref, send_ref, done_ref
):
    rows = arrived_rows(cycled_ref, hop_ref, halo_ref)
    project(rows, weight_ref, (1, 2), keep_ref, send_ref)
    done_ref[...] = jnp.zeros_like(done_ref)


def project_query_body(
    cycled_ref, hop_ref, halo_ref, weight_ref, first_ref, order_ref,
    own_ref, one_ref, two_ref, three_ref, keep_ref, taps_ref, send_ref, done_ref
):
    rows = arrived_rows(cycled_ref, hop_ref, halo_ref)
    count = first_ref.shape[0]
    send_ref[:count, :] = first_ref[...]
    after_query = count + rows.shape[0]
    project(rows, weight_ref, (0,), keep_ref, send_ref.at[count:after_query, :])
    position = lax.axis_index("seq")
    first = lax.axis_index("fsdp") == 0
    _, tap_rows, half = taps_ref.shape
    for step, tap_ref in enumerate((own_ref, one_ref, two_ref, three_ref)):
        block = position ^ step
        low, high = (tap_ref[:, :half], tap_ref[:, half:])
        taps_ref[block] = jnp.where(first, low, high)
        start = pl.multiple_of(after_query + block * tap_rows, HALO)
        send_ref[pl.ds(start, tap_rows), :] = jnp.where(first, high, low)
    done_ref[...] = jnp.zeros_like(done_ref)


def after_body(*refs):
    pass


def after(value, *orders, cost_estimate=None):
    return pl.pallas_call(
        after_body,
        in_specs=whole_specs(1 + len(orders)),
        out_specs=whole_specs(1)[0],
        out_shape=shape(value.shape, value.dtype),
        input_output_aliases={0: 0},
        cost_estimate=cost_estimate,
        compiler_params=pltpu.CompilerParams(vmem_limit_bytes=32 * 1024 * 1024),
    )(value, *orders)


def taps_body(table_ref, keep_ref, got_ref, real_ref, imag_ref):
    first = lax.axis_index("fsdp") == 0
    blocks = keep_ref.shape[0]
    size = table_ref.shape[1]
    sign = 1.0 - 2.0 * (lax.broadcasted_iota(jnp.int32, (size, 1), 0) % 2).astype(F32)
    sign = sign * (1.0 / size)
    before_real = before_imag = None
    for block in range(blocks):
        start = got_ref.shape[0] - (blocks - block) * keep_ref.shape[1]
        keep, got = (keep_ref[block], got_ref[start : start + keep_ref.shape[1], :])
        taps = jnp.concatenate(
            [jnp.where(first, keep, got), jnp.where(first, got, keep)], axis=0
        )
        waves = jnp.dot(table_ref[...], taps, preferred_element_type=F32)
        real, imag = (waves[:size], -waves[size:])
        if block == 0:
            real_ref[block] = real * (1.0 / size)
            imag_ref[block] = imag * (1.0 / size)
        else:
            real_ref[block] = real * (1.0 / size) - sign * before_imag
            imag_ref[block] = imag * (1.0 / size) + sign * before_real
        before_real, before_imag = (real, imag)


def mixed_branches(branches, keep_first, keep_second, got_first, got_second, short_ref, joined):
    own = lax.axis_index("fsdp")
    rows = keep_first.shape[0]
    half = keep_second.shape[1] // len(branches)
    joined[:HALO, :] = keep_second[:HALO, :] + got_second[:HALO, :].astype(F32)
    own_start = pl.multiple_of(HALO + own * rows, HALO)
    other_start = pl.multiple_of(HALO + (1 - own) * rows, HALO)
    joined[pl.ds(own_start, rows), :] = keep_first[...] + got_second[HALO:, :].astype(F32)
    joined[pl.ds(other_start, rows), :] = keep_second[HALO:, :] + got_first[...].astype(F32)
    mixed = []
    for place, branch in enumerate(branches):
        lanes = slice(place * half, (place + 1) * half)
        total = None
        for tap in range(3):
            taps = short_ref[tap, branch : branch + 1, :]
            taps = jnp.where(own == 0, taps[:, :half], taps[:, half:])
            term = taps * joined[pl.ds(HALO - tap, 2 * rows), lanes]
            total = term if total is None else total + term
        mixed.append(total)
    return mixed


def product_body(
    keep_first, keep_second, got_first, got_second, short_ref, order_ref, product_ref, joined
):
    key, value = mixed_branches(
        (1, 2), keep_first, keep_second, got_first, got_second, short_ref, joined
    )
    product_ref[...] = (key * value).astype(BF16)


def query_body(keep_first, keep_second, got_ref, short_ref, query_ref, joined):
    rows = keep_first.shape[0]
    got_first = got_ref.at[:rows, :]
    got_second = got_ref.at[rows : rows + keep_second.shape[0], :]
    (query,) = mixed_branches(
        (0,), keep_first, keep_second, got_first, got_second, short_ref, joined
    )
    query_ref[...] = query


def spectrum_term(step, block_ref, real_ref, imag_ref, table_ref):
    position = lax.axis_index("seq")
    size = table_ref.shape[1]
    source = position ^ step
    back = jnp.maximum(position - source, 0)
    block = block_ref[...]
    if step:
        block = jnp.where(source < position, block, jnp.zeros_like(block))
    part = size // 2
    waves = [
        jnp.dot(table_ref[start : start + part, :], block, preferred_element_type=F32)
        for start in range(0, 2 * size, part)
    ]
    real = jnp.concatenate(waves[:2], axis=0)
    imag = -jnp.concatenate(waves[2:], axis=0)
    tap_real, tap_imag = (real_ref[back], imag_ref[back])
    return (real * tap_real - imag * tap_imag, real * tap_imag + imag * tap_real)


def conv_early_body(own_ref, near_ref, far_ref, real_ref, imag_ref, table_ref, total_ref):
    total_ref[0], total_ref[1] = spectrum_term(0, own_ref, real_ref, imag_ref, table_ref)
    for step, block_ref in ((1, near_ref), (3, far_ref)):
        real, imag = spectrum_term(step, block_ref, real_ref, imag_ref, table_ref)
        total_ref[0] += real
        total_ref[1] += imag


def gated_rows(place, rows, stacked, turned_ref, query_ref, gain_ref, own_ref):
    half = own_ref.shape[1]
    lines = pl.ds(pl.multiple_of(place * rows, rows), rows)
    size = stacked.shape[0] // 2
    conv = jnp.dot(turned_ref[lines, :size], stacked[:size], preferred_element_type=F32)
    conv += jnp.dot(turned_ref[lines, size:], stacked[size:], preferred_element_type=F32)
    first = lax.axis_index("fsdp") == 0
    gain = jnp.where(first, gain_ref[:, :half], gain_ref[:, half:])
    gated = query_ref[lines, :] * (conv + gain * own_ref[lines, :].astype(F32))
    return gated.astype(BF16)


def conv_last_body(
    last_ref, total_ref, real_ref, imag_ref, table_ref, turned_ref, query_ref, gain_ref, own_ref,
    go_ref, stacked_ref
):
    real, imag = spectrum_term(2, last_ref, real_ref, imag_ref, table_ref)
    stacked = jnp.concatenate([total_ref[0] + real, -(total_ref[1] + imag)], axis=0).astype(BF16)
    stacked_ref[...] = stacked
    other = 1 - lax.axis_index("fsdp")
    go_ref[...] = gated_rows(
        other, go_ref.shape[0], stacked, turned_ref, query_ref, gain_ref, own_ref
    )


def conv_stay_body(stacked_ref, turned_ref, query_ref, gain_ref, own_ref, stay_ref):
    own = lax.axis_index("fsdp")
    stay_ref[...] = gated_rows(
        own, stay_ref.shape[0], stacked_ref[...], turned_ref, query_ref, gain_ref, own_ref
    )


def join_body(stay_ref, got_ref, out_ref):
    first = lax.axis_index("fsdp") == 0
    half = stay_ref.shape[1]
    out_ref[:, :half] = jnp.where(first, stay_ref[...], got_ref[...])
    out_ref[:, half:] = jnp.where(first, got_ref[...], stay_ref[...])


def shape(dims, kind):
    return jax.ShapeDtypeStruct(dims, kind)


def pair_mesh(tokens, proj_weight, short_weight, skip_gain, filter_taps):
    rows = tokens.shape[0]
    width = proj_weight.shape[2]
    half = width // 2
    size = 2 * rows
    blocks = lax.axis_size("seq")
    weight = jnp.transpose(proj_weight, (1, 0, 2))
    pairs = [[(s, s ^ step) for s in range(blocks)] for step in range(blocks)]
    call = functools.partial(
        pl.pallas_call, compiler_params=pltpu.CompilerParams(vmem_limit_bytes=32 * 1024 * 1024)
    )

    cycled = lax.ppermute(tokens, ("fsdp", "chan"), [(1, 3), (3, 2), (2, 0), (0, 1)])
    token = shape((8, 128), F32)
    pack = call(
        pack_body,
        cost_estimate=LONG,
        in_specs=whole_specs(1),
        out_specs=whole_specs(1)[0],
        out_shape=shape((HALO, width), BF16),
    )(tokens)
    pack_got = lax.ppermute(
        pack,
        ("seq", "fsdp", "chan"),
        [
            (4 * s + 2 * f + c, 4 * ((s + 1) % blocks) + 2 * (f ^ (1 - c)) + c)
            for s in range(blocks)
            for f in range(2)
            for c in range(2)
        ],
    )
    tap_blocks = [filter_taps] + [
        lax.ppermute(filter_taps, "seq", pairs[step]) for step in range(1, blocks)
    ]
    cycled = after(cycled, pack_got)
    hop = exchange(cycled, "chan")
    pack_hop = exchange(pack_got, "chan")
    keep_first, send_first, keep_first_query, send_first_query = call(
        project_first_body,
        cost_estimate=LONG,
        in_specs=whole_specs(3),
        out_specs=whole_specs(4),
        out_shape=(
            shape((rows, 2 * half), F32),
            shape((rows, 2 * half), BF16),
            shape((rows, half), F32),
            shape((rows, half), BF16),
        ),
    )(tokens, cycled, weight)
    got_first = exchange(send_first, "fsdp")
    halo = call(
        halo_body,
        in_specs=whole_specs(2),
        out_specs=whole_specs(1)[0],
        out_shape=shape((HALO, tokens.shape[1]), BF16),
    )(pack_got, pack_hop)
    arrived = (cycled, hop, halo, weight)
    keep_second, send_second, second_done = call(
        project_product_body,
        in_specs=whole_specs(4),
        out_specs=whole_specs(3),
        out_shape=(
            shape((HALO + rows, 2 * half), F32),
            shape((HALO + rows, 2 * half), BF16),
            token,
        ),
    )(*arrived)
    keep_second_query, tap_keep, send_late, late_done = call(
        project_query_body,
        in_specs=whole_specs(6 + blocks),
        out_specs=whole_specs(4),
        out_shape=(
            shape((HALO + rows, half), F32),
            shape((blocks, rows, half), BF16),
            shape((rows + HALO + rows + blocks * rows, half), BF16),
            token,
        ),
    )(*arrived, send_first_query, second_done, *tap_blocks)
    got_second = exchange(send_second, "fsdp")

    product = call(
        product_body,
        cost_estimate=LONG,
        in_specs=whole_specs(6),
        out_specs=whole_specs(1)[0],
        out_shape=shape((size, half), BF16),
        scratch_shapes=[pltpu.VMEM((HALO + size, 2 * half), F32)],
    )(keep_first, keep_second, got_first, got_second, short_weight, late_done)
    got_late = exchange(after(send_late, got_first, cost_estimate=LONG), "fsdp")
    query = call(
        query_body,
        in_specs=whole_specs(4),
        out_specs=whole_specs(1)[0],
        out_shape=shape((size, half), F32),
        scratch_shapes=[pltpu.VMEM((HALO + size, half), F32)],
    )(keep_first_query, keep_second_query, got_late, short_weight)
    last, near, far = (lax.ppermute(product, "seq", pairs[step]) for step in (2, 1, 3))
    table = wave_table(size)
    forward = jnp.asarray(table, dtype=BF16)
    inverse = jnp.asarray(table.T, dtype=BF16)
    tap_real, tap_imag = call(
        taps_body,
        in_specs=whole_specs(3),
        out_specs=whole_specs(2),
        out_shape=(shape((blocks, size, half), F32), shape((blocks, size, half), F32)),
    )(forward, tap_keep, got_late)
    total = call(
        conv_early_body,
        in_specs=whole_specs(6),
        out_specs=whole_specs(1)[0],
        out_shape=shape((2, size, half), F32),
    )(product, near, far, tap_real, tap_imag, forward)
    ending = (inverse, query, skip_gain.reshape(1, width), product)
    go, stacked = call(
        conv_last_body,
        in_specs=whole_specs(9),
        out_specs=whole_specs(2),
        out_shape=(shape((rows, half), BF16), shape((2 * size, half), BF16)),
    )(last, total, tap_real, tap_imag, forward, *ending)
    stay = call(
        conv_stay_body,
        in_specs=whole_specs(5),
        out_specs=whole_specs(1)[0],
        out_shape=shape((rows, half), BF16),
    )(stacked, *ending)
    back = exchange(go, "fsdp")
    return call(
        join_body,
        in_specs=whole_specs(2),
        out_specs=whole_specs(1)[0],
        out_shape=shape((rows, width), BF16),
    )(stay, back)


def solution(mesh):
    in_specs = (
        P(("grp", "seq", "fsdp"), "chan"),
        P("fsdp", None, "chan"),
        P(None, None, "chan"),
        P("chan"),
        P(("seq", "fsdp"), "chan"),
    )
    out_specs = P(("grp", "seq", "fsdp"), "chan")
    sizes = mesh.shape
    paired = sizes["fsdp"] == 2 and sizes["chan"] == 2 and sizes["seq"] == 4
    per_device = pair_mesh if paired else any_mesh
    return jax.shard_map(
        per_device, mesh=mesh, in_specs=in_specs, out_specs=out_specs, check_vma=False
    )
```

```python
import functools
import math

import jax
import jax.numpy as jnp
import numpy as np
from jax import lax
from jax.experimental import pallas as pl
from jax.experimental.pallas import tpu as pltpu
from jax.sharding import PartitionSpec as P

HALO = 16
LONG = pl.CostEstimate(flops=10_000_000_000, bytes_accessed=40_000_000, transcendentals=0)
F32 = jnp.float32
BF16 = jnp.bfloat16


def shifted(value, axis, steps):
    count = lax.axis_size(axis)
    initial, last = (max(0, -steps), min(count, count - steps))
    return lax.ppermute(value, axis, [(source, source + steps) for source in range(initial, last)])


def index_grid(row_count, col_count):
    return (
        lax.broadcasted_iota(jnp.int32, (row_count, col_count), 0),
        lax.broadcasted_iota(jnp.int32, (row_count, col_count), 1),
    )


def phase_pair(row_ids, col_ids, period):
    wrapped = row_ids * col_ids % period
    phase = wrapped.astype(jnp.float32) * (2.0 * math.pi / period)
    return (jnp.cos(phase), jnp.sin(phase))


def multiply(real_x, imag_x):
    sig_real = real_x[0].astype(jnp.float32)
    sig_imag = imag_x[0].astype(jnp.float32)
    tap_real = real_x[1].astype(jnp.float32)
    tap_imag = imag_x[1].astype(jnp.float32)
    real_z = (sig_real * tap_real - sig_imag * tap_imag).astype(jnp.bfloat16)
    imag_z = (sig_real * tap_imag + sig_imag * tap_real).astype(jnp.bfloat16)
    return (real_z, imag_z)


def spread(stacked, groups, inner_shape):
    shaped = stacked.reshape((2, groups, 1) + inner_shape)
    moved = lax.all_to_all(shaped, ("seq", "fsdp"), split_axis=1, concat_axis=2, tiled=True)
    return moved.reshape((2, groups) + inner_shape)


def any_mesh(tokens, proj_weight, short_weight, skip_gain, filter_taps):
    whole = lax.all_gather(tokens, "chan", axis=1, tiled=True)
    row_count = whole.shape[0]
    width = proj_weight.shape[2]
    flat_width = 3 * width
    piece = lax.all_gather(proj_weight, "fsdp", axis=0, tiled=True)
    summed = jnp.dot(
        whole, piece.reshape(piece.shape[0], flat_width), preferred_element_type=jnp.float32
    )
    projected = summed.astype(jnp.bfloat16).reshape(row_count, 3, width)
    earlier = shifted(projected[row_count - 2 :], ("seq", "fsdp"), 1)
    extended = jnp.concatenate([earlier, projected], axis=0).astype(jnp.float32)
    mixed = (
        short_weight[0] * extended[2:]
        + short_weight[1] * extended[1:-1]
        + short_weight[2] * extended[:-2]
    )
    query = mixed[:, 0]
    product = (mixed[:, 1] * mixed[:, 2]).astype(jnp.bfloat16)
    groups = lax.axis_size(("seq", "fsdp"))
    position = lax.axis_index(("seq", "fsdp"))
    period_rows = 2 * groups
    length = period_rows * row_count
    scale = 1.0 / length
    bin_ids, tap_ids = index_grid(period_rows, groups)
    first_cos, first_sin = phase_pair(bin_ids, tap_ids, period_rows)
    first_cos = first_cos.astype(jnp.bfloat16)
    first_sin = first_sin.astype(jnp.bfloat16)
    col_ids, freq_ids = index_grid(row_count, row_count)
    last_cos, last_sin = phase_pair(col_ids, freq_ids, row_count)
    last_cos = last_cos.astype(jnp.bfloat16)
    last_sin = last_sin.astype(jnp.bfloat16)
    stacked = jnp.stack([product, filter_taps])
    f32 = jnp.float32
    per_dev = row_count // groups
    per_bins = period_rows // groups
    arrived = spread(stacked.reshape(2, groups, per_dev, width), groups, (per_dev, width))
    real_a = jnp.einsum("qp,kpmc->kqmc", first_cos, arrived, preferred_element_type=f32)
    imag_a = -jnp.einsum("qp,kpmc->kqmc", first_sin, arrived, preferred_element_type=f32)
    row_ids, mid_ids = index_grid(period_rows, per_dev)
    twist_cos, twist_sin = phase_pair(row_ids, mid_ids + position * per_dev, length)
    twist_cos = twist_cos[:, :, None]
    twist_sin = twist_sin[:, :, None]
    real_b = (real_a * twist_cos + imag_a * twist_sin).astype(jnp.bfloat16)
    imag_b = (imag_a * twist_cos - real_a * twist_sin).astype(jnp.bfloat16)
    outgoing = jnp.stack([real_b, imag_b]).reshape(2, 2, groups, per_bins, 1, per_dev, width)
    turned = lax.all_to_all(outgoing, ("seq", "fsdp"), split_axis=2, concat_axis=4, tiled=True)
    turned = turned.reshape(2, 2, per_bins, row_count, width)
    real_b = turned[0]
    imag_b = turned[1]
    real_x = (
        jnp.einsum("kqmc,mr->kqrc", real_b, last_cos, preferred_element_type=f32)
        + jnp.einsum("kqmc,mr->kqrc", imag_b, last_sin, preferred_element_type=f32)
    ).astype(jnp.bfloat16)
    imag_x = (
        jnp.einsum("kqmc,mr->kqrc", imag_b, last_cos, preferred_element_type=f32)
        - jnp.einsum("kqmc,mr->kqrc", real_b, last_sin, preferred_element_type=f32)
    ).astype(jnp.bfloat16)
    real_z, imag_z = multiply(real_x, imag_x)
    real_v = jnp.einsum("qrc,mr->qmc", real_z, last_cos, preferred_element_type=f32) - jnp.einsum(
        "qrc,mr->qmc", imag_z, last_sin, preferred_element_type=f32
    )
    imag_v = jnp.einsum("qrc,mr->qmc", imag_z, last_cos, preferred_element_type=f32) + jnp.einsum(
        "qrc,mr->qmc", real_z, last_sin, preferred_element_type=f32
    )
    row_ids, mid_ids = index_grid(per_bins, row_count)
    twist_cos, twist_sin = phase_pair(row_ids + position * per_bins, mid_ids, length)
    twist_cos = twist_cos[:, :, None]
    twist_sin = twist_sin[:, :, None]
    real_w = (real_v * twist_cos - imag_v * twist_sin).astype(jnp.bfloat16)
    imag_w = (imag_v * twist_cos + real_v * twist_sin).astype(jnp.bfloat16)
    backward = jnp.stack([real_w, imag_w]).reshape(2, 1, per_bins, groups, per_dev, width)
    returned = lax.all_to_all(backward, ("seq", "fsdp"), split_axis=3, concat_axis=1, tiled=True)
    returned = returned.reshape(2, period_rows, per_dev, width)
    conv_rows = jnp.einsum(
        "qp,qmc->pmc", first_cos, returned[0], preferred_element_type=f32
    ) - jnp.einsum("qp,qmc->pmc", first_sin, returned[1], preferred_element_type=f32)
    conv_rows = (conv_rows * scale).astype(jnp.bfloat16)
    homed = lax.all_to_all(
        conv_rows.reshape(groups, 1, per_dev, width),
        ("seq", "fsdp"),
        split_axis=0,
        concat_axis=1,
        tiled=True,
    )
    conv = homed.reshape(row_count, width)
    result = query * (conv.astype(jnp.float32) + skip_gain * product.astype(jnp.float32))
    return result.astype(jnp.bfloat16)


def wave_table(size):
    freq, time = np.meshgrid(np.arange(size), np.arange(size), indexing="ij")
    angle = ((2 * freq + 1) * time % (4 * size)) * (math.pi / (2 * size))
    return np.concatenate([np.cos(angle), np.sin(angle)], axis=0)


def exchange(value, axis):
    return lax.ppermute(value, axis, [(0, 1), (1, 0)])


def whole_specs(count):
    return [pl.BlockSpec(memory_space=pltpu.VMEM)] * count


def split_channels(summed, own_half):
    half = summed.shape[1] // 2
    low, high = (summed[:, :half], summed[:, half:])
    first = own_half == 0
    return (jnp.where(first, low, high), jnp.where(first, high, low))


def pick_rows(source, target):
    lines = lax.broadcasted_iota(jnp.int32, (HALO, HALO), 0)
    places = lax.broadcasted_iota(jnp.int32, (HALO, HALO), 1)
    wanted = (lines - target == places - source) & (places >= source) & (places < source + 2)
    return wanted.astype(F32).astype(BF16)


def pack_body(rows_ref, pack_ref):
    width = pack_ref.shape[1]
    last = rows_ref[rows_ref.shape[0] - HALO :, :]
    total = jnp.zeros((HALO, width), F32)
    for piece in range(last.shape[1] // width):
        part = last[:, piece * width : (piece + 1) * width]
        total += jnp.dot(pick_rows(HALO - 2, 2 * piece), part, preferred_element_type=F32)
    pack_ref[...] = total.astype(BF16)


def unpack_halo(pieces, count):
    parts = [
        jnp.dot(pick_rows(2 * piece, HALO - 2), pieces, preferred_element_type=F32).astype(BF16)
        for piece in range(count)
    ]
    return jnp.concatenate(parts, axis=1)


def project(rows, weight_ref, branches, keep_ref, send_ref):
    own_half = lax.axis_index("fsdp")
    half = weight_ref.shape[2] // 2
    for place, branch in enumerate(branches):
        summed = jnp.dot(rows, weight_ref[branch], preferred_element_type=F32)
        keep, send = split_channels(summed, own_half)
        lanes = slice(place * half, (place + 1) * half)
        keep_ref[:, lanes] = keep
        send_ref[:, lanes] = send.astype(BF16)


def project_first_body(rows_ref, cycled_ref, weight_ref, keep_ref, send_ref):
    here = lax.axis_index("chan") == lax.axis_index("fsdp")
    rows = jnp.where(here, rows_ref[...], cycled_ref[...])
    project(rows, weight_ref, (1, 2), keep_ref, send_ref)


def halo_body(pack_ref, pack_hop_ref, halo_ref):
    here = lax.axis_index("chan") == lax.axis_index("fsdp")
    pieces = halo_ref.shape[1] // pack_ref.shape[1]
    halo = unpack_halo(jnp.where(here, pack_ref[...], pack_hop_ref[...]), pieces)
    halo_ref[...] = jnp.where(lax.axis_index("seq") > 0, halo, jnp.zeros_like(halo))


def arrived_rows(cycled_ref, hop_ref, halo_ref):
    here = lax.axis_index("chan") == lax.axis_index("fsdp")
    rows = jnp.where(here, cycled_ref[...], hop_ref[...])
    return jnp.concatenate([halo_ref[...], rows], axis=0)


def project_product_body(
    cycled_ref, hop_ref, halo_ref, weight_ref, keep_ref, send_ref, done_ref
):
    rows = arrived_rows(cycled_ref, hop_ref, halo_ref)
    project(rows, weight_ref, (1, 2), keep_ref, send_ref)
    done_ref[...] = jnp.zeros_like(done_ref)


def project_query_body(
    cycled_ref, hop_ref, halo_ref, weight_ref, rows_ref, order_ref,
    own_ref, one_ref, two_ref, three_ref, keep_ref, taps_ref, send_ref, done_ref
):
    here = lax.axis_index("chan") == lax.axis_index("fsdp")
    own = jnp.where(here, rows_ref[...], cycled_ref[...])
    rows = jnp.concatenate([own, arrived_rows(cycled_ref, hop_ref, halo_ref)], axis=0)
    after_query = rows.shape[0]
    project(rows, weight_ref, (0,), keep_ref, send_ref.at[:after_query, :])
    position = lax.axis_index("seq")
    first = lax.axis_index("fsdp") == 0
    _, tap_rows, half = taps_ref.shape
    for step, tap_ref in enumerate((own_ref, one_ref, two_ref, three_ref)):
        block = position ^ step
        low, high = (tap_ref[:, :half], tap_ref[:, half:])
        taps_ref[block] = jnp.where(first, low, high)
        start = pl.multiple_of(after_query + block * tap_rows, HALO)
        send_ref[pl.ds(start, tap_rows), :] = jnp.where(first, high, low)
    done_ref[...] = jnp.zeros_like(done_ref)


def after_body(*refs):
    pass


def after(value, *orders, cost_estimate=None):
    return pl.pallas_call(
        after_body,
        in_specs=whole_specs(1 + len(orders)),
        out_specs=whole_specs(1)[0],
        out_shape=shape(value.shape, value.dtype),
        input_output_aliases={0: 0},
        cost_estimate=cost_estimate,
        compiler_params=pltpu.CompilerParams(vmem_limit_bytes=32 * 1024 * 1024),
    )(value, *orders)


def taps_body(table_ref, keep_ref, got_ref, real_ref, imag_ref):
    first = lax.axis_index("fsdp") == 0
    blocks = keep_ref.shape[0]
    size = table_ref.shape[1]
    sign = 1.0 - 2.0 * (lax.broadcasted_iota(jnp.int32, (size, 1), 0) % 2).astype(F32)
    sign = sign * (1.0 / size)
    before_real = before_imag = None
    for block in range(blocks):
        start = got_ref.shape[0] - (blocks - block) * keep_ref.shape[1]
        keep, got = (keep_ref[block], got_ref[start : start + keep_ref.shape[1], :])
        taps = jnp.concatenate(
            [jnp.where(first, keep, got), jnp.where(first, got, keep)], axis=0
        )
        waves = jnp.dot(table_ref[...], taps, preferred_element_type=F32)
        real, imag = (waves[:size], -waves[size:])
        if block == 0:
            real_ref[block] = real * (1.0 / size)
            imag_ref[block] = imag * (1.0 / size)
        else:
            real_ref[block] = real * (1.0 / size) - sign * before_imag
            imag_ref[block] = imag * (1.0 / size) + sign * before_real
        before_real, before_imag = (real, imag)


def mixed_branches(branches, keep_first, keep_second, got_first, got_second, short_ref, joined):
    own = lax.axis_index("fsdp")
    rows = keep_first.shape[0]
    half = keep_second.shape[1] // len(branches)
    joined[:HALO, :] = keep_second[:HALO, :] + got_second[:HALO, :].astype(F32)
    own_start = pl.multiple_of(HALO + own * rows, HALO)
    other_start = pl.multiple_of(HALO + (1 - own) * rows, HALO)
    joined[pl.ds(own_start, rows), :] = keep_first[...] + got_second[HALO:, :].astype(F32)
    joined[pl.ds(other_start, rows), :] = keep_second[HALO:, :] + got_first[...].astype(F32)
    mixed = []
    for place, branch in enumerate(branches):
        lanes = slice(place * half, (place + 1) * half)
        total = None
        for tap in range(3):
            taps = short_ref[tap, branch : branch + 1, :]
            taps = jnp.where(own == 0, taps[:, :half], taps[:, half:])
            term = taps * joined[pl.ds(HALO - tap, 2 * rows), lanes]
            total = term if total is None else total + term
        mixed.append(total)
    return mixed


def product_body(
    keep_first, keep_second, got_first, got_second, short_ref, order_ref, product_ref, joined
):
    key, value = mixed_branches(
        (1, 2), keep_first, keep_second, got_first, got_second, short_ref, joined
    )
    product_ref[...] = (key * value).astype(BF16)


def query_body(keep_ref, got_ref, short_ref, query_ref, joined):
    rows = (keep_ref.shape[0] - HALO) // 2
    first, second = (pl.ds(0, rows), pl.ds(rows, HALO + rows))
    (query,) = mixed_branches(
        (0,),
        keep_ref.at[first, :],
        keep_ref.at[second, :],
        got_ref.at[first, :],
        got_ref.at[second, :],
        short_ref,
        joined,
    )
    query_ref[...] = query


def spectrum_term(step, block_ref, real_ref, imag_ref, table_ref):
    position = lax.axis_index("seq")
    size = table_ref.shape[1]
    source = position ^ step
    back = jnp.maximum(position - source, 0)
    block = block_ref[...]
    if step:
        block = jnp.where(source < position, block, jnp.zeros_like(block))
    waves = jnp.dot(table_ref[...], block, preferred_element_type=F32)
    real, imag = (waves[:size], -waves[size:])
    tap_real, tap_imag = (real_ref[back], imag_ref[back])
    return (real * tap_real - imag * tap_imag, real * tap_imag + imag * tap_real)


def conv_early_body(own_ref, far_ref, near_ref, real_ref, imag_ref, table_ref, total_ref):
    total_ref[0], total_ref[1] = spectrum_term(0, own_ref, real_ref, imag_ref, table_ref)
    for step, block_ref in ((3, far_ref), (1, near_ref)):
        real, imag = spectrum_term(step, block_ref, real_ref, imag_ref, table_ref)
        total_ref[0] += real
        total_ref[1] += imag


def gated_rows(place, rows, stacked, turned_ref, query_ref, gain_ref, own_ref):
    half = own_ref.shape[1]
    lines = pl.ds(pl.multiple_of(place * rows, rows), rows)
    conv = jnp.dot(turned_ref[lines, :], stacked, preferred_element_type=F32)
    first = lax.axis_index("fsdp") == 0
    gain = jnp.where(first, gain_ref[:, :half], gain_ref[:, half:])
    gated = query_ref[lines, :] * (conv + gain * own_ref[lines, :].astype(F32))
    return gated.astype(BF16)


def conv_last_body(
    last_ref, total_ref, real_ref, imag_ref, table_ref, turned_ref, query_ref, gain_ref, own_ref,
    go_ref, stacked_ref
):
    real, imag = spectrum_term(2, last_ref, real_ref, imag_ref, table_ref)
    stacked = jnp.concatenate([total_ref[0] + real, -(total_ref[1] + imag)], axis=0).astype(BF16)
    stacked_ref[...] = stacked
    other = 1 - lax.axis_index("fsdp")
    go_ref[...] = gated_rows(
        other, go_ref.shape[0], stacked, turned_ref, query_ref, gain_ref, own_ref
    )


def conv_stay_body(stacked_ref, turned_ref, query_ref, gain_ref, own_ref, stay_ref):
    own = lax.axis_index("fsdp")
    stay_ref[...] = gated_rows(
        own, stay_ref.shape[0], stacked_ref[...], turned_ref, query_ref, gain_ref, own_ref
    )


def join_body(stay_ref, got_ref, out_ref):
    first = lax.axis_index("fsdp") == 0
    half = stay_ref.shape[1]
    out_ref[:, :half] = jnp.where(first, stay_ref[...], got_ref[...])
    out_ref[:, half:] = jnp.where(first, got_ref[...], stay_ref[...])


def shape(dims, kind):
    return jax.ShapeDtypeStruct(dims, kind)


def pair_mesh(tokens, proj_weight, short_weight, skip_gain, filter_taps):
    rows = tokens.shape[0]
    width = proj_weight.shape[2]
    half = width // 2
    size = 2 * rows
    blocks = lax.axis_size("seq")
    weight = jnp.transpose(proj_weight, (1, 0, 2))
    pairs = [[(s, s ^ step) for s in range(blocks)] for step in range(blocks)]
    call = functools.partial(
        pl.pallas_call, compiler_params=pltpu.CompilerParams(vmem_limit_bytes=32 * 1024 * 1024)
    )

    cycled = lax.ppermute(tokens, ("fsdp", "chan"), [(1, 3), (3, 2), (2, 0), (0, 1)])
    token = shape((8, 128), F32)
    pack = call(
        pack_body,
        cost_estimate=LONG,
        in_specs=whole_specs(1),
        out_specs=whole_specs(1)[0],
        out_shape=shape((HALO, width), BF16),
    )(tokens)
    pack_got = lax.ppermute(
        pack,
        ("seq", "fsdp", "chan"),
        [
            (4 * s + 2 * f + c, 4 * ((s + 1) % blocks) + 2 * (f ^ (1 - c)) + c)
            for s in range(blocks)
            for f in range(2)
            for c in range(2)
        ],
    )
    tap_blocks = [filter_taps] + [
        lax.ppermute(filter_taps, "seq", pairs[step]) for step in range(1, blocks)
    ]
    cycled = after(cycled, pack_got)
    hop = exchange(cycled, "chan")
    pack_hop = exchange(pack_got, "chan")
    keep_first, send_first = call(
        project_first_body,
        cost_estimate=LONG,
        in_specs=whole_specs(3),
        out_specs=whole_specs(2),
        out_shape=(shape((rows, 2 * half), F32), shape((rows, 2 * half), BF16)),
    )(tokens, cycled, weight)
    got_first = exchange(send_first, "fsdp")
    halo = call(
        halo_body,
        in_specs=whole_specs(2),
        out_specs=whole_specs(1)[0],
        out_shape=shape((HALO, tokens.shape[1]), BF16),
    )(pack_got, pack_hop)
    arrived = (cycled, hop, halo, weight)
    keep_second, send_second, second_done = call(
        project_product_body,
        in_specs=whole_specs(4),
        out_specs=whole_specs(3),
        out_shape=(
            shape((HALO + rows, 2 * half), F32),
            shape((HALO + rows, 2 * half), BF16),
            token,
        ),
    )(*arrived)
    keep_query, tap_keep, send_late, late_done = call(
        project_query_body,
        in_specs=whole_specs(6 + blocks),
        out_specs=whole_specs(4),
        out_shape=(
            shape((rows + HALO + rows, half), F32),
            shape((blocks, rows, half), BF16),
            shape((rows + HALO + rows + blocks * rows, half), BF16),
            token,
        ),
    )(*arrived, tokens, second_done, *tap_blocks)
    got_second = exchange(send_second, "fsdp")

    product = call(
        product_body,
        cost_estimate=LONG,
        in_specs=whole_specs(6),
        out_specs=whole_specs(1)[0],
        out_shape=shape((size, half), BF16),
        scratch_shapes=[pltpu.VMEM((HALO + size, 2 * half), F32)],
    )(keep_first, keep_second, got_first, got_second, short_weight, late_done)
    got_late = exchange(after(send_late, got_first, cost_estimate=LONG), "fsdp")
    query = call(
        query_body,
        in_specs=whole_specs(3),
        out_specs=whole_specs(1)[0],
        out_shape=shape((size, half), F32),
        scratch_shapes=[pltpu.VMEM((HALO + size, half), F32)],
    )(keep_query, got_late, short_weight)
    last, far, near = (lax.ppermute(product, "seq", pairs[step]) for step in (2, 3, 1))
    table = wave_table(size)
    forward = jnp.asarray(table, dtype=BF16)
    inverse = jnp.asarray(table.T, dtype=BF16)
    tap_real, tap_imag = call(
        taps_body,
        in_specs=whole_specs(3),
        out_specs=whole_specs(2),
        out_shape=(shape((blocks, size, half), F32), shape((blocks, size, half), F32)),
    )(forward, tap_keep, got_late)
    total = call(
        conv_early_body,
        in_specs=whole_specs(6),
        out_specs=whole_specs(1)[0],
        out_shape=shape((2, size, half), F32),
    )(product, far, near, tap_real, tap_imag, forward)
    ending = (inverse, query, skip_gain.reshape(1, width), product)
    go, stacked = call(
        conv_last_body,
        in_specs=whole_specs(9),
        out_specs=whole_specs(2),
        out_shape=(shape((rows, half), BF16), shape((2 * size, half), BF16)),
    )(last, total, tap_real, tap_imag, forward, *ending)
    stay = call(
        conv_stay_body,
        in_specs=whole_specs(5),
        out_specs=whole_specs(1)[0],
        out_shape=shape((rows, half), BF16),
    )(stacked, *ending)
    back = exchange(go, "fsdp")
    return call(
        join_body,
        in_specs=whole_specs(2),
        out_specs=whole_specs(1)[0],
        out_shape=shape((rows, width), BF16),
    )(stay, back)


def solution(mesh):
    in_specs = (
        P(("grp", "seq", "fsdp"), "chan"),
        P("fsdp", None, "chan"),
        P(None, None, "chan"),
        P("chan"),
        P(("seq", "fsdp"), "chan"),
    )
    out_specs = P(("grp", "seq", "fsdp"), "chan")
    sizes = mesh.shape
    paired = sizes["fsdp"] == 2 and sizes["chan"] == 2 and sizes["seq"] == 4
    per_device = pair_mesh if paired else any_mesh
    return jax.shard_map(
        per_device, mesh=mesh, in_specs=in_specs, out_specs=out_specs, check_vma=False
    )
```

```python
import functools
import math

import jax
import jax.numpy as jnp
import numpy as np
from jax import lax
from jax.experimental import pallas as pl
from jax.experimental.pallas import tpu as pltpu
from jax.sharding import PartitionSpec as P

HALO = 16
LONG = pl.CostEstimate(flops=10_000_000_000, bytes_accessed=40_000_000, transcendentals=0)
F32 = jnp.float32
BF16 = jnp.bfloat16


def shifted(value, axis, steps):
    count = lax.axis_size(axis)
    initial, last = (max(0, -steps), min(count, count - steps))
    return lax.ppermute(value, axis, [(source, source + steps) for source in range(initial, last)])


def index_grid(row_count, col_count):
    return (
        lax.broadcasted_iota(jnp.int32, (row_count, col_count), 0),
        lax.broadcasted_iota(jnp.int32, (row_count, col_count), 1),
    )


def phase_pair(row_ids, col_ids, period):
    wrapped = row_ids * col_ids % period
    phase = wrapped.astype(jnp.float32) * (2.0 * math.pi / period)
    return (jnp.cos(phase), jnp.sin(phase))


def multiply(real_x, imag_x):
    sig_real = real_x[0].astype(jnp.float32)
    sig_imag = imag_x[0].astype(jnp.float32)
    tap_real = real_x[1].astype(jnp.float32)
    tap_imag = imag_x[1].astype(jnp.float32)
    real_z = (sig_real * tap_real - sig_imag * tap_imag).astype(jnp.bfloat16)
    imag_z = (sig_real * tap_imag + sig_imag * tap_real).astype(jnp.bfloat16)
    return (real_z, imag_z)


def spread(stacked, groups, inner_shape):
    shaped = stacked.reshape((2, groups, 1) + inner_shape)
    moved = lax.all_to_all(shaped, ("seq", "fsdp"), split_axis=1, concat_axis=2, tiled=True)
    return moved.reshape((2, groups) + inner_shape)


def any_mesh(tokens, proj_weight, short_weight, skip_gain, filter_taps):
    whole = lax.all_gather(tokens, "chan", axis=1, tiled=True)
    row_count = whole.shape[0]
    width = proj_weight.shape[2]
    flat_width = 3 * width
    piece = lax.all_gather(proj_weight, "fsdp", axis=0, tiled=True)
    summed = jnp.dot(
        whole, piece.reshape(piece.shape[0], flat_width), preferred_element_type=jnp.float32
    )
    projected = summed.astype(jnp.bfloat16).reshape(row_count, 3, width)
    earlier = shifted(projected[row_count - 2 :], ("seq", "fsdp"), 1)
    extended = jnp.concatenate([earlier, projected], axis=0).astype(jnp.float32)
    mixed = (
        short_weight[0] * extended[2:]
        + short_weight[1] * extended[1:-1]
        + short_weight[2] * extended[:-2]
    )
    query = mixed[:, 0]
    product = (mixed[:, 1] * mixed[:, 2]).astype(jnp.bfloat16)
    groups = lax.axis_size(("seq", "fsdp"))
    position = lax.axis_index(("seq", "fsdp"))
    period_rows = 2 * groups
    length = period_rows * row_count
    scale = 1.0 / length
    bin_ids, tap_ids = index_grid(period_rows, groups)
    first_cos, first_sin = phase_pair(bin_ids, tap_ids, period_rows)
    first_cos = first_cos.astype(jnp.bfloat16)
    first_sin = first_sin.astype(jnp.bfloat16)
    col_ids, freq_ids = index_grid(row_count, row_count)
    last_cos, last_sin = phase_pair(col_ids, freq_ids, row_count)
    last_cos = last_cos.astype(jnp.bfloat16)
    last_sin = last_sin.astype(jnp.bfloat16)
    stacked = jnp.stack([product, filter_taps])
    f32 = jnp.float32
    per_dev = row_count // groups
    per_bins = period_rows // groups
    arrived = spread(stacked.reshape(2, groups, per_dev, width), groups, (per_dev, width))
    real_a = jnp.einsum("qp,kpmc->kqmc", first_cos, arrived, preferred_element_type=f32)
    imag_a = -jnp.einsum("qp,kpmc->kqmc", first_sin, arrived, preferred_element_type=f32)
    row_ids, mid_ids = index_grid(period_rows, per_dev)
    twist_cos, twist_sin = phase_pair(row_ids, mid_ids + position * per_dev, length)
    twist_cos = twist_cos[:, :, None]
    twist_sin = twist_sin[:, :, None]
    real_b = (real_a * twist_cos + imag_a * twist_sin).astype(jnp.bfloat16)
    imag_b = (imag_a * twist_cos - real_a * twist_sin).astype(jnp.bfloat16)
    outgoing = jnp.stack([real_b, imag_b]).reshape(2, 2, groups, per_bins, 1, per_dev, width)
    turned = lax.all_to_all(outgoing, ("seq", "fsdp"), split_axis=2, concat_axis=4, tiled=True)
    turned = turned.reshape(2, 2, per_bins, row_count, width)
    real_b = turned[0]
    imag_b = turned[1]
    real_x = (
        jnp.einsum("kqmc,mr->kqrc", real_b, last_cos, preferred_element_type=f32)
        + jnp.einsum("kqmc,mr->kqrc", imag_b, last_sin, preferred_element_type=f32)
    ).astype(jnp.bfloat16)
    imag_x = (
        jnp.einsum("kqmc,mr->kqrc", imag_b, last_cos, preferred_element_type=f32)
        - jnp.einsum("kqmc,mr->kqrc", real_b, last_sin, preferred_element_type=f32)
    ).astype(jnp.bfloat16)
    real_z, imag_z = multiply(real_x, imag_x)
    real_v = jnp.einsum("qrc,mr->qmc", real_z, last_cos, preferred_element_type=f32) - jnp.einsum(
        "qrc,mr->qmc", imag_z, last_sin, preferred_element_type=f32
    )
    imag_v = jnp.einsum("qrc,mr->qmc", imag_z, last_cos, preferred_element_type=f32) + jnp.einsum(
        "qrc,mr->qmc", real_z, last_sin, preferred_element_type=f32
    )
    row_ids, mid_ids = index_grid(per_bins, row_count)
    twist_cos, twist_sin = phase_pair(row_ids + position * per_bins, mid_ids, length)
    twist_cos = twist_cos[:, :, None]
    twist_sin = twist_sin[:, :, None]
    real_w = (real_v * twist_cos - imag_v * twist_sin).astype(jnp.bfloat16)
    imag_w = (imag_v * twist_cos + real_v * twist_sin).astype(jnp.bfloat16)
    backward = jnp.stack([real_w, imag_w]).reshape(2, 1, per_bins, groups, per_dev, width)
    returned = lax.all_to_all(backward, ("seq", "fsdp"), split_axis=3, concat_axis=1, tiled=True)
    returned = returned.reshape(2, period_rows, per_dev, width)
    conv_rows = jnp.einsum(
        "qp,qmc->pmc", first_cos, returned[0], preferred_element_type=f32
    ) - jnp.einsum("qp,qmc->pmc", first_sin, returned[1], preferred_element_type=f32)
    conv_rows = (conv_rows * scale).astype(jnp.bfloat16)
    homed = lax.all_to_all(
        conv_rows.reshape(groups, 1, per_dev, width),
        ("seq", "fsdp"),
        split_axis=0,
        concat_axis=1,
        tiled=True,
    )
    conv = homed.reshape(row_count, width)
    result = query * (conv.astype(jnp.float32) + skip_gain * product.astype(jnp.float32))
    return result.astype(jnp.bfloat16)


def wave_table(size):
    freq, time = np.meshgrid(np.arange(size), np.arange(size), indexing="ij")
    angle = ((2 * freq + 1) * time % (4 * size)) * (math.pi / (2 * size))
    return np.concatenate([np.cos(angle), np.sin(angle)], axis=0)


def exchange(value, axis):
    return lax.ppermute(value, axis, [(0, 1), (1, 0)])


def whole_specs(count):
    return [pl.BlockSpec(memory_space=pltpu.VMEM)] * count


def split_channels(summed, own_half):
    half = summed.shape[1] // 2
    low, high = (summed[:, :half], summed[:, half:])
    first = own_half == 0
    return (jnp.where(first, low, high), jnp.where(first, high, low))


def pick_rows(source, target):
    lines = lax.broadcasted_iota(jnp.int32, (HALO, HALO), 0)
    places = lax.broadcasted_iota(jnp.int32, (HALO, HALO), 1)
    wanted = (lines - target == places - source) & (places >= source) & (places < source + 2)
    return wanted.astype(F32).astype(BF16)


def pack_body(rows_ref, pack_ref):
    width = pack_ref.shape[1]
    last = rows_ref[rows_ref.shape[0] - HALO :, :]
    total = jnp.zeros((HALO, width), F32)
    for piece in range(last.shape[1] // width):
        part = last[:, piece * width : (piece + 1) * width]
        total += jnp.dot(pick_rows(HALO - 2, 2 * piece), part, preferred_element_type=F32)
    pack_ref[...] = total.astype(BF16)


def unpack_halo(pieces, count):
    parts = [
        jnp.dot(pick_rows(2 * piece, HALO - 2), pieces, preferred_element_type=F32).astype(BF16)
        for piece in range(count)
    ]
    return jnp.concatenate(parts, axis=1)


def project(rows, weight_ref, branches, keep_ref, send_ref):
    own_half = lax.axis_index("fsdp")
    half = weight_ref.shape[2] // 2
    for place, branch in enumerate(branches):
        summed = jnp.dot(rows, weight_ref[branch], preferred_element_type=F32)
        keep, send = split_channels(summed, own_half)
        lanes = slice(place * half, (place + 1) * half)
        keep_ref[:, lanes] = keep
        send_ref[:, lanes] = send.astype(BF16)


def project_first_body(
    rows_ref, cycled_ref, weight_ref, keep_product, send_product, keep_query, send_query
):
    here = lax.axis_index("chan") == lax.axis_index("fsdp")
    rows = jnp.where(here, rows_ref[...], cycled_ref[...])
    project(rows, weight_ref, (1, 2), keep_product, send_product)
    project(rows, weight_ref, (0,), keep_query, send_query)


def halo_body(pack_ref, pack_hop_ref, halo_ref):
    here = lax.axis_index("chan") == lax.axis_index("fsdp")
    pieces = halo_ref.shape[1] // pack_ref.shape[1]
    halo = unpack_halo(jnp.where(here, pack_ref[...], pack_hop_ref[...]), pieces)
    halo_ref[...] = jnp.where(lax.axis_index("seq") > 0, halo, jnp.zeros_like(halo))


def arrived_rows(cycled_ref, hop_ref, halo_ref):
    here = lax.axis_index("chan") == lax.axis_index("fsdp")
    rows = jnp.where(here, cycled_ref[...], hop_ref[...])
    return jnp.concatenate([halo_ref[...], rows], axis=0)


def project_product_body(
    cycled_ref, hop_ref, halo_ref, weight_ref, keep_ref, send_ref, done_ref
):
    rows = arrived_rows(cycled_ref, hop_ref, halo_ref)
    project(rows, weight_ref, (1, 2), keep_ref, send_ref)
    done_ref[...] = jnp.zeros_like(done_ref)


def project_query_body(
    cycled_ref, hop_ref, halo_ref, weight_ref, first_ref, order_ref,
    own_ref, one_ref, two_ref, three_ref, keep_ref, taps_ref, send_ref, done_ref
):
    rows = arrived_rows(cycled_ref, hop_ref, halo_ref)
    count = first_ref.shape[0]
    send_ref[:count, :] = first_ref[...]
    after_query = count + rows.shape[0]
    project(rows, weight_ref, (0,), keep_ref, send_ref.at[count:after_query, :])
    position = lax.axis_index("seq")
    first = lax.axis_index("fsdp") == 0
    _, tap_rows, half = taps_ref.shape
    for step, tap_ref in enumerate((own_ref, one_ref, two_ref, three_ref)):
        block = position ^ step
        low, high = (tap_ref[:, :half], tap_ref[:, half:])
        taps_ref[block] = jnp.where(first, low, high)
        start = pl.multiple_of(after_query + block * tap_rows, HALO)
        send_ref[pl.ds(start, tap_rows), :] = jnp.where(first, high, low)
    done_ref[...] = jnp.zeros_like(done_ref)


def after_body(*refs):
    pass


def after(value, *orders, cost_estimate=None):
    return pl.pallas_call(
        after_body,
        in_specs=whole_specs(1 + len(orders)),
        out_specs=whole_specs(1)[0],
        out_shape=shape(value.shape, value.dtype),
        input_output_aliases={0: 0},
        cost_estimate=cost_estimate,
        compiler_params=pltpu.CompilerParams(vmem_limit_bytes=32 * 1024 * 1024),
    )(value, *orders)


def taps_body(table_ref, keep_ref, got_ref, real_ref, imag_ref):
    first = lax.axis_index("fsdp") == 0
    blocks = keep_ref.shape[0]
    size = table_ref.shape[1]
    sign = 1.0 - 2.0 * (lax.broadcasted_iota(jnp.int32, (size, 1), 0) % 2).astype(F32)
    sign = sign * (1.0 / size)
    before_real = before_imag = None
    for block in range(blocks):
        start = got_ref.shape[0] - (blocks - block) * keep_ref.shape[1]
        keep, got = (keep_ref[block], got_ref[start : start + keep_ref.shape[1], :])
        taps = jnp.concatenate(
            [jnp.where(first, keep, got), jnp.where(first, got, keep)], axis=0
        )
        waves = jnp.dot(table_ref[...], taps, preferred_element_type=F32)
        real, imag = (waves[:size], -waves[size:])
        if block == 0:
            real_ref[block] = real * (1.0 / size)
            imag_ref[block] = imag * (1.0 / size)
        else:
            real_ref[block] = real * (1.0 / size) - sign * before_imag
            imag_ref[block] = imag * (1.0 / size) + sign * before_real
        before_real, before_imag = (real, imag)


def mixed_branches(branches, keep_first, keep_second, got_first, got_second, short_ref, joined):
    own = lax.axis_index("fsdp")
    rows = keep_first.shape[0]
    half = keep_second.shape[1] // len(branches)
    joined[:HALO, :] = keep_second[:HALO, :] + got_second[:HALO, :].astype(F32)
    own_start = pl.multiple_of(HALO + own * rows, HALO)
    other_start = pl.multiple_of(HALO + (1 - own) * rows, HALO)
    joined[pl.ds(own_start, rows), :] = keep_first[...] + got_second[HALO:, :].astype(F32)
    joined[pl.ds(other_start, rows), :] = keep_second[HALO:, :] + got_first[...].astype(F32)
    mixed = []
    for place, branch in enumerate(branches):
        lanes = slice(place * half, (place + 1) * half)
        total = None
        for tap in range(3):
            taps = short_ref[tap, branch : branch + 1, :]
            taps = jnp.where(own == 0, taps[:, :half], taps[:, half:])
            term = taps * joined[pl.ds(HALO - tap, 2 * rows), lanes]
            total = term if total is None else total + term
        mixed.append(total)
    return mixed


def product_body(
    keep_first, keep_second, got_first, got_second, short_ref, order_ref, product_ref, joined
):
    key, value = mixed_branches(
        (1, 2), keep_first, keep_second, got_first, got_second, short_ref, joined
    )
    product_ref[...] = (key * value).astype(BF16)


def query_body(keep_first, keep_second, got_ref, short_ref, query_ref, joined):
    rows = keep_first.shape[0]
    got_first = got_ref.at[:rows, :]
    got_second = got_ref.at[rows : rows + keep_second.shape[0], :]
    (query,) = mixed_branches(
        (0,), keep_first, keep_second, got_first, got_second, short_ref, joined
    )
    query_ref[...] = query


def spectrum_term(step, block_ref, real_ref, imag_ref, table_ref):
    position = lax.axis_index("seq")
    size = table_ref.shape[1]
    source = position ^ step
    back = jnp.maximum(position - source, 0)
    block = block_ref[...]
    if step:
        block = jnp.where(source < position, block, jnp.zeros_like(block))
    waves = jnp.dot(table_ref[...], block, preferred_element_type=F32)
    real, imag = (waves[:size], -waves[size:])
    tap_real, tap_imag = (real_ref[back], imag_ref[back])
    return (real * tap_real - imag * tap_imag, real * tap_imag + imag * tap_real)


def conv_early_body(own_ref, near_ref, far_ref, real_ref, imag_ref, table_ref, total_ref):
    total_ref[0], total_ref[1] = spectrum_term(0, own_ref, real_ref, imag_ref, table_ref)
    for step, block_ref in ((1, near_ref), (3, far_ref)):
        real, imag = spectrum_term(step, block_ref, real_ref, imag_ref, table_ref)
        total_ref[0] += real
        total_ref[1] += imag


def gated_rows(place, rows, stacked, turned_ref, query_ref, gain_ref, own_ref):
    half = own_ref.shape[1]
    lines = pl.ds(pl.multiple_of(place * rows, rows), rows)
    conv = jnp.dot(turned_ref[lines, :], stacked, preferred_element_type=F32)
    first = lax.axis_index("fsdp") == 0
    gain = jnp.where(first, gain_ref[:, :half], gain_ref[:, half:])
    gated = query_ref[lines, :] * (conv + gain * own_ref[lines, :].astype(F32))
    return gated.astype(BF16)


def conv_last_body(
    last_ref, total_ref, real_ref, imag_ref, table_ref, turned_ref, query_ref, gain_ref, own_ref,
    go_ref, stacked_ref
):
    real, imag = spectrum_term(2, last_ref, real_ref, imag_ref, table_ref)
    stacked = jnp.concatenate([total_ref[0] + real, -(total_ref[1] + imag)], axis=0).astype(BF16)
    stacked_ref[...] = stacked
    other = 1 - lax.axis_index("fsdp")
    go_ref[...] = gated_rows(
        other, go_ref.shape[0], stacked, turned_ref, query_ref, gain_ref, own_ref
    )


def conv_stay_body(stacked_ref, turned_ref, query_ref, gain_ref, own_ref, stay_ref):
    own = lax.axis_index("fsdp")
    stay_ref[...] = gated_rows(
        own, stay_ref.shape[0], stacked_ref[...], turned_ref, query_ref, gain_ref, own_ref
    )


def join_body(stay_ref, got_ref, out_ref):
    first = lax.axis_index("fsdp") == 0
    half = stay_ref.shape[1]
    out_ref[:, :half] = jnp.where(first, stay_ref[...], got_ref[...])
    out_ref[:, half:] = jnp.where(first, got_ref[...], stay_ref[...])


def shape(dims, kind):
    return jax.ShapeDtypeStruct(dims, kind)


def pair_mesh(tokens, proj_weight, short_weight, skip_gain, filter_taps):
    rows = tokens.shape[0]
    width = proj_weight.shape[2]
    half = width // 2
    size = 2 * rows
    blocks = lax.axis_size("seq")
    weight = jnp.transpose(proj_weight, (1, 0, 2))
    pairs = [[(s, s ^ step) for s in range(blocks)] for step in range(blocks)]
    call = functools.partial(
        pl.pallas_call, compiler_params=pltpu.CompilerParams(vmem_limit_bytes=32 * 1024 * 1024)
    )

    cycled = lax.ppermute(tokens, ("fsdp", "chan"), [(1, 3), (3, 2), (2, 0), (0, 1)])
    token = shape((8, 128), F32)
    pack = call(
        pack_body,
        cost_estimate=LONG,
        in_specs=whole_specs(1),
        out_specs=whole_specs(1)[0],
        out_shape=shape((HALO, width), BF16),
    )(tokens)
    pack_got = lax.ppermute(
        pack,
        ("seq", "fsdp", "chan"),
        [
            (4 * s + 2 * f + c, 4 * ((s + 1) % blocks) + 2 * (f ^ (1 - c)) + c)
            for s in range(blocks)
            for f in range(2)
            for c in range(2)
        ],
    )
    tap_blocks = [filter_taps] + [
        lax.ppermute(filter_taps, "seq", pairs[step]) for step in range(1, blocks)
    ]
    cycled = after(cycled, pack)
    hop = exchange(cycled, "chan")
    pack_hop = exchange(pack_got, "chan")
    keep_first, send_first, keep_first_query, send_first_query = call(
        project_first_body,
        cost_estimate=LONG,
        in_specs=whole_specs(3),
        out_specs=whole_specs(4),
        out_shape=(
            shape((rows, 2 * half), F32),
            shape((rows, 2 * half), BF16),
            shape((rows, half), F32),
            shape((rows, half), BF16),
        ),
    )(tokens, cycled, weight)
    got_first = exchange(send_first, "fsdp")
    halo = call(
        halo_body,
        in_specs=whole_specs(2),
        out_specs=whole_specs(1)[0],
        out_shape=shape((HALO, tokens.shape[1]), BF16),
    )(pack_got, pack_hop)
    arrived = (cycled, hop, halo, weight)
    keep_second, send_second, second_done = call(
        project_product_body,
        in_specs=whole_specs(4),
        out_specs=whole_specs(3),
        out_shape=(
            shape((HALO + rows, 2 * half), F32),
            shape((HALO + rows, 2 * half), BF16),
            token,
        ),
    )(*arrived)
    keep_second_query, tap_keep, send_late, late_done = call(
        project_query_body,
        in_specs=whole_specs(6 + blocks),
        out_specs=whole_specs(4),
        out_shape=(
            shape((HALO + rows, half), F32),
            shape((blocks, rows, half), BF16),
            shape((rows + HALO + rows + blocks * rows, half), BF16),
            token,
        ),
    )(*arrived, send_first_query, second_done, *tap_blocks)
    got_second = exchange(send_second, "fsdp")

    product = call(
        product_body,
        cost_estimate=LONG,
        in_specs=whole_specs(6),
        out_specs=whole_specs(1)[0],
        out_shape=shape((size, half), BF16),
        scratch_shapes=[pltpu.VMEM((HALO + size, 2 * half), F32)],
    )(keep_first, keep_second, got_first, got_second, short_weight, late_done)
    got_late = exchange(after(send_late, got_first, cost_estimate=LONG), "fsdp")
    query = call(
        query_body,
        in_specs=whole_specs(4),
        out_specs=whole_specs(1)[0],
        out_shape=shape((size, half), F32),
        scratch_shapes=[pltpu.VMEM((HALO + size, half), F32)],
    )(keep_first_query, keep_second_query, got_late, short_weight)
    last, near, far = (lax.ppermute(product, "seq", pairs[step]) for step in (2, 1, 3))
    table = wave_table(size)
    forward = jnp.asarray(table, dtype=BF16)
    inverse = jnp.asarray(table.T, dtype=BF16)
    tap_real, tap_imag = call(
        taps_body,
        in_specs=whole_specs(3),
        out_specs=whole_specs(2),
        out_shape=(shape((blocks, size, half), F32), shape((blocks, size, half), F32)),
    )(forward, tap_keep, got_late)
    total = call(
        conv_early_body,
        in_specs=whole_specs(6),
        out_specs=whole_specs(1)[0],
        out_shape=shape((2, size, half), F32),
    )(product, near, far, tap_real, tap_imag, forward)
    ending = (inverse, query, skip_gain.reshape(1, width), product)
    go, stacked = call(
        conv_last_body,
        in_specs=whole_specs(9),
        out_specs=whole_specs(2),
        out_shape=(shape((rows, half), BF16), shape((2 * size, half), BF16)),
    )(last, total, tap_real, tap_imag, forward, *ending)
    stay = call(
        conv_stay_body,
        in_specs=whole_specs(5),
        out_specs=whole_specs(1)[0],
        out_shape=shape((rows, half), BF16),
    )(stacked, *ending)
    back = exchange(go, "fsdp")
    return call(
        join_body,
        in_specs=whole_specs(2),
        out_specs=whole_specs(1)[0],
        out_shape=shape((rows, width), BF16),
    )(stay, back)


def solution(mesh):
    in_specs = (
        P(("grp", "seq", "fsdp"), "chan"),
        P("fsdp", None, "chan"),
        P(None, None, "chan"),
        P("chan"),
        P(("seq", "fsdp"), "chan"),
    )
    out_specs = P(("grp", "seq", "fsdp"), "chan")
    sizes = mesh.shape
    paired = sizes["fsdp"] == 2 and sizes["chan"] == 2 and sizes["seq"] == 4
    per_device = pair_mesh if paired else any_mesh
    return jax.shard_map(
        per_device, mesh=mesh, in_specs=in_specs, out_specs=out_specs, check_vma=False
    )
```

```python
import functools
import math

import jax
import jax.numpy as jnp
import numpy as np
from jax import lax
from jax.experimental import pallas as pl
from jax.experimental.pallas import tpu as pltpu
from jax.sharding import PartitionSpec as P

HALO = 16
LONG = pl.CostEstimate(flops=10_000_000_000, bytes_accessed=40_000_000, transcendentals=0)
F32 = jnp.float32
BF16 = jnp.bfloat16


def shifted(value, axis, steps):
    count = lax.axis_size(axis)
    initial, last = (max(0, -steps), min(count, count - steps))
    return lax.ppermute(value, axis, [(source, source + steps) for source in range(initial, last)])


def index_grid(row_count, col_count):
    return (
        lax.broadcasted_iota(jnp.int32, (row_count, col_count), 0),
        lax.broadcasted_iota(jnp.int32, (row_count, col_count), 1),
    )


def phase_pair(row_ids, col_ids, period):
    wrapped = row_ids * col_ids % period
    phase = wrapped.astype(jnp.float32) * (2.0 * math.pi / period)
    return (jnp.cos(phase), jnp.sin(phase))


def multiply(real_x, imag_x):
    sig_real = real_x[0].astype(jnp.float32)
    sig_imag = imag_x[0].astype(jnp.float32)
    tap_real = real_x[1].astype(jnp.float32)
    tap_imag = imag_x[1].astype(jnp.float32)
    real_z = (sig_real * tap_real - sig_imag * tap_imag).astype(jnp.bfloat16)
    imag_z = (sig_real * tap_imag + sig_imag * tap_real).astype(jnp.bfloat16)
    return (real_z, imag_z)


def spread(stacked, groups, inner_shape):
    shaped = stacked.reshape((2, groups, 1) + inner_shape)
    moved = lax.all_to_all(shaped, ("seq", "fsdp"), split_axis=1, concat_axis=2, tiled=True)
    return moved.reshape((2, groups) + inner_shape)


def any_mesh(tokens, proj_weight, short_weight, skip_gain, filter_taps):
    whole = lax.all_gather(tokens, "chan", axis=1, tiled=True)
    row_count = whole.shape[0]
    width = proj_weight.shape[2]
    flat_width = 3 * width
    piece = lax.all_gather(proj_weight, "fsdp", axis=0, tiled=True)
    summed = jnp.dot(
        whole, piece.reshape(piece.shape[0], flat_width), preferred_element_type=jnp.float32
    )
    projected = summed.astype(jnp.bfloat16).reshape(row_count, 3, width)
    earlier = shifted(projected[row_count - 2 :], ("seq", "fsdp"), 1)
    extended = jnp.concatenate([earlier, projected], axis=0).astype(jnp.float32)
    mixed = (
        short_weight[0] * extended[2:]
        + short_weight[1] * extended[1:-1]
        + short_weight[2] * extended[:-2]
    )
    query = mixed[:, 0]
    product = (mixed[:, 1] * mixed[:, 2]).astype(jnp.bfloat16)
    groups = lax.axis_size(("seq", "fsdp"))
    position = lax.axis_index(("seq", "fsdp"))
    period_rows = 2 * groups
    length = period_rows * row_count
    scale = 1.0 / length
    bin_ids, tap_ids = index_grid(period_rows, groups)
    first_cos, first_sin = phase_pair(bin_ids, tap_ids, period_rows)
    first_cos = first_cos.astype(jnp.bfloat16)
    first_sin = first_sin.astype(jnp.bfloat16)
    col_ids, freq_ids = index_grid(row_count, row_count)
    last_cos, last_sin = phase_pair(col_ids, freq_ids, row_count)
    last_cos = last_cos.astype(jnp.bfloat16)
    last_sin = last_sin.astype(jnp.bfloat16)
    stacked = jnp.stack([product, filter_taps])
    f32 = jnp.float32
    per_dev = row_count // groups
    per_bins = period_rows // groups
    arrived = spread(stacked.reshape(2, groups, per_dev, width), groups, (per_dev, width))
    real_a = jnp.einsum("qp,kpmc->kqmc", first_cos, arrived, preferred_element_type=f32)
    imag_a = -jnp.einsum("qp,kpmc->kqmc", first_sin, arrived, preferred_element_type=f32)
    row_ids, mid_ids = index_grid(period_rows, per_dev)
    twist_cos, twist_sin = phase_pair(row_ids, mid_ids + position * per_dev, length)
    twist_cos = twist_cos[:, :, None]
    twist_sin = twist_sin[:, :, None]
    real_b = (real_a * twist_cos + imag_a * twist_sin).astype(jnp.bfloat16)
    imag_b = (imag_a * twist_cos - real_a * twist_sin).astype(jnp.bfloat16)
    outgoing = jnp.stack([real_b, imag_b]).reshape(2, 2, groups, per_bins, 1, per_dev, width)
    turned = lax.all_to_all(outgoing, ("seq", "fsdp"), split_axis=2, concat_axis=4, tiled=True)
    turned = turned.reshape(2, 2, per_bins, row_count, width)
    real_b = turned[0]
    imag_b = turned[1]
    real_x = (
        jnp.einsum("kqmc,mr->kqrc", real_b, last_cos, preferred_element_type=f32)
        + jnp.einsum("kqmc,mr->kqrc", imag_b, last_sin, preferred_element_type=f32)
    ).astype(jnp.bfloat16)
    imag_x = (
        jnp.einsum("kqmc,mr->kqrc", imag_b, last_cos, preferred_element_type=f32)
        - jnp.einsum("kqmc,mr->kqrc", real_b, last_sin, preferred_element_type=f32)
    ).astype(jnp.bfloat16)
    real_z, imag_z = multiply(real_x, imag_x)
    real_v = jnp.einsum("qrc,mr->qmc", real_z, last_cos, preferred_element_type=f32) - jnp.einsum(
        "qrc,mr->qmc", imag_z, last_sin, preferred_element_type=f32
    )
    imag_v = jnp.einsum("qrc,mr->qmc", imag_z, last_cos, preferred_element_type=f32) + jnp.einsum(
        "qrc,mr->qmc", real_z, last_sin, preferred_element_type=f32
    )
    row_ids, mid_ids = index_grid(per_bins, row_count)
    twist_cos, twist_sin = phase_pair(row_ids + position * per_bins, mid_ids, length)
    twist_cos = twist_cos[:, :, None]
    twist_sin = twist_sin[:, :, None]
    real_w = (real_v * twist_cos - imag_v * twist_sin).astype(jnp.bfloat16)
    imag_w = (imag_v * twist_cos + real_v * twist_sin).astype(jnp.bfloat16)
    backward = jnp.stack([real_w, imag_w]).reshape(2, 1, per_bins, groups, per_dev, width)
    returned = lax.all_to_all(backward, ("seq", "fsdp"), split_axis=3, concat_axis=1, tiled=True)
    returned = returned.reshape(2, period_rows, per_dev, width)
    conv_rows = jnp.einsum(
        "qp,qmc->pmc", first_cos, returned[0], preferred_element_type=f32
    ) - jnp.einsum("qp,qmc->pmc", first_sin, returned[1], preferred_element_type=f32)
    conv_rows = (conv_rows * scale).astype(jnp.bfloat16)
    homed = lax.all_to_all(
        conv_rows.reshape(groups, 1, per_dev, width),
        ("seq", "fsdp"),
        split_axis=0,
        concat_axis=1,
        tiled=True,
    )
    conv = homed.reshape(row_count, width)
    result = query * (conv.astype(jnp.float32) + skip_gain * product.astype(jnp.float32))
    return result.astype(jnp.bfloat16)


def wave_table(size):
    freq, time = np.meshgrid(np.arange(size), np.arange(size), indexing="ij")
    angle = ((2 * freq + 1) * time % (4 * size)) * (math.pi / (2 * size))
    return np.concatenate([np.cos(angle), np.sin(angle)], axis=0)


def exchange(value, axis):
    return lax.ppermute(value, axis, [(0, 1), (1, 0)])


def whole_specs(count):
    return [pl.BlockSpec(memory_space=pltpu.VMEM)] * count


def split_channels(summed, own_half):
    half = summed.shape[1] // 2
    low, high = (summed[:, :half], summed[:, half:])
    first = own_half == 0
    return (jnp.where(first, low, high), jnp.where(first, high, low))


def pick_rows(source, target):
    lines = lax.broadcasted_iota(jnp.int32, (HALO, HALO), 0)
    places = lax.broadcasted_iota(jnp.int32, (HALO, HALO), 1)
    wanted = (lines - target == places - source) & (places >= source) & (places < source + 2)
    return wanted.astype(F32).astype(BF16)


def pack_body(rows_ref, pack_ref):
    width = pack_ref.shape[1]
    last = rows_ref[rows_ref.shape[0] - HALO :, :]
    total = jnp.zeros((HALO, width), F32)
    for piece in range(last.shape[1] // width):
        part = last[:, piece * width : (piece + 1) * width]
        total += jnp.dot(pick_rows(HALO - 2, 2 * piece), part, preferred_element_type=F32)
    pack_ref[...] = total.astype(BF16)


def unpack_halo(pieces, count):
    parts = [
        jnp.dot(pick_rows(2 * piece, HALO - 2), pieces, preferred_element_type=F32).astype(BF16)
        for piece in range(count)
    ]
    return jnp.concatenate(parts, axis=1)


def project(rows, weight_ref, branches, keep_ref, send_ref):
    own_half = lax.axis_index("fsdp")
    half = weight_ref.shape[2] // 2
    for place, branch in enumerate(branches):
        summed = jnp.dot(rows, weight_ref[branch], preferred_element_type=F32)
        keep, send = split_channels(summed, own_half)
        lanes = slice(place * half, (place + 1) * half)
        keep_ref[:, lanes] = keep
        send_ref[:, lanes] = send.astype(BF16)


def project_first_body(
    rows_ref, cycled_ref, weight_ref, keep_product, send_product, keep_query, send_query
):
    here = lax.axis_index("chan") == lax.axis_index("fsdp")
    rows = jnp.where(here, rows_ref[...], cycled_ref[...])
    project(rows, weight_ref, (1, 2), keep_product, send_product)
    project(rows, weight_ref, (0,), keep_query, send_query)


def halo_body(pack_ref, pack_hop_ref, halo_ref):
    here = lax.axis_index("chan") == lax.axis_index("fsdp")
    pieces = halo_ref.shape[1] // pack_ref.shape[1]
    halo = unpack_halo(jnp.where(here, pack_ref[...], pack_hop_ref[...]), pieces)
    halo_ref[...] = jnp.where(lax.axis_index("seq") > 0, halo, jnp.zeros_like(halo))


def arrived_rows(cycled_ref, hop_ref, halo_ref):
    here = lax.axis_index("chan") == lax.axis_index("fsdp")
    rows = jnp.where(here, cycled_ref[...], hop_ref[...])
    return jnp.concatenate([halo_ref[...], rows], axis=0)


def project_product_body(
    cycled_ref, hop_ref, halo_ref, weight_ref, keep_ref, send_ref, done_ref
):
    rows = arrived_rows(cycled_ref, hop_ref, halo_ref)
    project(rows, weight_ref, (1, 2), keep_ref, send_ref)
    done_ref[...] = jnp.zeros_like(done_ref)


def project_query_body(
    cycled_ref, hop_ref, halo_ref, weight_ref, first_ref, order_ref,
    own_ref, one_ref, two_ref, three_ref, keep_ref, taps_ref, send_ref, done_ref
):
    rows = arrived_rows(cycled_ref, hop_ref, halo_ref)
    count = first_ref.shape[0]
    send_ref[:count, :] = first_ref[...]
    after_query = count + rows.shape[0]
    project(rows, weight_ref, (0,), keep_ref, send_ref.at[count:after_query, :])
    position = lax.axis_index("seq")
    first = lax.axis_index("fsdp") == 0
    _, tap_rows, half = taps_ref.shape
    for step, tap_ref in enumerate((own_ref, one_ref, two_ref, three_ref)):
        block = position ^ step
        low, high = (tap_ref[:, :half], tap_ref[:, half:])
        taps_ref[block] = jnp.where(first, low, high)
        start = pl.multiple_of(after_query + block * tap_rows, HALO)
        send_ref[pl.ds(start, tap_rows), :] = jnp.where(first, high, low)
    done_ref[...] = jnp.zeros_like(done_ref)


def after_body(*refs):
    pass


def after(value, *orders, cost_estimate=None):
    return pl.pallas_call(
        after_body,
        in_specs=whole_specs(1 + len(orders)),
        out_specs=whole_specs(1)[0],
        out_shape=shape(value.shape, value.dtype),
        input_output_aliases={0: 0},
        cost_estimate=cost_estimate,
        compiler_params=pltpu.CompilerParams(vmem_limit_bytes=32 * 1024 * 1024),
    )(value, *orders)


def taps_body(table_ref, keep_ref, got_ref, real_ref, imag_ref):
    first = lax.axis_index("fsdp") == 0
    blocks = keep_ref.shape[0]
    size = table_ref.shape[1]
    sign = 1.0 - 2.0 * (lax.broadcasted_iota(jnp.int32, (size, 1), 0) % 2).astype(F32)
    sign = sign * (1.0 / size)
    before_real = before_imag = None
    for block in range(blocks):
        start = got_ref.shape[0] - (blocks - block) * keep_ref.shape[1]
        keep, got = (keep_ref[block], got_ref[start : start + keep_ref.shape[1], :])
        taps = jnp.concatenate(
            [jnp.where(first, keep, got), jnp.where(first, got, keep)], axis=0
        )
        waves = jnp.dot(table_ref[...], taps, preferred_element_type=F32)
        real, imag = (waves[:size], -waves[size:])
        if block == 0:
            real_ref[block] = real * (1.0 / size)
            imag_ref[block] = imag * (1.0 / size)
        else:
            real_ref[block] = real * (1.0 / size) - sign * before_imag
            imag_ref[block] = imag * (1.0 / size) + sign * before_real
        before_real, before_imag = (real, imag)


def mixed_branches(branches, keep_first, keep_second, got_first, got_second, short_ref, joined):
    own = lax.axis_index("fsdp")
    rows = keep_first.shape[0]
    half = keep_second.shape[1] // len(branches)
    joined[:HALO, :] = keep_second[:HALO, :] + got_second[:HALO, :].astype(F32)
    own_start = pl.multiple_of(HALO + own * rows, HALO)
    other_start = pl.multiple_of(HALO + (1 - own) * rows, HALO)
    joined[pl.ds(own_start, rows), :] = keep_first[...] + got_second[HALO:, :].astype(F32)
    joined[pl.ds(other_start, rows), :] = keep_second[HALO:, :] + got_first[...].astype(F32)
    mixed = []
    for place, branch in enumerate(branches):
        lanes = slice(place * half, (place + 1) * half)
        total = None
        for tap in range(3):
            taps = short_ref[tap, branch : branch + 1, :]
            taps = jnp.where(own == 0, taps[:, :half], taps[:, half:])
            term = taps * joined[pl.ds(HALO - tap, 2 * rows), lanes]
            total = term if total is None else total + term
        mixed.append(total)
    return mixed


def product_body(
    keep_first, keep_second, got_first, got_second, short_ref, order_ref, product_ref, joined
):
    key, value = mixed_branches(
        (1, 2), keep_first, keep_second, got_first, got_second, short_ref, joined
    )
    product_ref[...] = (key * value).astype(BF16)


def query_body(keep_first, keep_second, got_ref, short_ref, query_ref, joined):
    rows = keep_first.shape[0]
    got_first = got_ref.at[:rows, :]
    got_second = got_ref.at[rows : rows + keep_second.shape[0], :]
    (query,) = mixed_branches(
        (0,), keep_first, keep_second, got_first, got_second, short_ref, joined
    )
    query_ref[...] = query


def spectrum_term(step, block_ref, real_ref, imag_ref, table_ref):
    position = lax.axis_index("seq")
    size = table_ref.shape[1]
    source = position ^ step
    back = jnp.maximum(position - source, 0)
    block = block_ref[...]
    if step:
        block = jnp.where(source < position, block, jnp.zeros_like(block))
    waves = jnp.dot(table_ref[...], block, preferred_element_type=F32)
    real, imag = (waves[:size], -waves[size:])
    tap_real, tap_imag = (real_ref[back], imag_ref[back])
    return (real * tap_real - imag * tap_imag, real * tap_imag + imag * tap_real)


def conv_early_body(own_ref, near_ref, far_ref, real_ref, imag_ref, table_ref, total_ref):
    total_ref[0], total_ref[1] = spectrum_term(0, own_ref, real_ref, imag_ref, table_ref)
    for step, block_ref in ((1, near_ref), (3, far_ref)):
        real, imag = spectrum_term(step, block_ref, real_ref, imag_ref, table_ref)
        total_ref[0] += real
        total_ref[1] += imag


def gated_rows(place, rows, stacked, turned_ref, query_ref, gain_ref, own_ref):
    half = own_ref.shape[1]
    lines = pl.ds(pl.multiple_of(place * rows, rows), rows)
    conv = jnp.dot(turned_ref[lines, :], stacked, preferred_element_type=F32)
    first = lax.axis_index("fsdp") == 0
    gain = jnp.where(first, gain_ref[:, :half], gain_ref[:, half:])
    gated = query_ref[lines, :] * (conv + gain * own_ref[lines, :].astype(F32))
    return gated.astype(BF16)


def conv_last_body(
    last_ref, total_ref, real_ref, imag_ref, table_ref, turned_ref, query_ref, gain_ref, own_ref,
    go_ref, stacked_ref
):
    real, imag = spectrum_term(2, last_ref, real_ref, imag_ref, table_ref)
    stacked = jnp.concatenate([total_ref[0] + real, -(total_ref[1] + imag)], axis=0).astype(BF16)
    stacked_ref[...] = stacked
    other = 1 - lax.axis_index("fsdp")
    go_ref[...] = gated_rows(
        other, go_ref.shape[0], stacked, turned_ref, query_ref, gain_ref, own_ref
    )


def conv_stay_body(stacked_ref, turned_ref, query_ref, gain_ref, own_ref, stay_ref):
    own = lax.axis_index("fsdp")
    stay_ref[...] = gated_rows(
        own, stay_ref.shape[0], stacked_ref[...], turned_ref, query_ref, gain_ref, own_ref
    )


def join_body(stay_ref, got_ref, out_ref):
    first = lax.axis_index("fsdp") == 0
    half = stay_ref.shape[1]
    out_ref[:, :half] = jnp.where(first, stay_ref[...], got_ref[...])
    out_ref[:, half:] = jnp.where(first, got_ref[...], stay_ref[...])


def shape(dims, kind):
    return jax.ShapeDtypeStruct(dims, kind)


def pair_mesh(tokens, proj_weight, short_weight, skip_gain, filter_taps):
    rows = tokens.shape[0]
    width = proj_weight.shape[2]
    half = width // 2
    size = 2 * rows
    blocks = lax.axis_size("seq")
    weight = jnp.transpose(proj_weight, (1, 0, 2))
    pairs = [[(s, s ^ step) for s in range(blocks)] for step in range(blocks)]
    call = functools.partial(
        pl.pallas_call, compiler_params=pltpu.CompilerParams(vmem_limit_bytes=32 * 1024 * 1024)
    )

    cycled = lax.ppermute(tokens, ("fsdp", "chan"), [(1, 3), (3, 2), (2, 0), (0, 1)])
    token = shape((8, 128), F32)
    pack = call(
        pack_body,
        cost_estimate=LONG,
        in_specs=whole_specs(1),
        out_specs=whole_specs(1)[0],
        out_shape=shape((HALO, width), BF16),
    )(tokens)
    pack_got = lax.ppermute(
        pack,
        ("seq", "fsdp", "chan"),
        [
            (4 * s + 2 * f + c, 4 * ((s + 1) % blocks) + 2 * (f ^ (1 - c)) + c)
            for s in range(blocks)
            for f in range(2)
            for c in range(2)
        ],
    )
    arrived_taps = {
        step: lax.ppermute(filter_taps, "seq", pairs[step]) for step in (2, 1, 3)
    }
    tap_blocks = [filter_taps] + [arrived_taps[step] for step in range(1, blocks)]
    cycled = after(cycled, pack_got)
    hop = exchange(cycled, "chan")
    pack_hop = exchange(pack_got, "chan")
    keep_first, send_first, keep_first_query, send_first_query = call(
        project_first_body,
        cost_estimate=LONG,
        in_specs=whole_specs(3),
        out_specs=whole_specs(4),
        out_shape=(
            shape((rows, 2 * half), F32),
            shape((rows, 2 * half), BF16),
            shape((rows, half), F32),
            shape((rows, half), BF16),
        ),
    )(tokens, cycled, weight)
    got_first = exchange(send_first, "fsdp")
    halo = call(
        halo_body,
        in_specs=whole_specs(2),
        out_specs=whole_specs(1)[0],
        out_shape=shape((HALO, tokens.shape[1]), BF16),
    )(pack_got, pack_hop)
    arrived = (cycled, hop, halo, weight)
    keep_second, send_second, second_done = call(
        project_product_body,
        in_specs=whole_specs(4),
        out_specs=whole_specs(3),
        out_shape=(
            shape((HALO + rows, 2 * half), F32),
            shape((HALO + rows, 2 * half), BF16),
            token,
        ),
    )(*arrived)
    keep_second_query, tap_keep, send_late, late_done = call(
        project_query_body,
        in_specs=whole_specs(6 + blocks),
        out_specs=whole_specs(4),
        out_shape=(
            shape((HALO + rows, half), F32),
            shape((blocks, rows, half), BF16),
            shape((rows + HALO + rows + blocks * rows, half), BF16),
            token,
        ),
    )(*arrived, send_first_query, second_done, *tap_blocks)
    got_second = exchange(send_second, "fsdp")

    product = call(
        product_body,
        cost_estimate=LONG,
        in_specs=whole_specs(6),
        out_specs=whole_specs(1)[0],
        out_shape=shape((size, half), BF16),
        scratch_shapes=[pltpu.VMEM((HALO + size, 2 * half), F32)],
    )(keep_first, keep_second, got_first, got_second, short_weight, late_done)
    got_late = exchange(after(send_late, got_first, cost_estimate=LONG), "fsdp")
    query = call(
        query_body,
        in_specs=whole_specs(4),
        out_specs=whole_specs(1)[0],
        out_shape=shape((size, half), F32),
        scratch_shapes=[pltpu.VMEM((HALO + size, half), F32)],
    )(keep_first_query, keep_second_query, got_late, short_weight)
    last, near, far = (lax.ppermute(product, "seq", pairs[step]) for step in (2, 1, 3))
    table = wave_table(size)
    forward = jnp.asarray(table, dtype=BF16)
    inverse = jnp.asarray(table.T, dtype=BF16)
    tap_real, tap_imag = call(
        taps_body,
        in_specs=whole_specs(3),
        out_specs=whole_specs(2),
        out_shape=(shape((blocks, size, half), F32), shape((blocks, size, half), F32)),
    )(forward, tap_keep, got_late)
    total = call(
        conv_early_body,
        in_specs=whole_specs(6),
        out_specs=whole_specs(1)[0],
        out_shape=shape((2, size, half), F32),
    )(product, near, far, tap_real, tap_imag, forward)
    ending = (inverse, query, skip_gain.reshape(1, width), product)
    go, stacked = call(
        conv_last_body,
        in_specs=whole_specs(9),
        out_specs=whole_specs(2),
        out_shape=(shape((rows, half), BF16), shape((2 * size, half), BF16)),
    )(last, total, tap_real, tap_imag, forward, *ending)
    stay = call(
        conv_stay_body,
        in_specs=whole_specs(5),
        out_specs=whole_specs(1)[0],
        out_shape=shape((rows, half), BF16),
    )(stacked, *ending)
    back = exchange(go, "fsdp")
    return call(
        join_body,
        in_specs=whole_specs(2),
        out_specs=whole_specs(1)[0],
        out_shape=shape((rows, width), BF16),
    )(stay, back)


def solution(mesh):
    in_specs = (
        P(("grp", "seq", "fsdp"), "chan"),
        P("fsdp", None, "chan"),
        P(None, None, "chan"),
        P("chan"),
        P(("seq", "fsdp"), "chan"),
    )
    out_specs = P(("grp", "seq", "fsdp"), "chan")
    sizes = mesh.shape
    paired = sizes["fsdp"] == 2 and sizes["chan"] == 2 and sizes["seq"] == 4
    per_device = pair_mesh if paired else any_mesh
    return jax.shard_map(
        per_device, mesh=mesh, in_specs=in_specs, out_specs=out_specs, check_vma=False
    )
```

```python
import functools
import math

import jax
import jax.numpy as jnp
import numpy as np
from jax import lax
from jax.experimental import pallas as pl
from jax.experimental.pallas import tpu as pltpu
from jax.sharding import PartitionSpec as P

HALO = 16
LONG = pl.CostEstimate(flops=10_000_000_000, bytes_accessed=40_000_000, transcendentals=0)
F32 = jnp.float32
BF16 = jnp.bfloat16


def shifted(value, axis, steps):
    count = lax.axis_size(axis)
    initial, last = (max(0, -steps), min(count, count - steps))
    return lax.ppermute(value, axis, [(source, source + steps) for source in range(initial, last)])


def index_grid(row_count, col_count):
    return (
        lax.broadcasted_iota(jnp.int32, (row_count, col_count), 0),
        lax.broadcasted_iota(jnp.int32, (row_count, col_count), 1),
    )


def phase_pair(row_ids, col_ids, period):
    wrapped = row_ids * col_ids % period
    phase = wrapped.astype(jnp.float32) * (2.0 * math.pi / period)
    return (jnp.cos(phase), jnp.sin(phase))


def multiply(real_x, imag_x):
    sig_real = real_x[0].astype(jnp.float32)
    sig_imag = imag_x[0].astype(jnp.float32)
    tap_real = real_x[1].astype(jnp.float32)
    tap_imag = imag_x[1].astype(jnp.float32)
    real_z = (sig_real * tap_real - sig_imag * tap_imag).astype(jnp.bfloat16)
    imag_z = (sig_real * tap_imag + sig_imag * tap_real).astype(jnp.bfloat16)
    return (real_z, imag_z)


def spread(stacked, groups, inner_shape):
    shaped = stacked.reshape((2, groups, 1) + inner_shape)
    moved = lax.all_to_all(shaped, ("seq", "fsdp"), split_axis=1, concat_axis=2, tiled=True)
    return moved.reshape((2, groups) + inner_shape)


def any_mesh(tokens, proj_weight, short_weight, skip_gain, filter_taps):
    whole = lax.all_gather(tokens, "chan", axis=1, tiled=True)
    row_count = whole.shape[0]
    width = proj_weight.shape[2]
    flat_width = 3 * width
    piece = lax.all_gather(proj_weight, "fsdp", axis=0, tiled=True)
    summed = jnp.dot(
        whole, piece.reshape(piece.shape[0], flat_width), preferred_element_type=jnp.float32
    )
    projected = summed.astype(jnp.bfloat16).reshape(row_count, 3, width)
    earlier = shifted(projected[row_count - 2 :], ("seq", "fsdp"), 1)
    extended = jnp.concatenate([earlier, projected], axis=0).astype(jnp.float32)
    mixed = (
        short_weight[0] * extended[2:]
        + short_weight[1] * extended[1:-1]
        + short_weight[2] * extended[:-2]
    )
    query = mixed[:, 0]
    product = (mixed[:, 1] * mixed[:, 2]).astype(jnp.bfloat16)
    groups = lax.axis_size(("seq", "fsdp"))
    position = lax.axis_index(("seq", "fsdp"))
    period_rows = 2 * groups
    length = period_rows * row_count
    scale = 1.0 / length
    bin_ids, tap_ids = index_grid(period_rows, groups)
    first_cos, first_sin = phase_pair(bin_ids, tap_ids, period_rows)
    first_cos = first_cos.astype(jnp.bfloat16)
    first_sin = first_sin.astype(jnp.bfloat16)
    col_ids, freq_ids = index_grid(row_count, row_count)
    last_cos, last_sin = phase_pair(col_ids, freq_ids, row_count)
    last_cos = last_cos.astype(jnp.bfloat16)
    last_sin = last_sin.astype(jnp.bfloat16)
    stacked = jnp.stack([product, filter_taps])
    f32 = jnp.float32
    per_dev = row_count // groups
    per_bins = period_rows // groups
    arrived = spread(stacked.reshape(2, groups, per_dev, width), groups, (per_dev, width))
    real_a = jnp.einsum("qp,kpmc->kqmc", first_cos, arrived, preferred_element_type=f32)
    imag_a = -jnp.einsum("qp,kpmc->kqmc", first_sin, arrived, preferred_element_type=f32)
    row_ids, mid_ids = index_grid(period_rows, per_dev)
    twist_cos, twist_sin = phase_pair(row_ids, mid_ids + position * per_dev, length)
    twist_cos = twist_cos[:, :, None]
    twist_sin = twist_sin[:, :, None]
    real_b = (real_a * twist_cos + imag_a * twist_sin).astype(jnp.bfloat16)
    imag_b = (imag_a * twist_cos - real_a * twist_sin).astype(jnp.bfloat16)
    outgoing = jnp.stack([real_b, imag_b]).reshape(2, 2, groups, per_bins, 1, per_dev, width)
    turned = lax.all_to_all(outgoing, ("seq", "fsdp"), split_axis=2, concat_axis=4, tiled=True)
    turned = turned.reshape(2, 2, per_bins, row_count, width)
    real_b = turned[0]
    imag_b = turned[1]
    real_x = (
        jnp.einsum("kqmc,mr->kqrc", real_b, last_cos, preferred_element_type=f32)
        + jnp.einsum("kqmc,mr->kqrc", imag_b, last_sin, preferred_element_type=f32)
    ).astype(jnp.bfloat16)
    imag_x = (
        jnp.einsum("kqmc,mr->kqrc", imag_b, last_cos, preferred_element_type=f32)
        - jnp.einsum("kqmc,mr->kqrc", real_b, last_sin, preferred_element_type=f32)
    ).astype(jnp.bfloat16)
    real_z, imag_z = multiply(real_x, imag_x)
    real_v = jnp.einsum("qrc,mr->qmc", real_z, last_cos, preferred_element_type=f32) - jnp.einsum(
        "qrc,mr->qmc", imag_z, last_sin, preferred_element_type=f32
    )
    imag_v = jnp.einsum("qrc,mr->qmc", imag_z, last_cos, preferred_element_type=f32) + jnp.einsum(
        "qrc,mr->qmc", real_z, last_sin, preferred_element_type=f32
    )
    row_ids, mid_ids = index_grid(per_bins, row_count)
    twist_cos, twist_sin = phase_pair(row_ids + position * per_bins, mid_ids, length)
    twist_cos = twist_cos[:, :, None]
    twist_sin = twist_sin[:, :, None]
    real_w = (real_v * twist_cos - imag_v * twist_sin).astype(jnp.bfloat16)
    imag_w = (imag_v * twist_cos + real_v * twist_sin).astype(jnp.bfloat16)
    backward = jnp.stack([real_w, imag_w]).reshape(2, 1, per_bins, groups, per_dev, width)
    returned = lax.all_to_all(backward, ("seq", "fsdp"), split_axis=3, concat_axis=1, tiled=True)
    returned = returned.reshape(2, period_rows, per_dev, width)
    conv_rows = jnp.einsum(
        "qp,qmc->pmc", first_cos, returned[0], preferred_element_type=f32
    ) - jnp.einsum("qp,qmc->pmc", first_sin, returned[1], preferred_element_type=f32)
    conv_rows = (conv_rows * scale).astype(jnp.bfloat16)
    homed = lax.all_to_all(
        conv_rows.reshape(groups, 1, per_dev, width),
        ("seq", "fsdp"),
        split_axis=0,
        concat_axis=1,
        tiled=True,
    )
    conv = homed.reshape(row_count, width)
    result = query * (conv.astype(jnp.float32) + skip_gain * product.astype(jnp.float32))
    return result.astype(jnp.bfloat16)


def wave_table(size):
    freq, time = np.meshgrid(np.arange(size), np.arange(size), indexing="ij")
    angle = ((2 * freq + 1) * time % (4 * size)) * (math.pi / (2 * size))
    return np.concatenate([np.cos(angle), np.sin(angle)], axis=0)


def exchange(value, axis):
    return lax.ppermute(value, axis, [(0, 1), (1, 0)])


def whole_specs(count):
    return [pl.BlockSpec(memory_space=pltpu.VMEM)] * count


def split_channels(summed, own_half):
    half = summed.shape[1] // 2
    low, high = (summed[:, :half], summed[:, half:])
    first = own_half == 0
    return (jnp.where(first, low, high), jnp.where(first, high, low))


def pick_rows(source, target):
    lines = lax.broadcasted_iota(jnp.int32, (HALO, HALO), 0)
    places = lax.broadcasted_iota(jnp.int32, (HALO, HALO), 1)
    wanted = (lines - target == places - source) & (places >= source) & (places < source + 2)
    return wanted.astype(F32).astype(BF16)


def pack_body(rows_ref, pack_ref):
    width = pack_ref.shape[1]
    last = rows_ref[rows_ref.shape[0] - HALO :, :]
    total = jnp.zeros((HALO, width), F32)
    for piece in range(last.shape[1] // width):
        part = last[:, piece * width : (piece + 1) * width]
        total += jnp.dot(pick_rows(HALO - 2, 2 * piece), part, preferred_element_type=F32)
    pack_ref[...] = total.astype(BF16)


def unpack_halo(pieces, count):
    parts = [
        jnp.dot(pick_rows(2 * piece, HALO - 2), pieces, preferred_element_type=F32).astype(BF16)
        for piece in range(count)
    ]
    return jnp.concatenate(parts, axis=1)


def project(rows, weight_ref, branches, keep_ref, send_ref):
    own_half = lax.axis_index("fsdp")
    half = weight_ref.shape[2] // 2
    for place, branch in enumerate(branches):
        summed = jnp.dot(rows, weight_ref[branch], preferred_element_type=F32)
        keep, send = split_channels(summed, own_half)
        lanes = slice(place * half, (place + 1) * half)
        keep_ref[:, lanes] = keep
        send_ref[:, lanes] = send.astype(BF16)


def project_first_body(
    rows_ref, cycled_ref, weight_ref, keep_product, send_product, keep_query, send_query
):
    here = lax.axis_index("chan") == lax.axis_index("fsdp")
    rows = jnp.where(here, rows_ref[...], cycled_ref[...])
    project(rows, weight_ref, (1, 2), keep_product, send_product)
    project(rows, weight_ref, (0,), keep_query, send_query)


def halo_body(pack_ref, pack_hop_ref, halo_ref):
    here = lax.axis_index("chan") == lax.axis_index("fsdp")
    pieces = halo_ref.shape[1] // pack_ref.shape[1]
    halo = unpack_halo(jnp.where(here, pack_ref[...], pack_hop_ref[...]), pieces)
    halo_ref[...] = jnp.where(lax.axis_index("seq") > 0, halo, jnp.zeros_like(halo))


def arrived_rows(cycled_ref, hop_ref, halo_ref):
    here = lax.axis_index("chan") == lax.axis_index("fsdp")
    rows = jnp.where(here, cycled_ref[...], hop_ref[...])
    return jnp.concatenate([halo_ref[...], rows], axis=0)


def project_product_body(
    cycled_ref, hop_ref, halo_ref, weight_ref, keep_ref, send_ref, done_ref
):
    rows = arrived_rows(cycled_ref, hop_ref, halo_ref)
    project(rows, weight_ref, (1, 2), keep_ref, send_ref)
    done_ref[...] = jnp.zeros_like(done_ref)


def project_query_body(
    cycled_ref, hop_ref, halo_ref, weight_ref, first_ref, order_ref,
    own_ref, one_ref, two_ref, three_ref, keep_ref, taps_ref, send_ref, done_ref
):
    rows = arrived_rows(cycled_ref, hop_ref, halo_ref)
    count = first_ref.shape[0]
    send_ref[:count, :] = first_ref[...]
    after_query = count + rows.shape[0]
    project(rows, weight_ref, (0,), keep_ref, send_ref.at[count:after_query, :])
    position = lax.axis_index("seq")
    first = lax.axis_index("fsdp") == 0
    _, tap_rows, half = taps_ref.shape
    for step, tap_ref in enumerate((own_ref, one_ref, two_ref, three_ref)):
        block = position ^ step
        low, high = (tap_ref[:, :half], tap_ref[:, half:])
        taps_ref[block] = jnp.where(first, low, high)
        start = pl.multiple_of(after_query + block * tap_rows, HALO)
        send_ref[pl.ds(start, tap_rows), :] = jnp.where(first, high, low)
    done_ref[...] = jnp.zeros_like(done_ref)


def after_body(*refs):
    pass


def after(value, *orders, cost_estimate=None):
    return pl.pallas_call(
        after_body,
        in_specs=whole_specs(1 + len(orders)),
        out_specs=whole_specs(1)[0],
        out_shape=shape(value.shape, value.dtype),
        input_output_aliases={0: 0},
        cost_estimate=cost_estimate,
        compiler_params=pltpu.CompilerParams(vmem_limit_bytes=32 * 1024 * 1024),
    )(value, *orders)


def taps_body(table_ref, keep_ref, got_ref, real_ref, imag_ref):
    first = lax.axis_index("fsdp") == 0
    blocks = keep_ref.shape[0]
    size = table_ref.shape[1]
    sign = 1.0 - 2.0 * (lax.broadcasted_iota(jnp.int32, (size, 1), 0) % 2).astype(F32)
    sign = sign * (1.0 / size)
    before_real = before_imag = None
    for block in range(blocks):
        start = got_ref.shape[0] - (blocks - block) * keep_ref.shape[1]
        keep, got = (keep_ref[block], got_ref[start : start + keep_ref.shape[1], :])
        taps = jnp.concatenate(
            [jnp.where(first, keep, got), jnp.where(first, got, keep)], axis=0
        )
        waves = jnp.dot(table_ref[...], taps, preferred_element_type=F32)
        real, imag = (waves[:size], -waves[size:])
        if block == 0:
            real_ref[block] = real * (1.0 / size)
            imag_ref[block] = imag * (1.0 / size)
        else:
            real_ref[block] = real * (1.0 / size) - sign * before_imag
            imag_ref[block] = imag * (1.0 / size) + sign * before_real
        before_real, before_imag = (real, imag)


def mixed_branches(branches, keep_first, keep_second, got_first, got_second, short_ref, joined):
    own = lax.axis_index("fsdp")
    rows = keep_first.shape[0]
    half = keep_second.shape[1] // len(branches)
    joined[:HALO, :] = keep_second[:HALO, :] + got_second[:HALO, :].astype(F32)
    own_start = pl.multiple_of(HALO + own * rows, HALO)
    other_start = pl.multiple_of(HALO + (1 - own) * rows, HALO)
    joined[pl.ds(own_start, rows), :] = keep_first[...] + got_second[HALO:, :].astype(F32)
    joined[pl.ds(other_start, rows), :] = keep_second[HALO:, :] + got_first[...].astype(F32)
    mixed = []
    for place, branch in enumerate(branches):
        lanes = slice(place * half, (place + 1) * half)
        total = None
        for tap in range(3):
            taps = short_ref[tap, branch : branch + 1, :]
            taps = jnp.where(own == 0, taps[:, :half], taps[:, half:])
            term = taps * joined[pl.ds(HALO - tap, 2 * rows), lanes]
            total = term if total is None else total + term
        mixed.append(total)
    return mixed


def product_body(
    keep_first, keep_second, got_first, got_second, short_ref, order_ref, product_ref, joined
):
    key, value = mixed_branches(
        (1, 2), keep_first, keep_second, got_first, got_second, short_ref, joined
    )
    product_ref[...] = (key * value).astype(BF16)


def query_body(keep_first, keep_second, got_ref, short_ref, query_ref, joined):
    rows = keep_first.shape[0]
    got_first = got_ref.at[:rows, :]
    got_second = got_ref.at[rows : rows + keep_second.shape[0], :]
    (query,) = mixed_branches(
        (0,), keep_first, keep_second, got_first, got_second, short_ref, joined
    )
    query_ref[...] = query


def spectrum_term(step, block_ref, real_ref, imag_ref, table_ref):
    position = lax.axis_index("seq")
    size = table_ref.shape[1]
    source = position ^ step
    back = jnp.maximum(position - source, 0)
    block = block_ref[...]
    if step:
        block = jnp.where(source < position, block, jnp.zeros_like(block))
    part = size // 2
    waves = [
        jnp.dot(table_ref[start : start + part, :], block, preferred_element_type=F32)
        for start in range(0, 2 * size, part)
    ]
    real = jnp.concatenate(waves[:2], axis=0)
    imag = -jnp.concatenate(waves[2:], axis=0)
    tap_real, tap_imag = (real_ref[back], imag_ref[back])
    return (real * tap_real - imag * tap_imag, real * tap_imag + imag * tap_real)


def conv_early_body(own_ref, near_ref, far_ref, real_ref, imag_ref, table_ref, total_ref):
    total_ref[0], total_ref[1] = spectrum_term(0, own_ref, real_ref, imag_ref, table_ref)
    for step, block_ref in ((1, near_ref), (3, far_ref)):
        real, imag = spectrum_term(step, block_ref, real_ref, imag_ref, table_ref)
        total_ref[0] += real
        total_ref[1] += imag


def gated_rows(place, rows, stacked, turned_ref, query_ref, gain_ref, own_ref):
    half = own_ref.shape[1]
    lines = pl.ds(pl.multiple_of(place * rows, rows), rows)
    conv = jnp.dot(turned_ref[lines, :], stacked, preferred_element_type=F32)
    first = lax.axis_index("fsdp") == 0
    gain = jnp.where(first, gain_ref[:, :half], gain_ref[:, half:])
    gated = query_ref[lines, :] * (conv + gain * own_ref[lines, :].astype(F32))
    return gated.astype(BF16)


def conv_last_body(
    last_ref, total_ref, real_ref, imag_ref, table_ref, turned_ref, query_ref, gain_ref, own_ref,
    go_ref, stacked_ref
):
    real, imag = spectrum_term(2, last_ref, real_ref, imag_ref, table_ref)
    stacked = jnp.concatenate([total_ref[0] + real, -(total_ref[1] + imag)], axis=0).astype(BF16)
    stacked_ref[...] = stacked
    other = 1 - lax.axis_index("fsdp")
    go_ref[...] = gated_rows(
        other, go_ref.shape[0], stacked, turned_ref, query_ref, gain_ref, own_ref
    )


def conv_stay_body(stacked_ref, turned_ref, query_ref, gain_ref, own_ref, stay_ref):
    own = lax.axis_index("fsdp")
    stay_ref[...] = gated_rows(
        own, stay_ref.shape[0], stacked_ref[...], turned_ref, query_ref, gain_ref, own_ref
    )


def join_body(stay_ref, got_ref, out_ref):
    first = lax.axis_index("fsdp") == 0
    half = stay_ref.shape[1]
    out_ref[:, :half] = jnp.where(first, stay_ref[...], got_ref[...])
    out_ref[:, half:] = jnp.where(first, got_ref[...], stay_ref[...])


def shape(dims, kind):
    return jax.ShapeDtypeStruct(dims, kind)


def pair_mesh(tokens, proj_weight, short_weight, skip_gain, filter_taps):
    rows = tokens.shape[0]
    width = proj_weight.shape[2]
    half = width // 2
    size = 2 * rows
    blocks = lax.axis_size("seq")
    weight = jnp.transpose(proj_weight, (1, 0, 2))
    pairs = [[(s, s ^ step) for s in range(blocks)] for step in range(blocks)]
    call = functools.partial(
        pl.pallas_call, compiler_params=pltpu.CompilerParams(vmem_limit_bytes=32 * 1024 * 1024)
    )

    cycled = lax.ppermute(tokens, ("fsdp", "chan"), [(1, 3), (3, 2), (2, 0), (0, 1)])
    token = shape((8, 128), F32)
    pack = call(
        pack_body,
        cost_estimate=LONG,
        in_specs=whole_specs(1),
        out_specs=whole_specs(1)[0],
        out_shape=shape((HALO, width), BF16),
    )(tokens)
    pack_got = lax.ppermute(
        pack,
        ("seq", "fsdp", "chan"),
        [
            (4 * s + 2 * f + c, 4 * ((s + 1) % blocks) + 2 * (f ^ (1 - c)) + c)
            for s in range(blocks)
            for f in range(2)
            for c in range(2)
        ],
    )
    arrived_taps = {
        step: lax.ppermute(filter_taps, "seq", pairs[step]) for step in (2, 1, 3)
    }
    tap_blocks = [filter_taps] + [arrived_taps[step] for step in range(1, blocks)]
    cycled = after(cycled, pack_got)
    hop = exchange(cycled, "chan")
    pack_hop = exchange(pack_got, "chan")
    keep_first, send_first, keep_first_query, send_first_query = call(
        project_first_body,
        cost_estimate=LONG,
        in_specs=whole_specs(3),
        out_specs=whole_specs(4),
        out_shape=(
            shape((rows, 2 * half), F32),
            shape((rows, 2 * half), BF16),
            shape((rows, half), F32),
            shape((rows, half), BF16),
        ),
    )(tokens, cycled, weight)
    got_first = exchange(send_first, "fsdp")
    halo = call(
        halo_body,
        in_specs=whole_specs(2),
        out_specs=whole_specs(1)[0],
        out_shape=shape((HALO, tokens.shape[1]), BF16),
    )(pack_got, pack_hop)
    arrived = (cycled, hop, halo, weight)
    keep_second, send_second, second_done = call(
        project_product_body,
        in_specs=whole_specs(4),
        out_specs=whole_specs(3),
        out_shape=(
            shape((HALO + rows, 2 * half), F32),
            shape((HALO + rows, 2 * half), BF16),
            token,
        ),
    )(*arrived)
    keep_second_query, tap_keep, send_late, late_done = call(
        project_query_body,
        in_specs=whole_specs(6 + blocks),
        out_specs=whole_specs(4),
        out_shape=(
            shape((HALO + rows, half), F32),
            shape((blocks, rows, half), BF16),
            shape((rows + HALO + rows + blocks * rows, half), BF16),
            token,
        ),
    )(*arrived, send_first_query, second_done, *tap_blocks)
    got_second = exchange(send_second, "fsdp")

    product = call(
        product_body,
        cost_estimate=LONG,
        in_specs=whole_specs(6),
        out_specs=whole_specs(1)[0],
        out_shape=shape((size, half), BF16),
        scratch_shapes=[pltpu.VMEM((HALO + size, 2 * half), F32)],
    )(keep_first, keep_second, got_first, got_second, short_weight, late_done)
    got_late = exchange(after(send_late, got_first, cost_estimate=LONG), "fsdp")
    query = call(
        query_body,
        in_specs=whole_specs(4),
        out_specs=whole_specs(1)[0],
        out_shape=shape((size, half), F32),
        scratch_shapes=[pltpu.VMEM((HALO + size, half), F32)],
    )(keep_first_query, keep_second_query, got_late, short_weight)
    last, near, far = (lax.ppermute(product, "seq", pairs[step]) for step in (2, 1, 3))
    table = wave_table(size)
    forward = jnp.asarray(table, dtype=BF16)
    inverse = jnp.asarray(table.T, dtype=BF16)
    tap_real, tap_imag = call(
        taps_body,
        in_specs=whole_specs(3),
        out_specs=whole_specs(2),
        out_shape=(shape((blocks, size, half), F32), shape((blocks, size, half), F32)),
    )(forward, tap_keep, got_late)
    total = call(
        conv_early_body,
        in_specs=whole_specs(6),
        out_specs=whole_specs(1)[0],
        out_shape=shape((2, size, half), F32),
    )(product, near, far, tap_real, tap_imag, forward)
    ending = (inverse, query, skip_gain.reshape(1, width), product)
    go, stacked = call(
        conv_last_body,
        in_specs=whole_specs(9),
        out_specs=whole_specs(2),
        out_shape=(shape((rows, half), BF16), shape((2 * size, half), BF16)),
    )(last, total, tap_real, tap_imag, forward, *ending)
    stay = call(
        conv_stay_body,
        in_specs=whole_specs(5),
        out_specs=whole_specs(1)[0],
        out_shape=shape((rows, half), BF16),
    )(stacked, *ending)
    back = exchange(go, "fsdp")
    return call(
        join_body,
        in_specs=whole_specs(2),
        out_specs=whole_specs(1)[0],
        out_shape=shape((rows, width), BF16),
    )(stay, back)


def solution(mesh):
    in_specs = (
        P(("grp", "seq", "fsdp"), "chan"),
        P("fsdp", None, "chan"),
        P(None, None, "chan"),
        P("chan"),
        P(("seq", "fsdp"), "chan"),
    )
    out_specs = P(("grp", "seq", "fsdp"), "chan")
    sizes = mesh.shape
    paired = sizes["fsdp"] == 2 and sizes["chan"] == 2 and sizes["seq"] == 4
    per_device = pair_mesh if paired else any_mesh
    return jax.shard_map(
        per_device, mesh=mesh, in_specs=in_specs, out_specs=out_specs, check_vma=False
    )
```
